128 devices in a mesh: batch: 32 (over y, x, core), chan: 4 (over z).
Axes of the slice: x: 4, y: 4, z: 4, core: 2. Of those that a mesh axis runs over, the one named last changes fastest.
Arguments:
- image_global: bfloat16 [192, 14, 14, 1024], P('batch', None, None, 'chan'), may hold values from -32 to 32
- image_local: bfloat16 [384, 6, 6, 1024], P('batch', None, None, 'chan'), may hold values from -32 to 32
- cotangent_global: bfloat16 [192, 7, 7, 2048], P('batch', None, None, 'chan'), may hold values from -6 to 6
- cotangent_local: bfloat16 [384, 3, 3, 2048], P('batch', None, None, 'chan'), may hold values from -6 to 6
- reduce_one: bfloat16 [1024, 512], P(None, 'chan'), may hold values from -0.1875 to 0.1875
- spatial_one: bfloat16 [3, 3, 512, 512], P(None, None, None, 'chan'), may hold values from -0.09375 to 0.09375
- expand_one: bfloat16 [512, 2048], P(None, 'chan'), may hold values from -0.25 to 0.25
- shortcut: bfloat16 [1024, 2048], P(None, 'chan'), may hold values from -0.1875 to 0.1875
- reduce_two: bfloat16 [2048, 512], P(None, 'chan'), may hold values from -0.125 to 0.125
- spatial_two: bfloat16 [3, 3, 512, 512], P(None, None, None, 'chan'), may hold values from -0.09375 to 0.09375
- expand_two: bfloat16 [512, 2048], P(None, 'chan'), may hold values from -0.25 to 0.25
- factors_mid: float32 [4, 512], P(None, 'chan'), may hold values from 0.5 to 1.5
- factors_out: float32 [3, 2048], P(None, 'chan'), may hold values from 0.5 to 1.5
- shifts_mid: float32 [4, 512], P(None, 'chan'), may hold values from -2 to 2
- shifts_out: float32 [3, 2048], P(None, 'chan'), may hold values from -2 to 2
Outputs:
- output_global: float32 [192, 7, 7, 2048], P('batch', None, None, 'chan')
- output_local: float32 [384, 3, 3, 2048], P('batch', None, None, 'chan')
- image_global_grad: float32 [192, 14, 14, 1024], P('batch', None, None, 'chan')
- image_local_grad: float32 [384, 6, 6, 1024], P('batch', None, None, 'chan')
- reduce_one_grad: float32 [1024, 512], P(None, 'chan')
- spatial_one_grad: float32 [3, 3, 512, 512], P(None, None, None, 'chan')
- expand_one_grad: float32 [512, 2048], P(None, 'chan')
- shortcut_grad: float32 [1024, 2048], P(None, 'chan')
- reduce_two_grad: float32 [2048, 512], P(None, 'chan')
- spatial_two_grad: float32 [3, 3, 512, 512], P(None, None, None, 'chan')
- expand_two_grad: float32 [512, 2048], P(None, 'chan')
- factors_mid_grad: float32 [4, 512], P(None, 'chan')
- factors_out_grad: float32 [3, 2048], P(None, 'chan')
- shifts_mid_grad: float32 [4, 512], P(None, 'chan')
- shifts_out_grad: float32 [3, 2048], P(None, 'chan')
- ratios: float32 [7], replicated
The draws below stay inside these ranges and needn't reach their ends.
All inputs are finite; a program needn't handle non-finite values.
Results may differ from the reference program's by a relative error of at most 0.03.
Values may be sent and summed in bfloat16 or wider, within the bound.
No kernel may reach another device: no remote copies, remote signals or barrier semaphores. Data moves between devices by JAX's collectives and lax.ppermute only.
A program may use at most 192 MiB of HBM per device.

```python
import math
import jax
import jax.numpy as jnp
from jax import lax

CIN = 1024
MID = 512
COUT = 2048
GSIDE = 14
LSIDE = 6
GOUT = 7
LOUT = 3
GLOBAL = 192
LOCAL = 384
PIX = 12864


def crop_field(key, crops, extent, channels, ramp):
    keys = jax.random.split(key, 4)
    normal_part = jnp.clip(jax.random.normal(keys[0], (crops, extent, extent, channels), jnp.float32), -4.0, 4.0)
    noise = normal_part
    offsets = jax.random.uniform(keys[2], (channels,), jnp.float32, -1.0, 1.0)
    position = jnp.arange(crops, dtype=jnp.float32) / max(crops - 1, 1)
    jitter = jax.random.uniform(keys[3], (crops,), jnp.float32, 0.7, 1.4)
    scales = jnp.exp(position * math.log(ramp)) * jitter
    return (noise + offsets) * scales[:, None, None, None]


def draw_image_global(key, part):
    key = jax.random.fold_in(key, 11)
    return crop_field(key, GLOBAL, GSIDE, CIN, 3.0).astype(jnp.bfloat16)


def draw_image_local(key, part):
    key = jax.random.fold_in(key, 23)
    return crop_field(key, LOCAL, LSIDE, CIN, 3.0).astype(jnp.bfloat16)


def block_levels(own_key, dims, shards, smallest, high):
    factor_of = 1.0
    for dim, parts in shards:
        steps = jax.random.uniform(jax.random.fold_in(jax.random.fold_in(own_key, 6), dim), (parts,), jnp.float32, smallest / len(shards), high / len(shards))
        factor_of = factor_of * jnp.repeat(jnp.exp(steps), dims[dim] // parts).reshape((-1,) + (1,) * (len(dims) - 1 - dim))
    return factor_of


def scatter_about(own_key, dims, width, most, cuts=(), kind=jnp.bfloat16):
    array = jax.random.normal(own_key, dims, jnp.float32) * width
    if len(cuts) > 0:
        array = block_levels(own_key, dims, cuts, -0.22, 0.18) * array
    return jnp.clip(array, min=-most, max=most).astype(kind)


def setup_inputs(seed: int = 0) -> dict:
    key_list = jax.random.split(jax.random.key(seed), 16)
    image_global = draw_image_global(jax.random.fold_in(key_list[15], 71), 0)
    image_local = draw_image_local(jax.random.fold_in(key_list[15], 71), 0)
    cotangent_global = scatter_about(key_list[2], (GLOBAL, GOUT, GOUT, COUT), 1.0, 6.0, ((0, 32), (3, 4)))
    cotangent_local = scatter_about(key_list[3], (LOCAL, LOUT, LOUT, COUT), 1.0, 6.0, ((0, 32), (3, 4)))
    reduce_one = scatter_about(key_list[4], (CIN, MID), CIN ** -0.5, 0.1875, ((1, 4),))
    spatial_one = scatter_about(key_list[5], (3, 3, MID, MID), (9 * MID) ** -0.5, 0.09375, ((3, 4),))
    expand_one = scatter_about(key_list[6], (MID, COUT), MID ** -0.5, 0.25, ((1, 4),))
    shortcut = scatter_about(key_list[7], (CIN, COUT), CIN ** -0.5, 0.1875, ((1, 4),))
    reduce_two = scatter_about(key_list[8], (COUT, MID), COUT ** -0.5, 0.125, ((1, 4),))
    spatial_two = scatter_about(key_list[9], (3, 3, MID, MID), (9 * MID) ** -0.5, 0.09375, ((3, 4),))
    expand_two = scatter_about(key_list[10], (MID, COUT), MID ** -0.5, 0.25, ((1, 4),))
    factors_mid = jnp.clip(1.0 + 0.1 * jax.random.normal(key_list[11], (4, MID), jnp.float32), 0.5, 1.5)
    factors_out = jnp.clip(1.0 + 0.1 * jax.random.normal(key_list[12], (3, COUT), jnp.float32), 0.5, 1.5)
    shifts_mid = scatter_about(key_list[13], (4, MID), 0.5, 2.0, ((1, 4),), jnp.float32)
    shifts_out = scatter_about(key_list[14], (3, COUT), 0.5, 2.0, ((1, 4),), jnp.float32)
    return dict(image_global=image_global, image_local=image_local, cotangent_global=cotangent_global, cotangent_local=cotangent_local, reduce_one=reduce_one, spatial_one=spatial_one, expand_one=expand_one, shortcut=shortcut, reduce_two=reduce_two, spatial_two=spatial_two, expand_two=expand_two, factors_mid=factors_mid, factors_out=factors_out, shifts_mid=shifts_mid, shifts_out=shifts_out)


EPS = 1e-05
DECAY = 5e-05

@jax.custom_vjp
def low(v):
    return lax.optimization_barrier(v.astype(jnp.bfloat16)).astype(jnp.float32)

@jax.custom_vjp
def low_back(v):
    return v

def low_keep(v):
    return (low(v), None)

def low_pass(kept, grad):
    return (grad,)

def back_keep(v):
    return (v, None)

def back_low(kept, grad):
    return (low(grad),)
low.defvjp(low_keep, low_pass)
low_back.defvjp(back_keep, back_low)

def activate(argument):
    return jax.nn.gelu(argument, approximate=True)

def window_taps(surface, stride):
    extent = surface.shape[1]
    out_side = (extent - 1) // stride + 1
    padded = jnp.pad(surface, ((0, 0), (1, 1), (1, 1), (0, 0)))
    pieces = []
    for row_off in range(3):
        for col_off in range(3):
            pieces.append(padded[:, row_off:row_off + stride * (out_side - 1) + 1:stride, col_off:col_off + stride * (out_side - 1) + 1:stride, :])
    return jnp.concatenate(pieces, axis=-1)

def project(operand, weight):
    leading = operand.shape[:-1]
    flattened = operand.reshape(-1, operand.shape[-1])
    result = jnp.dot(flattened, weight, precision=lax.Precision.HIGHEST)
    return low_back(result.reshape(leading + (weight.shape[1],)))

def normalize(signal, factor, offset):
    average = lax.optimization_barrier(jnp.mean(signal, axis=(0, 1, 2)))
    squares = lax.optimization_barrier(jnp.mean(signal * signal, axis=(0, 1, 2)))
    inverse = lax.rsqrt(squares - average * average + EPS)
    return (signal - average) * inverse * factor + offset

def group_forward(image_in, weights, norm_params):
    reduce_one, spatial_one, expand_one, shortcut, reduce_two, spatial_two, expand_two = weights
    factors_mid, factors_out, shifts_mid, shifts_out = norm_params
    spatial_rows_one = spatial_one.reshape(-1, spatial_one.shape[-1])
    spatial_rows_two = spatial_two.reshape(-1, spatial_two.shape[-1])
    hidden_one = low(activate(normalize(project(image_in, reduce_one), factors_mid[0], shifts_mid[0])))
    hidden_two = low(activate(normalize(project(window_taps(hidden_one, 2), spatial_rows_one), factors_mid[1], shifts_mid[1])))
    branch = normalize(project(hidden_two, expand_one), factors_out[0], shifts_out[0])
    skipped = normalize(project(image_in[:, ::2, ::2, :], shortcut), factors_out[1], shifts_out[1])
    middle = activate(branch + skipped)
    hidden_four = low(activate(normalize(project(low(middle), reduce_two), factors_mid[2], shifts_mid[2])))
    hidden_five = low(activate(normalize(project(window_taps(hidden_four, 1), spatial_rows_two), factors_mid[3], shifts_mid[3])))
    last_part = normalize(project(hidden_five, expand_two), factors_out[2], shifts_out[2])
    return activate(last_part + middle)

def whole_pass(global_in, local_in, weights, norm_params):
    return (group_forward(global_in, weights, norm_params), group_forward(local_in, weights, norm_params))

def reference(image_global, image_local, cotangent_global, cotangent_local, reduce_one, spatial_one, expand_one, shortcut, reduce_two, spatial_two, expand_two, factors_mid, factors_out, shifts_mid, shifts_out):
    weights = tuple((matrix.astype(jnp.float32) for matrix in (reduce_one, spatial_one, expand_one, shortcut, reduce_two, spatial_two, expand_two)))
    norm_params = tuple((vector.astype(jnp.float32) for vector in (factors_mid, factors_out, shifts_mid, shifts_out)))
    outputs, pullback = jax.vjp(whole_pass, image_global.astype(jnp.float32), image_local.astype(jnp.float32), weights, norm_params)
    global_grad, local_grad, weight_grads, norm_grads = pullback((cotangent_global.astype(jnp.float32), cotangent_local.astype(jnp.float32)))
    weight_sq = jnp.stack([jnp.sum(jnp.square(matrix)) for matrix in weights])
    grad_sq = jnp.stack([jnp.sum(jnp.square(matrix)) for matrix in weight_grads])
    weight_norm = jnp.sqrt(weight_sq)
    ratios = weight_norm / (jnp.sqrt(grad_sq) / PIX + DECAY * weight_norm)
    return (outputs[0], outputs[1], global_grad, local_grad, weight_grads[0], weight_grads[1], weight_grads[2], weight_grads[3], weight_grads[4], weight_grads[5], weight_grads[6], norm_grads[0], norm_grads[1], norm_grads[2], norm_grads[3], ratios)
```

```python
import functools
import math

import jax
import jax.numpy as jnp
import numpy as np
from jax import lax
from jax.experimental import pallas as pl
from jax.experimental.pallas import tpu as pltpu
from jax.sharding import Mesh, PartitionSpec as P

EPS = 1e-05
DECAY = 5e-05
BATCH = ("y", "x", "c")
PLANE = ("y", "x")
EVERY = ("y", "x", "c", "z")
BF = jnp.bfloat16
F32 = jnp.float32
SLOPE = math.sqrt(2.0 / math.pi)
CUBE = 0.044715

LIN, GIN, RIN = 576, 1568, 2144
LOUT, GOUT, ROUT = 144, 392, 544
M_IN = (36 * 12 * 32.0, 196 * 6 * 32.0)
M_OUT = (9 * 12 * 32.0, 49 * 6 * 32.0)
ANY = pl.BlockSpec(memory_space=pl.ANY)
VM = pl.BlockSpec(memory_space=pltpu.VMEM)
SM = pl.BlockSpec(memory_space=pltpu.SMEM)


def shape(dims, dtype=F32):
    return jax.ShapeDtypeStruct(dims, dtype)


def launch(name, body, ins, outs, scratch=(), cost=(0, 0)):
    return pl.pallas_call(
        body,
        name=name,
        out_shape=tuple(outs),
        in_specs=[s for _, s in ins],
        out_specs=tuple(VM for _ in outs),
        scratch_shapes=list(scratch),
        compiler_params=pltpu.CompilerParams(vmem_limit_bytes=56 * 1024 * 1024),
        cost_estimate=pl.CostEstimate(flops=cost[0], bytes_accessed=cost[1], transcendentals=0),
    )(*[a for a, _ in ins])


def act(v):
    return 0.5 * v * (1.0 + jnp.tanh(SLOPE * (v + CUBE * (v * v * v))))


def slope(v):
    s = v * v
    t = jnp.tanh(SLOPE * (v + CUBE * (v * s)))
    return 0.5 * (1.0 + t) + (0.5 * SLOPE) * v * (1.0 - t * t) * (1.0 + (3.0 * CUBE) * s)


def rows8(v):
    return jnp.sum(v.reshape(-1, 8, v.shape[-1]), axis=0)


def row1(v):
    return jnp.sum(v, axis=0, keepdims=True)


def coefs(sums, k, members, g, b):
    m = sums[2 * k : 2 * k + 1] / members
    inv = lax.rsqrt(sums[2 * k + 1 : 2 * k + 2] / members - m * m + EPS)
    a = inv * g
    return m, inv, a, b - m * a


def back_coefs(sums, grads, k, members, g, b):
    m, inv, a, _ = coefs(sums, k, members, g, b)
    c1 = a * inv * (grads[2 * k + 1 : 2 * k + 2] / members)
    return a, c1, a * (grads[2 * k : 2 * k + 1] / members) - m * c1


def keep(rows, width, group, start):
    i = lax.broadcasted_iota(jnp.int32, (rows, width), 0)
    if group == 0:
        return (i & 15) < 12
    return ((i & 7) < 6) & (i + start < LOUT + GOUT)


def sweep(body, init):
    done = []
    for group, (first, steps, rows) in enumerate(((0, 3, 48), (144, 5, 80))):

        def step(s, carry, group=group, first=first, rows=rows):
            return body(group, pl.multiple_of(first + s * rows, 16), rows, carry)

        done.append(lax.fori_loop(0, steps, step, init))
    return done


def wide_sweep(body, init):
    done = []
    for group, (first, steps, rows) in enumerate(((0, 6, 96), (576, 14, 112))):

        def step(s, carry, group=group, first=first, rows=rows):
            return body(group, s, pl.multiple_of(first + s * rows, 16), rows, carry)

        done.append(lax.fori_loop(0, steps, step, init))
    return done


def two(width):
    z = jnp.zeros((8, width), F32)
    return (z, z)


def put_stats(out, done, cols=None):
    rows = jnp.concatenate([row1(s) for group in done for s in group], axis=0)
    if cols is None:
        for p in range(out.shape[0]):
            out[p] = rows
    else:
        out[:, cols] = rows


def moments(z_ref, cols):
    width = cols.size if hasattr(cols, "size") else z_ref.shape[1]

    def body(group, start, rows, carry):
        v = z_ref[pl.ds(start, rows), cols]
        return carry[0] + rows8(v), carry[1] + rows8(v * v)

    return sweep(body, two(width))


def dot(a, b):
    return jnp.dot(a, b, preferred_element_type=F32)


def dot_t(a, b):
    return lax.dot_general(a, b, (((1,), (1,)), ((), ())), preferred_element_type=F32)


def fetch(copies, sem):
    started = []
    for i, (src, dst) in enumerate(copies):
        c = pltpu.make_async_copy(src, dst, sem.at[i])
        c.start()
        started.append(c)
    return started


def wait(started):
    for c in started:
        c.wait()


def pack_kernel(side, local, glob, out, tmp):
    tmp[...] = jnp.zeros_like(tmp)
    base = side[0] * side[0] * 16
    for lane in range(tmp.shape[0]):
        cols = slice(lane * 128, lane * 128 + 128)
        for n in range(12):
            for h in range(side[0]):
                v = local[n, h, :, cols].astype(F32)
                tmp[lane, pl.ds(h * side[0] * 16 + n, side[0], stride=16), :] = v
        for n in range(6):
            for h in range(side[1]):
                v = glob[n, h, :, cols].astype(F32)
                tmp[lane, pl.ds(base + h * side[1] * 8 + n, side[1], stride=8), :] = v
        out[:, cols] = tmp[lane].astype(out.dtype)


def pack(name, local, glob, side, rows):
    c = local.shape[-1]
    return launch(
        name,
        functools.partial(pack_kernel, side),
        [(local, VM), (glob, VM)],
        [shape((rows, c), BF)],
        [pltpu.VMEM((c // 128, rows, 128), F32)],
        (0, 4 * rows * c),
    )[0]


def unpack_kernel(side, lanes, local, glob):
    base = side[0] * side[0] * 16
    for lane in range(lanes.shape[0]):
        cols = slice(lane * 128, lane * 128 + 128)
        for n in range(12):
            for h in range(side[0]):
                v = lanes[lane, pl.ds(h * side[0] * 16 + n, side[0], stride=16), :]
                local[n, h, :, cols] = v
        for n in range(6):
            for h in range(side[1]):
                v = lanes[lane, pl.ds(base + h * side[1] * 8 + n, side[1], stride=8), :]
                glob[n, h, :, cols] = v


def unpack_whole(side, rows, local, glob, lanes):
    for lane in range(lanes.shape[0]):
        lanes[lane] = rows[:, lane * 128 : lane * 128 + 128]
    unpack_kernel(side, lanes, local, glob)


def unpack(name, rows, side):
    c = rows.shape[-1]
    return launch(
        name,
        functools.partial(unpack_whole, side),
        [(rows, VM)],
        [shape((12, side[0], side[0], c)), shape((6, side[1], side[1], c))],
        [pltpu.VMEM((c // 128,) + rows.shape[:1] + (128,), F32)],
        (0, 8 * rows.size),
    )


def first_kernel(zi, x0, x1, x2, x3, g1, z1, stats, w, sem):
    started = fetch([(g1.at[:, z], w.at[:, :, pl.ds(z * 128, 128)]) for z in range(4)], sem)
    wait(started)
    wf = w.reshape(1024, 512)
    done = []

    def body(group, s, start, rows, carry):
        acc = jnp.zeros((rows, 512), F32)
        for k, x in enumerate((x0, x1, x2, x3)):
            q = pl.multiple_of(zi[k] * 256, 256)
            acc = acc + dot(x[pl.ds(start, rows), :], wf[pl.ds(q, 256), :])
        z1[pl.ds(start, rows), :] = acc
        return carry[0] + rows8(acc), carry[1] + rows8(acc * acc)

    for group, (first, steps, rows) in enumerate(((0, 2, 288), (576, 4, 392))):

        def step(s, carry, group=group, first=first, rows=rows):
            return body(group, s, pl.multiple_of(first + s * rows, 8), rows, carry)

        if group == 0:
            done.append(lax.fori_loop(0, steps, step, two(512)))
        else:
            rows = 224

            def step(s, carry):
                return body(1, s, pl.multiple_of(576 + s * 224, 16), 224, carry)

            done.append(lax.fori_loop(0, 7, step, two(512)))
    put_stats(stats, done)


def gather_weight(g, w, sem, at=0):
    rows = w.shape[1]
    return fetch(
        [(g.at[:, z, pl.ds(at, rows), :], w.at[:, :, pl.ds(z * 128, 128)]) for z in range(4)], sem
    )


def load_taps(local, glob, i, j, stride):
    c = local.shape[-1]
    if stride == 2:
        lv = local.reshape(4, 2, 4, 2, 16, c)
        gv = glob.reshape(8, 2, 8, 2, 8, c)
        a, p, b, q = i // 2, i % 2, j // 2, j % 2
        lt = lv[a : a + 3, p, b : b + 3, q]
        gt = gv[a : a + 7, p, b : b + 7, q]
    else:
        lt = local[i : i + 3, j : j + 3]
        gt = glob[i : i + 7, j : j + 7]
    return jnp.concatenate(
        [lt.reshape(LOUT, c), gt.reshape(GOUT, c), jnp.zeros((8, c), F32)], axis=0
    )


def clear_border(ref):
    side = ref.shape[0]
    zero = jnp.zeros((side,) + ref.shape[2:], F32)
    ref[0] = zero
    ref[side - 1] = zero
    for r in range(1, side - 1):
        ref[r, 0] = zero[0]
        ref[r, side - 1] = zero[0]


def conv_tail(taps, w, z):
    wf = w.reshape(4608, 512)
    z[...] = dot(taps[:, 0:512], wf[0:512, :])

    def step(k, carry):
        at = pl.multiple_of(k * 512, 512)
        z[...] += dot(taps[:, pl.ds(at, 512)], wf[pl.ds(at, 512), :])
        return carry

    lax.fori_loop(1, 9, step, 0)


def second_kernel(st, z1, gb, g2, taps, z2, stats, hl, hg, w, sem):
    started = gather_weight(g2, w, sem)
    sums = jnp.sum(st[...], axis=0)
    g, b = gb[0:1], gb[1:2]
    cs = [coefs(sums, k, M_IN[k], g, b) for k in (0, 1)]
    clear_border(hl)
    clear_border(hg)

    def body(group, s, start, rows, carry):
        _, _, a, sh = cs[group]
        i = lax.broadcasted_iota(jnp.int32, (rows, 512), 0)
        ok = (i & 15) < 12 if group == 0 else (i & 7) < 6
        h = jnp.where(ok, act(z1[pl.ds(start, rows), :] * a + sh), 0.0)
        if group == 0:
            hl[s + 1, 1:7] = h.reshape(6, 16, 512)
        else:
            hg[s + 1, 1:15] = h.reshape(14, 8, 512)
        return carry

    wide_sweep(body, 0)
    for i in range(3):
        for j in range(3):
            k = 3 * i + j
            taps[:, k * 512 : (k + 1) * 512] = load_taps(hl, hg, i, j, 2).astype(BF)
    wait(started)
    conv_tail(taps, w, z2)
    put_stats(stats, moments(z2, slice(None)))


def fifth_kernel(st, z4, gb, late, taps, z5, stats, hl, hg, w, sem):
    started = gather_weight(late, w, sem, 64)
    sums = jnp.sum(st[...], axis=0)
    g, b = gb[0:1], gb[1:2]
    cs = [coefs(sums, k, M_OUT[k], g, b) for k in (0, 1)]
    hl[...] = jnp.zeros_like(hl)
    hg[...] = jnp.zeros_like(hg)
    for group, (first, side, rows) in enumerate(((0, 3, 48), (144, 7, 56))):
        _, _, a, sh = cs[group]
        i = lax.broadcasted_iota(jnp.int32, (rows, 512), 0)
        ok = (i & 15) < 12 if group == 0 else (i & 7) < 6

        def step(s, carry, group=group, first=first, side=side, rows=rows, a=a, sh=sh, ok=ok):
            v = z4[pl.ds(pl.multiple_of(first + s * rows, 8), rows), :]
            h = jnp.where(ok, act(v * a + sh), 0.0)
            if group == 0:
                hl[s + 1, 1:4] = h.reshape(3, 16, 512)
            else:
                hg[s + 1, 1:8] = h.reshape(7, 8, 512)
            return carry

        lax.fori_loop(0, side, step, 0)
    for i in range(3):
        for j in range(3):
            k = 3 * i + j
            taps[:, k * 512 : (k + 1) * 512] = load_taps(hl, hg, i, j, 1).astype(BF)
    wait(started)
    conv_tail(taps, w, z5)
    put_stats(stats, moments(z5, slice(None)))


def conv_forward(name, kernel, st, z, gb, gw, sides):
    sl, sg = sides
    return launch(
        name,
        kernel,
        [(st, VM), (z, VM), (gb, VM), (gw, ANY)],
        [shape((ROUT, 4608), BF), shape((ROUT, 512)), shape((32, 4, 512))],
        [
            pltpu.VMEM((sl, sl, 16, 512), F32),
            pltpu.VMEM((sg, sg, 8, 512), F32),
            pltpu.VMEM((32, 144, 512), BF),
            pltpu.SemaphoreType.DMA((4,)),
        ],
        (2 * 544 * 4608 * 512, 20_000_000),
    )


def hidden_rows(st, z, gb, h):
    sums = jnp.sum(st[...], axis=0)
    g, b = gb[0:1], gb[1:2]
    cs = [coefs(sums, k, M_OUT[k], g, b) for k in (0, 1)]

    def body(group, start, rows, carry):
        _, _, a, sh = cs[group]
        v = act(z[pl.ds(start, rows), :] * a + sh)
        h[pl.ds(start, rows), :] = jnp.where(keep(rows, 512, group, start), v, 0.0).astype(BF)
        return carry

    sweep(body, 0)


def expand_kernel(plan, st, z, gb, zi, *refs):
    srcs, (h, zo, stats, w, sem) = refs[: len(refs) - 5], refs[len(refs) - 5 :]
    started = fetch(plan(zi, srcs, w), sem)
    hidden_rows(st, z, gb, h)
    wait(started)
    for n in range(4):
        cols = pl.ds(n * 512, 512)
        zo[:, cols] = dot(h[...], w[:, cols])
        put_stats(stats, moments(zo, cols), cols)


def plan_split(zi, srcs, w):
    own, mine, other = srcs
    copies = [(own, w.at[:, pl.ds(pl.multiple_of(zi[0] * 512, 512), 512)])]
    for k in (1, 2, 3):
        cols = pl.ds(pl.multiple_of(zi[k] * 512, 512), 512)
        r = pl.multiple_of(zi[4] * 256, 256)
        copies.append((mine.at[k - 1, pl.ds(512, 256), :], w.at[pl.ds(r, 256), cols]))
        copies.append((other.at[k - 1, pl.ds(512, 256), :], w.at[pl.ds(256 - r, 256), cols]))
    return copies


def plan_skip(zi, srcs, w):
    own, mine, other = srcs
    copies = [(own, w.at[:, pl.ds(pl.multiple_of(zi[0] * 512, 512), 512)])]
    for k in (1, 2, 3):
        cols = pl.ds(pl.multiple_of(zi[k] * 512, 512), 512)
        r = pl.multiple_of(zi[4] * 512, 512)
        copies.append((mine.at[k - 1, pl.ds(0, 512), :], w.at[pl.ds(r, 512), cols]))
        copies.append((other.at[k - 1, pl.ds(0, 512), :], w.at[pl.ds(512 - r, 512), cols]))
    return copies


def plan_late(zi, srcs, w):
    (late,) = srcs
    wv = w.reshape(32, 16, 2048)
    return [
        (late.at[:, z, pl.ds(208 + 16 * j, 16), :], wv.at[:, :, pl.ds(z * 512 + j * 128, 128)])
        for z in range(4)
        for j in range(4)
    ]


def expand_forward(name, plan, n, st, z, gb, zi, srcs):
    return launch(
        name,
        functools.partial(expand_kernel, plan),
        [(st, VM), (z, VM), (gb, VM), (zi, SM)] + [(s, ANY) for s in srcs],
        [shape((ROUT, 512), BF), shape((ROUT, 2048)), shape((4, 2048))],
        [pltpu.VMEM((512, 2048), BF), pltpu.SemaphoreType.DMA((n,))],
        (2 * 544 * 512 * 2048, 9_000_000),
    )


def skip_kernel(zi, x0, x1, x2, x3, own, mine, other, xe, zs, stats, tmp, w, sem):
    started = fetch(plan_skip(zi, (own, mine, other), w), sem)
    tmp[pl.ds(536, 8), :] = jnp.zeros((8, 256), F32)
    for k, x in enumerate((x0, x1, x2, x3)):
        for r in range(3):
            v = x[pl.ds(r * 192, 96), :].astype(F32).reshape(3, 2, 16, 256)[:, 0]
            tmp[pl.ds(r * 48, 48), :] = v.reshape(48, 256)
        for r in range(7):
            v = x[pl.ds(576 + r * 224, 112), :].astype(F32).reshape(7, 2, 8, 256)[:, 0]
            tmp[pl.ds(144 + r * 56, 56), :] = v.reshape(56, 256)
        at = pl.multiple_of(zi[k] * 256, 256)
        xe[:, pl.ds(at, 256)] = tmp[...].astype(BF)
    wait(started)
    for n in range(4):
        cols = pl.ds(n * 512, 512)
        zs[:, cols] = dot(xe[...], w[:, cols])
        put_stats(stats, moments(zs, cols), cols)


def middle_kernel(st3, sts, z3, zs, gb, late, mid, h3, z4, stats, w, sem):
    started = fetch(
        [
            (late.at[:, z, pl.ds(0, 64), :], w.at[:, :, pl.ds(z * 128, 128)])
            for z in range(4)
        ],
        sem,
    )
    for n in range(4):
        cols = pl.ds(n * 512, 512)
        s3 = jnp.sum(st3[:, :, cols], axis=0)
        ss = jnp.sum(sts[:, :, cols], axis=0)
        cs = []
        for k in (0, 1):
            _, _, a3, b3 = coefs(s3, k, M_OUT[k], gb[0:1, cols], gb[1:2, cols])
            _, _, a5, b5 = coefs(ss, k, M_OUT[k], gb[2:3, cols], gb[3:4, cols])
            cs.append((a3, a5, b3 + b5))

        def body(group, start, rows, carry, cols=cols, cs=cs):
            a3, a5, b = cs[group]
            here = (pl.ds(start, rows), cols)
            v = act(z3[here] * a3 + zs[here] * a5 + b)
            v = jnp.where(keep(rows, 512, group, start), v, 0.0)
            mid[here] = v
            h3[here] = v.astype(BF)
            return carry

        sweep(body, 0)
    wait(started)
    z4[...] = dot(h3[...], w.reshape(2048, 512)[...])
    put_stats(stats, moments(z4, slice(None)))


def last_kernel(zi, st, z6, mid, gb, c0, c1, c2, c3, out, dv6, stats):
    for k, cot in enumerate((c0, c1, c2, c3)):
        cols = pl.ds(pl.multiple_of(zi[k] * 512, 512), 512)
        sums = jnp.sum(st[:, :, cols], axis=0)
        cs = [coefs(sums, j, M_OUT[j], gb[0:1, cols], gb[1:2, cols]) for j in (0, 1)]

        def body(group, start, rows, carry, cols=cols, cs=cs, k=k, cot=cot):
            m, _, a, sh = cs[group]
            here = (pl.ds(start, rows), cols)
            z = z6[here]
            v = z * a + sh + mid[here]
            if k == 0:
                out[pl.ds(start, rows), :] = act(v)
            d = slope(v) * cot[pl.ds(start, rows), :].astype(F32)
            dv6[here] = d
            return carry[0] + rows8(d), carry[1] + rows8(d * (z - m))

        done = sweep(body, two(512))
        done = [(s, q * cs[j][1]) for j, (s, q) in enumerate(done)]
        put_stats(stats, done, cols)


def grads_out(ref, sums, rows=((0, 2), (1, 3))):
    for i, (a, b) in enumerate(rows):
        ref[i : i + 1, :] = sums[a : a + 1] + sums[b : b + 1]


def mid_sums(dy, z, cs):
    def body(group, start, rows, carry):
        here = (pl.ds(start, rows), slice(None))
        d = dy[here]
        return carry[0] + rows8(d), carry[1] + rows8(d * (z[here] - cs[group][0]))

    return [(s, q * cs[j][1]) for j, (s, q) in enumerate(sweep(body, two(512)))]


def slope_rows(dy, z, cs, mask=True):
    def body(group, start, rows, carry):
        m, _, a, sh = cs[group]
        here = (pl.ds(start, rows), slice(None))
        v = z[here]
        d = jnp.where(keep(rows, 512, group, start), slope(v * a + sh) * dy[here], 0.0)
        dy[here] = d
        return carry[0] + rows8(d), carry[1] + rows8(d * (v - m))

    return [(s, q * cs[j][1]) for j, (s, q) in enumerate(sweep(body, two(512)))]


def out_coefs(st, gb, at=0):
    sums = jnp.sum(st[...], axis=0)
    return [coefs(sums, k, M_OUT[k], gb[at : at + 1], gb[at + 1 : at + 2]) for k in (0, 1)]


def norm_rows(dy, z, sums, grads, g, b, cols, dz):
    cs = [back_coefs(sums, grads, k, M_OUT[k], g, b) for k in (0, 1)]

    def body(group, start, rows, carry):
        a, c1, c0 = cs[group]
        here = (pl.ds(start, rows), cols)
        d = a * dy[here] - c1 * z[here] - c0
        dz[here] = jnp.where(keep(rows, 512, group, start), d, 0.0).astype(BF)
        return carry

    sweep(body, 0)


def wide_norm(stb, st, z, dy, gb, dz, grad, at=0, rows=(0, 1, 2, 3)):
    for n in range(4):
        cols = pl.ds(n * 512, 512)
        grads = jnp.sum(stb[:, :, cols], axis=0)
        grads = jnp.concatenate([grads[r : r + 1] for r in rows], axis=0)
        sums = jnp.sum(st[:, :, cols], axis=0)
        norm_rows(dy, z, sums, grads, gb[at : at + 1, cols], gb[at + 1 : at + 2, cols], cols, dz)
        for i, (p, q) in enumerate(((0, 2), (1, 3))):
            grad[i : i + 1, cols] = grads[p : p + 1] + grads[q : q + 1]


def own_cols(dst, src, zi, width):
    at = pl.multiple_of(zi[0] * width, width)
    dst[...] = src[:, pl.ds(at, width)]


def back_six_kernel(zi, stb, st6, z6, dv6, gb6, st5, z5, gb5, late, own, dv5, stats, grad, dz, w, sem):
    started = fetch(plan_late(zi, (late,), w), sem)
    wide_norm(stb, st6, z6, dv6, gb6, dz, grad)
    own_cols(own, dz, zi, 512)
    wait(started)
    dv5[...] = dot_t(dz[...], w[...])
    put_stats(stats, slope_rows(dv5, z5, out_coefs(st5, gb5)))


def pad_back(dzl, dzg, dz, at):
    dzl[...] = jnp.zeros_like(dzl)
    dzg[...] = jnp.zeros_like(dzg)
    for r in range(3):
        dzl[at + r, at : at + 3] = dz[pl.ds(48 * r, 48), :].reshape(3, 16, 512)
    for r in range(7):
        dzg[at + r, at : at + 7] = dz[pl.ds(144 + 56 * r, 56), :].reshape(7, 8, 512)


def back_five_kernel(zi, stb, st5, z5, dv5, gb5, st4, z4, gb4, late, own, dv4, stats, grad, dzf, dz, dzl, dzg, w, sem):
    started = gather_weight(late, w, sem, 64)
    sums = jnp.sum(st5[...], axis=0)
    grads = jnp.sum(stb[...], axis=0)
    cs = [back_coefs(sums, grads, k, M_OUT[k], gb5[0:1], gb5[1:2]) for k in (0, 1)]

    def body(group, start, rows, carry):
        a, c1, c0 = cs[group]
        here = (pl.ds(start, rows), slice(None))
        d = a * dv5[here] - c1 * z5[here] - c0
        dzf[here] = jnp.where(keep(rows, 512, group, start), d, 0.0)
        return carry

    sweep(body, 0)
    at = pl.multiple_of(zi[0] * 128, 128)
    own[...] = dzf[:, pl.ds(at, 128)].astype(BF)
    grads_out(grad, grads)
    pad_back(dzl, dzg, dzf, 1)
    wait(started)
    wf = w.reshape(4608, 512)
    for i in range(3):
        for j in range(3):
            k = 3 * i + j
            dz[...] = load_taps(dzl, dzg, 2 - i, 2 - j, 1).astype(BF)
            part = dot_t(dz[...], wf[k * 512 : (k + 1) * 512, :])
            if k == 0:
                dv4[...] = part
            else:
                dv4[...] += part
    put_stats(stats, slope_rows(dv4, z4, out_coefs(st4, gb4)))


def back_four_kernel(zi, stb, st4, z4, dv4, gb4, dv6, st3, sts, z3, zs, gb3, late, own, dpre, stats, grad, dz, w, sem):
    started = fetch(
        [
            (late.at[:, z, pl.ds(0, 64), :], w.at[:, :, pl.ds(z * 128, 128)])
            for z in range(4)
        ],
        sem,
    )
    sums = jnp.sum(st4[...], axis=0)
    grads = jnp.sum(stb[...], axis=0)
    norm_rows(dv4, z4, sums, grads, gb4[0:1], gb4[1:2], slice(None), dz)
    own_cols(own, dz, zi, 128)
    grads_out(grad, grads)
    wait(started)
    wf = w.reshape(2048, 512)
    for n in range(4):
        cols = pl.ds(n * 512, 512)
        dpre[:, cols] = dot_t(dz[...], wf[n * 512 : (n + 1) * 512, :])
        s3 = jnp.sum(st3[:, :, cols], axis=0)
        ss = jnp.sum(sts[:, :, cols], axis=0)
        cs = []
        for k in (0, 1):
            m3, i3, a3, b3 = coefs(s3, k, M_OUT[k], gb3[0:1, cols], gb3[1:2, cols])
            ms, is_, a5, b5 = coefs(ss, k, M_OUT[k], gb3[2:3, cols], gb3[3:4, cols])
            cs.append((a3, a5, b3 + b5, m3, ms, i3, is_))

        def body(group, start, rows, carry, cols=cols, cs=cs):
            a3, a5, b, m3, ms, _, _ = cs[group]
            here = (pl.ds(start, rows), cols)
            u, v = z3[here], zs[here]
            d = slope(u * a3 + v * a5 + b) * (dpre[here] + dv6[here])
            d = jnp.where(keep(rows, 512, group, start), d, 0.0)
            dpre[here] = d
            return (
                carry[0] + rows8(d),
                carry[1] + rows8(d * (u - m3)),
                carry[2] + rows8(d * (v - ms)),
            )

        z8 = jnp.zeros((8, 512), F32)
        done = sweep(body, (z8, z8, z8))
        done = [(s, p * cs[j][5], q * cs[j][6]) for j, (s, p, q) in enumerate(done)]
        put_stats(stats, done, cols)


def back_three_kernel(zi, stb, st3, sts, z3, zs, dpre, gb3, st2, z2, gb2, e_own, e_mine, e_other, own3, dzs, dv2, stats, grad3, grads, dz, w, sem):
    started = fetch(plan_split(zi, (e_own, e_mine, e_other), w), sem)
    wide_norm(stb, st3, z3, dpre, gb3, dz, grad3, 0, (0, 1, 3, 4))
    own_cols(own3, dz, zi, 512)
    wait(started)
    dv2[...] = dot_t(dz[...], w[...])
    put_stats(stats, slope_rows(dv2, z2, out_coefs(st2, gb2)))
    wide_norm(stb, sts, zs, dpre, gb3, dzs, grads, 2, (0, 2, 3, 5))


def back_two_kernel(zi, stb, st2, z2, dv2, gb2, st1, z1, gb1, g2, own, dv1, stats, grad, dzf, dz, acc, dzl, dzg, w, sem):
    started = gather_weight(g2, w, sem)
    sums = jnp.sum(st2[...], axis=0)
    grads = jnp.sum(stb[...], axis=0)
    cs = [back_coefs(sums, grads, k, M_OUT[k], gb2[0:1], gb2[1:2]) for k in (0, 1)]

    def body(group, start, rows, carry):
        a, c1, c0 = cs[group]
        here = (pl.ds(start, rows), slice(None))
        d = a * dv2[here] - c1 * z2[here] - c0
        dzf[here] = jnp.where(keep(rows, 512, group, start), d, 0.0)
        return carry

    sweep(body, 0)
    at = pl.multiple_of(zi[0] * 128, 128)
    own[...] = dzf[:, pl.ds(at, 128)].astype(BF)
    grads_out(grad, grads)
    pad_back(dzl, dzg, dzf, 0)
    wait(started)
    wf = w.reshape(4608, 512)
    s1 = jnp.sum(st1[...], axis=0)
    c1s = [coefs(s1, k, M_IN[k], gb1[0:1], gb1[1:2]) for k in (0, 1)]
    reach = (((1, 0),), ((2, 0), (0, 1)))
    z8 = jnp.zeros((8, 512), F32)
    totals = [(z8, z8), (z8, z8)]
    for p in (0, 1):
        for q in (0, 1):
            first = True
            for i, di in reach[p]:
                for j, dj in reach[q]:
                    k = 3 * i + j
                    dz[...] = load_taps(dzl, dzg, di, dj, 1).astype(BF)
                    part = dot_t(dz[...], wf[k * 512 : (k + 1) * 512, :])
                    if first:
                        acc[...] = part
                    else:
                        acc[...] += part
                    first = False
            for group, (base, side, n, from_row) in enumerate(((0, 3, 16, 0), (576, 7, 8, 144))):
                m, _, a, sh = c1s[group]
                okay = lax.broadcasted_iota(jnp.int32, (n, 512), 0) < (12 if group == 0 else 6)

                def step(r, carry, side=side, n=n, base=base, from_row=from_row, m=m, a=a, sh=sh, okay=okay, p=p, q=q):
                    s, t = carry
                    for c in range(side):
                        at = base + ((2 * r + p) * 2 * side + 2 * c + q) * n
                        rows = pl.ds(pl.multiple_of(at, 8), n)
                        v = z1[rows, :]
                        g = acc[pl.ds(pl.multiple_of(from_row + (r * side + c) * n, 8), n), :]
                        d = jnp.where(okay, slope(v * a + sh) * g, 0.0)
                        dv1[rows, :] = d
                        s = s + rows8(d)
                        t = t + rows8(d * (v - m))
                    return s, t

                totals[group] = lax.fori_loop(0, side, step, totals[group])
    put_stats(stats, [(s, t * c1s[j][1]) for j, (s, t) in enumerate(totals)])


def back_one_kernel(zi, stb, st1, z1, dv1, gb1, g1, skip, own, local, glob, grad, dz, img, w, sem):
    started = gather_weight(g1, w, sem)
    sums = jnp.sum(st1[...], axis=0)
    grads = jnp.sum(stb[...], axis=0)
    cs = [back_coefs(sums, grads, k, M_IN[k], gb1[0:1], gb1[1:2]) for k in (0, 1)]

    def body(group, s, start, rows, carry):
        a, c1, c0 = cs[group]
        here = (pl.ds(start, rows), slice(None))
        i = lax.broadcasted_iota(jnp.int32, (rows, 512), 0)
        ok = (i & 15) < 12 if group == 0 else (i & 7) < 6
        d = a * dv1[here] - c1 * z1[here] - c0
        dz[here] = jnp.where(ok, d, 0.0).astype(BF)
        return carry

    wide_sweep(body, 0)
    own_cols(own, dz, zi, 128)
    grads_out(grad, grads)
    wait(started)
    mine = w.reshape(1024, 512)[pl.ds(pl.multiple_of(zi[0] * 256, 256), 256), :]
    for lane in range(2):
        cols = slice(lane * 128, lane * 128 + 128)
        img[lane] = dot_t(dz[...], mine[lane * 128 : lane * 128 + 128])
        lv = img.at[lane, pl.ds(0, LIN)].reshape(3, 2, 3, 2, 16, 128)
        gv = img.at[lane, pl.ds(LIN, GIN)].reshape(7, 2, 7, 2, 8, 128)
        lv[:, 0, :, 0] += skip[pl.ds(0, LOUT), cols].reshape(3, 3, 16, 128)
        gv[:, 0, :, 0] += skip[pl.ds(LOUT, GOUT), cols].reshape(7, 7, 8, 128)
    unpack_kernel((6, 14), img, local, glob)


def ring(n, k):
    return [(i, (i + k) % n) for i in range(n)]


def spread(v, axes, n):
    return lax.all_to_all(jnp.broadcast_to(v[None], (n,) + v.shape), axes, 0, 0)


def share(v):
    v = v + lax.ppermute(v, "c", ring(2, 1))
    return spread(v, PLANE, 16)


def tell(v):
    return lax.all_to_all(v, BATCH, 0, 0)


def batch_index():
    return (lax.axis_index("y") * 4 + lax.axis_index("x")) * 2 + lax.axis_index("c")


def piece(shard):
    n = shard.shape[0] // 32
    return lax.dynamic_slice_in_dim(shard, batch_index() * n, n, 0)


def around(v, half):
    left = lax.ppermute(v, "z", ring(4, 1))
    right = lax.ppermute(v, "z", ring(4, 3))
    far = jnp.concatenate(
        [lax.ppermute(left[:half], "z", ring(4, 1)), lax.ppermute(right[half:], "z", ring(4, 3))]
    )
    return right, far, left


def batch_total(parts):
    flat = [p.astype(BF).reshape(32, -1, 128) for p in parts]
    sizes = [f.shape[1] for f in flat]
    v = jnp.concatenate(flat, axis=1)
    half = v.reshape(2, 16, v.shape[1], 128)
    ci = lax.axis_index("c")
    keep_ = lax.dynamic_index_in_dim(half, ci, 0, keepdims=False)
    give = lax.dynamic_index_in_dim(half, 1 - ci, 0, keepdims=False)
    got = lax.ppermute(give, "c", ring(2, 1))
    s = (keep_.astype(F32) + got.astype(F32)).astype(BF)
    s = lax.all_to_all(s, PLANE, 0, 0)
    s = jnp.sum(s.astype(F32), axis=0).astype(BF)
    mine = spread(s, PLANE, 16)
    other = lax.ppermute(mine, "c", ring(2, 1))
    low = jnp.where(ci == 0, mine, other)
    high = jnp.where(ci == 0, other, mine)
    v = jnp.concatenate([low, high], axis=0)
    out, at = [], 0
    for p, size in zip(parts, sizes):
        out.append(v[:, at : at + size].reshape(p.shape).astype(F32))
        at += size
    return out


def dot_w(a, b):
    return lax.dot_general(a, b, (((0,), (0,)), ((), ())), preferred_element_type=F32)


def body(
    image_global,
    image_local,
    cotangent_global,
    cotangent_local,
    reduce_one,
    spatial_one,
    expand_one,
    shortcut,
    reduce_two,
    spatial_two,
    expand_two,
    factors_mid,
    factors_out,
    shifts_mid,
    shifts_out,
):
    zi = lax.axis_index("z")
    ci = lax.axis_index("c")
    where = jnp.stack([zi, (zi + 1) % 4, (zi + 2) % 4, (zi + 3) % 4, ci]).astype(jnp.int32)
    flat2, flat5 = spatial_one.reshape(-1, 128), spatial_two.reshape(-1, 128)
    own = [reduce_one, flat2, expand_one, shortcut, reduce_two, flat5, expand_two]

    early = spread(jnp.concatenate([piece(reduce_one), piece(flat2)]), "z", 4)
    g1 = spread(early[:, :32], BATCH, 32)
    g2 = spread(early[:, 32:], BATCH, 32)
    e2 = piece(expand_two)
    late = lax.all_gather(
        jnp.concatenate(
            [piece(reduce_two), piece(flat5)] + [e2[:, 128 * j : 128 * j + 128] for j in range(4)]
        ),
        EVERY,
        axis=0,
    ).reshape(32, 4, 272, 128)

    x = pack("pack_image", image_local, image_global, (6, 14), RIN)
    xs = (x,) + around(x, 1072)
    top = jnp.concatenate([shortcut[:512], expand_one[:256]])
    low = jnp.concatenate([shortcut[512:], expand_one[256:]])
    mine = jnp.stack(around(jnp.where(ci == 0, top, low), 384))
    other = lax.ppermute(mine, "c", ring(2, 1))
    cot = pack("pack_cotangent", cotangent_local, cotangent_global, (3, 7), ROUT)
    cots = (cot,) + around(cot, 272)

    norms = jnp.concatenate(
        [factors_mid, shifts_mid, factors_out.reshape(12, 128), shifts_out.reshape(12, 128)]
    )
    norms = spread(norms, "z", 4)
    fm = norms[:, 0:4].transpose(1, 0, 2).reshape(4, 512)
    sm = norms[:, 4:8].transpose(1, 0, 2).reshape(4, 512)
    fo = norms[:, 8:20].reshape(4, 3, 512).transpose(1, 0, 2).reshape(3, 2048)
    so = norms[:, 20:32].reshape(4, 3, 512).transpose(1, 0, 2).reshape(3, 2048)
    gb1, gb2, gb4, gb5 = [jnp.stack([fm[i], sm[i]]) for i in range(4)]
    gb3 = jnp.stack([fo[0], so[0], fo[1], so[1]])
    gb6 = jnp.stack([fo[2], so[2]])

    z1, s1 = launch(
        "reduce_one",
        first_kernel,
        [(where, SM)] + [(v, VM) for v in xs] + [(g1, ANY)],
        [shape((RIN, 512)), shape((32, 4, 512))],
        [pltpu.VMEM((32, 32, 512), BF), pltpu.SemaphoreType.DMA((4,))],
        (2 * RIN * 1024 * 512, 10_000_000),
    )
    st1 = tell(s1)
    xe, zs, ss = launch(
        "shortcut",
        skip_kernel,
        [(where, SM)] + [(v, VM) for v in xs] + [(shortcut, ANY), (mine, ANY), (other, ANY)],
        [shape((ROUT, 1024), BF), shape((ROUT, 2048)), shape((4, 2048))],
        [pltpu.VMEM((ROUT, 256), F32), pltpu.VMEM((1024, 2048), BF), pltpu.SemaphoreType.DMA((7,))],
        (2 * ROUT * 1024 * 2048, 14_000_000),
    )
    sts = share(ss)
    t1, z2, s2 = conv_forward("spatial_one", second_kernel, st1, z1, gb1, g2, (8, 16))
    st2 = tell(s2)
    h2, z3, s3 = expand_forward(
        "expand_one", plan_split, 7, st2, z2, gb2, where, (expand_one, mine, other)
    )
    st3 = share(s3)
    mid, h3, z4, s4 = launch(
        "reduce_two",
        middle_kernel,
        [(v, VM) for v in (st3, sts, z3, zs, gb3)] + [(late, ANY)],
        [shape((ROUT, 2048)), shape((ROUT, 2048), BF), shape((ROUT, 512)), shape((32, 4, 512))],
        [pltpu.VMEM((32, 64, 512), BF), pltpu.SemaphoreType.DMA((4,))],
        (2 * ROUT * 2048 * 512, 20_000_000),
    )
    st4 = tell(s4)
    t4, z5, s5 = conv_forward("spatial_two", fifth_kernel, st4, z4, gb4, late, (5, 9))
    st5 = tell(s5)
    h5, z6, s6 = expand_forward("expand_two", plan_late, 16, st5, z5, gb5, where, (late,))
    st6 = share(s6)
    out, dv6, b6 = launch(
        "output",
        last_kernel,
        [(where, SM)] + [(v, VM) for v in (st6, z6, mid, gb6) + cots],
        [shape((ROUT, 512)), shape((ROUT, 2048)), shape((4, 2048))],
        (),
        (0, 20_000_000),
    )
    output_local, output_global = unpack("unpack_output", out, (3, 7))
    bt6 = share(b6)

    mid_out = [shape((ROUT, 512)), shape((32, 4, 512))]
    mid_grad, out_grad = shape((2, 512)), shape((2, 2048))
    o6, dv5, b5, gr6 = launch(
        "back_expand_two",
        back_six_kernel,
        [(where, SM)] + [(v, VM) for v in (bt6, st6, z6, dv6, gb6, st5, z5, gb5)] + [(late, ANY)],
        [shape((ROUT, 512), BF)] + mid_out + [out_grad],
        [
            pltpu.VMEM((ROUT, 2048), BF),
            pltpu.VMEM((512, 2048), BF),
            pltpu.SemaphoreType.DMA((16,)),
        ],
        (2 * ROUT * 2048 * 512, 14_000_000),
    )
    bt5 = tell(b5)
    gw6 = dot_w(h5, o6)
    conv_scratch = [
        pltpu.VMEM((ROUT, 512), F32),
        pltpu.VMEM((ROUT, 512), BF),
    ]
    conv_weight = [pltpu.VMEM((32, 144, 512), BF), pltpu.SemaphoreType.DMA((4,))]
    o5, dv4, b4, gr5 = launch(
        "back_spatial_two",
        back_five_kernel,
        [(where, SM)] + [(v, VM) for v in (bt5, st5, z5, dv5, gb5, st4, z4, gb4)] + [(late, ANY)],
        [shape((ROUT, 128), BF)] + mid_out + [mid_grad],
        conv_scratch
        + [pltpu.VMEM((5, 5, 16, 512), F32), pltpu.VMEM((9, 9, 8, 512), F32)]
        + conv_weight,
        (2 * ROUT * 4608 * 512, 10_000_000),
    )
    bt4 = tell(b4)
    gw5 = dot_w(t4, o5)
    o4, dpre, b3, gr4 = launch(
        "back_reduce_two",
        back_four_kernel,
        [(where, SM)]
        + [(v, VM) for v in (bt4, st4, z4, dv4, gb4, dv6, st3, sts, z3, zs, gb3)]
        + [(late, ANY)],
        [shape((ROUT, 128), BF), shape((ROUT, 2048)), shape((6, 2048)), mid_grad],
        [
            pltpu.VMEM((ROUT, 512), BF),
            pltpu.VMEM((32, 64, 512), BF),
            pltpu.SemaphoreType.DMA((4,)),
        ],
        (2 * ROUT * 2048 * 512, 22_000_000),
    )
    bt3 = share(b3)
    gw4 = dot_w(h3, o4)
    o3, dzs, dv2, b2, gr3, grs = launch(
        "back_expand_one",
        back_three_kernel,
        [(where, SM)]
        + [(v, VM) for v in (bt3, st3, sts, z3, zs, dpre, gb3, st2, z2, gb2)]
        + [(v, ANY) for v in (expand_one, mine, other)],
        [shape((ROUT, 512), BF), shape((ROUT, 2048), BF)] + mid_out + [out_grad, out_grad],
        [
            pltpu.VMEM((ROUT, 2048), BF),
            pltpu.VMEM((512, 2048), BF),
            pltpu.SemaphoreType.DMA((7,)),
        ],
        (2 * ROUT * 2048 * 512, 22_000_000),
    )
    bt2 = tell(b2)
    gw3 = dot_w(h2, o3)
    own_s = lax.dynamic_slice_in_dim(dzs, zi * 512, 512, 1)
    gws = dot_w(xe, own_s)
    o2, dv1, b1, gr2 = launch(
        "back_spatial_one",
        back_two_kernel,
        [(where, SM)] + [(v, VM) for v in (bt2, st2, z2, dv2, gb2, st1, z1, gb1)] + [(g2, ANY)],
        [shape((ROUT, 128), BF), shape((RIN, 512)), shape((32, 4, 512)), mid_grad],
        conv_scratch
        + [
            pltpu.VMEM((ROUT, 512), F32),
            pltpu.VMEM((4, 4, 16, 512), F32),
            pltpu.VMEM((8, 8, 8, 512), F32),
        ]
        + conv_weight,
        (2 * ROUT * 4608 * 512, 20_000_000),
    )
    bt1 = tell(b1)
    gw2 = dot_w(t1, o2)
    skip_w = [lax.dynamic_slice_in_dim(shortcut, zi * 256, 256, 0)]
    at = zi * 256
    cut = jnp.concatenate(
        [jnp.where(ci == 0, mine[:, :512], other[:, :512]), jnp.where(ci == 0, other[:, :512], mine[:, :512])],
        axis=1,
    )
    cut = lax.dynamic_slice_in_dim(cut, at, 256, 1)
    skip = jnp.zeros((ROUT, 256), F32)
    for k, w in enumerate([skip_w[0], cut[0], cut[1], cut[2]]):
        part = lax.dynamic_slice_in_dim(dzs, where[k] * 512, 512, 1)
        skip = skip + dot_t(part, w)
    o1, dimage_local, dimage_global, gr1 = launch(
        "back_reduce_one",
        back_one_kernel,
        [(where, SM)] + [(v, VM) for v in (bt1, st1, z1, dv1, gb1)] + [(g1, ANY), (skip, VM)],
        [
            shape((RIN, 128), BF),
            shape((12, 6, 6, 256)),
            shape((6, 14, 14, 256)),
            mid_grad,
        ],
        [
            pltpu.VMEM((RIN, 512), BF),
            pltpu.VMEM((2, RIN, 128), F32),
            pltpu.VMEM((32, 32, 512), BF),
            pltpu.SemaphoreType.DMA((4,)),
        ],
        (2 * RIN * 512 * 256, 16_000_000),
    )
    gw1 = jnp.zeros((4, 256, 128), F32)
    for k in range(4):
        gw1 = lax.dynamic_update_index_in_dim(gw1, dot_w(xs[k], o1), where[k], 0)
    gw1 = gw1.reshape(1024, 128)

    t6, t5, t4w, t3, ts = batch_total([gw6, gw5, gw4, gw3, gws])
    t2, t1w = batch_total([gw2, gw1])
    totals = [t1w, t2, t3, ts, t4w, t5, t6]
    weight_sq = jnp.stack([jnp.sum(jnp.square(w.astype(F32))) for w in own])
    grad_sq = jnp.stack([jnp.sum(jnp.square(t)) for t in totals])
    sq = lax.psum(jnp.stack([weight_sq, grad_sq]), "z")
    weight_norm = jnp.sqrt(sq[0])
    ratios = weight_norm / (jnp.sqrt(sq[1]) / 12864.0 + DECAY * weight_norm)

    def cut_own(v, n):
        return lax.dynamic_slice_in_dim(v, zi * n, n, 2)

    mids = cut_own(jnp.stack([gr1, gr2, gr4, gr5]), 128)
    wides = cut_own(jnp.stack([gr3, grs, gr6]), 512)
    return (
        output_global,
        output_local,
        dimage_global,
        dimage_local,
        totals[0],
        totals[1].reshape(spatial_one.shape),
        totals[2],
        totals[3],
        totals[4],
        totals[5].reshape(spatial_two.shape),
        totals[6],
        mids[:, 1],
        wides[:, 1],
        mids[:, 0],
        wides[:, 0],
        ratios,
    )


def solution(mesh):
    fine = Mesh(np.asarray(mesh.devices).reshape(4, 4, 2, 4), EVERY)
    crops = P(BATCH, None, None, "z")
    mat = P(None, "z")
    conv = P(None, None, None, "z")
    weights = (mat, conv, mat, mat, mat, conv, mat)
    return jax.shard_map(
        body,
        mesh=fine,
        in_specs=(crops,) * 4 + weights + (mat,) * 4,
        out_specs=(crops,) * 4 + weights + (mat,) * 4 + (P(),),
        check_vma=False,
    )
```

```python
import functools
import math

import jax
import jax.numpy as jnp
import numpy as np
from jax import lax
from jax.experimental import pallas as pl
from jax.experimental.pallas import tpu as pltpu
from jax.sharding import Mesh, PartitionSpec as P

EPS = 1e-05
DECAY = 5e-05
BATCH = ("y", "x", "c")
PLANE = ("y", "x")
EVERY = ("y", "x", "c", "z")
BF = jnp.bfloat16
F32 = jnp.float32
SLOPE = math.sqrt(2.0 / math.pi)
CUBE = 0.044715

LIN, GIN, RIN = 576, 1568, 2144
LOUT, GOUT, ROUT = 144, 392, 544
M_IN = (36 * 12 * 32.0, 196 * 6 * 32.0)
M_OUT = (9 * 12 * 32.0, 49 * 6 * 32.0)
ANY = pl.BlockSpec(memory_space=pltpu.HBM)
VM = pl.BlockSpec(memory_space=pltpu.VMEM)
NEAR = "near"
FAR = "far"
SM = pl.BlockSpec(memory_space=pltpu.SMEM)


def shape(dims, dtype=F32):
    return jax.ShapeDtypeStruct(dims, dtype)


def launch(name, body, ins, outs, scratch=(), cost=(0, 0)):
    def placed(a, s):
        if s is VM or s is SM:
            return a
        return pltpu.with_memory_space_constraint(a, pltpu.VMEM if s is NEAR else pltpu.HBM)

    return pl.pallas_call(
        body,
        name=name,
        out_shape=tuple(pltpu.HBM(o.shape, o.dtype) if s is not VM else o for o, s in outs),
        in_specs=[VM if s is NEAR else s for _, s in ins],
        out_specs=tuple(VM if s is FAR else s for _, s in outs),
        scratch_shapes=list(scratch),
        compiler_params=pltpu.CompilerParams(vmem_limit_bytes=50 * 1024 * 1024),
        cost_estimate=pl.CostEstimate(flops=cost[0], bytes_accessed=cost[1], transcendentals=0),
    )(*[placed(a, s) for a, s in ins])


def sems(*dims):
    return pltpu.SemaphoreType.DMA(dims)


def go(src, dst, sem):
    c = pltpu.make_async_copy(src, dst, sem)
    c.start()
    return c


def wait(copies):
    for c in copies:
        c.wait()


def quarter(n):
    return pl.ds(n * 512, 512)


def act(v):
    t = jnp.tanh(v * (SLOPE + (SLOPE * CUBE) * (v * v)))
    h = 0.5 * v
    return h + h * t


def slope(v):
    s = v * v
    t = jnp.tanh(v * (SLOPE + (SLOPE * CUBE) * s))
    p = 0.5 + 0.5 * t
    return p + p * (1.0 - t) * (v * (SLOPE + (3.0 * SLOPE * CUBE) * s))


def rows8(v):
    return jnp.sum(v.reshape(-1, 8, v.shape[-1]), axis=0)


def row1(v):
    return jnp.sum(v, axis=0, keepdims=True)


def coefs(sums, k, members, gb):
    g, b = gb
    m = sums[2 * k : 2 * k + 1] / members
    inv = lax.rsqrt(sums[2 * k + 1 : 2 * k + 2] / members - m * m + EPS)
    a = inv * g
    return m, inv, a, b - m * a


def back_coefs(sums, grads, k, members, gb):
    m, inv, a, _ = coefs(sums, k, members, gb)
    c1 = a * inv * (grads[2 * k + 1 : 2 * k + 2] / members)
    return a, c1, a * (grads[2 * k : 2 * k + 1] / members) - m * c1


def mid_gb(norms, i):
    return [
        jnp.concatenate([norms[z, r : r + 1, :] for z in range(4)], axis=1) for r in (i, 4 + i)
    ]


def out_gb(norms, i, z):
    return [
        jnp.concatenate([norms[z, r + l : r + l + 1, :] for l in range(4)], axis=1)
        for r in (8 + 4 * i, 20 + 4 * i)
    ]


def keep(rows, width, group, start):
    i = lax.broadcasted_iota(jnp.int32, (rows, width), 0)
    if group == 0:
        return (i & 15) < 12
    return ((i & 7) < 6) & (i + start < LOUT + GOUT)


def sweep(body, init):
    done = []
    for group, (first, steps, rows) in enumerate(((0, 1, 144), (144, 5, 80))):

        def step(s, carry, group=group, first=first, rows=rows):
            return body(group, pl.multiple_of(first + s * rows, 16), rows, carry)

        done.append(lax.fori_loop(0, steps, step, init))
    return done


LINES = ((0, 6, 96), (576, 14, 112))


def wide_sweep(body, init):
    done = []
    for group, (first, steps, rows) in enumerate(LINES):

        def step(s, carry, group=group, first=first, rows=rows):
            return body(group, s, pl.multiple_of(first + s * rows, 16), rows, carry)

        done.append(lax.fori_loop(0, steps, step, init))
    return done


def lines_in(src, dst, sem):
    for group, (first, steps, rows) in enumerate(LINES):
        for s in range(steps):
            here = pl.ds(first + s * rows, rows)
            go(src.at[here, :], dst.at[here, :], sem.at[6 * group + s])


def line_wait(src, dst, sem, group, s, start, rows):
    here = pl.ds(start, rows)
    pltpu.make_async_copy(src.at[here, :], dst.at[here, :], sem.at[6 * group + s]).wait()


def two(width):
    z = jnp.zeros((8, width), F32)
    return (z, z)


def put_stats(out, done, cols=None):
    rows = jnp.concatenate([row1(s) for group in done for s in group], axis=0)
    if cols is None:
        for p in range(out.shape[0]):
            out[p] = rows
    else:
        out[:, cols] = rows


def moments(z_ref, cols=slice(None)):
    def body(group, start, rows, carry):
        v = z_ref[pl.ds(start, rows), cols]
        return carry[0] + rows8(v), carry[1] + rows8(v * v)

    return sweep(body, two(512))


def added(st, cols=None):
    return jnp.sum(st[...] if cols is None else st[:, :, cols], axis=0)


def dot(a, b):
    return jnp.dot(a, b, preferred_element_type=F32)


def dot_t(a, b):
    return lax.dot_general(a, b, (((1,), (1,)), ((), ())), preferred_element_type=F32)


def riding_in(zi, tops, w, sem):
    return [
        go(
            tops[k].at[pl.ds(TOP, 512), pl.ds(128 * i, 128)],
            w.at[pl.ds(512 * i, 512), pl.ds(pl.multiple_of(zi[k] * 128, 128), 128)],
            sem.at[2 * k + i],
        )
        for k in range(4)
        for i in (0, 1)
    ]


def bundle_in(bundle, at, w, sem):
    n = w.shape[1]
    return [
        go(bundle.at[:, z, pl.ds(at, n), :], w.at[:, :, pl.ds(z * 128, 128)], sem.at[z])
        for z in range(4)
    ]


def bundle_out_in(bundle, at, w, sem):
    n = w.shape[1]
    return [
        go(
            bundle.at[:, z, pl.ds(at + n * j, n), :],
            w.at[:, :, pl.ds(z * 512 + j * 128, 128)],
            sem.at[4 * z + j],
        )
        for z in range(4)
        for j in range(4)
    ]


def halves_in(zi, srcs, w, sem):
    copies = [go(srcs[0], w.at[:, pl.ds(pl.multiple_of(zi[0] * 512, 512), 512)], sem.at[0])]
    for c in (0, 1):
        r = zi[4] * 512 if c == 0 else 512 - zi[4] * 512
        for i in range(6):
            cols = pl.ds(pl.multiple_of(zi[1 + i // 2] * 512, 512), 512)
            dst = w.at[pl.ds(pl.multiple_of(r + 256 * (i % 2), 256), 256), cols]
            copies.append(go(srcs[1 + 6 * c + i], dst, sem.at[1 + 6 * c + i]))
    return copies


def pack_kernel(side, cuts, local, glob, *refs):
    more, outs, tmp = refs[: -1 - len(cuts)], refs[-1 - len(cuts) : -1], refs[-1]
    tmp[...] = jnp.zeros_like(tmp)
    base = side[0] * side[0] * 16
    if more:
        outs[0][pl.ds(outs[0].shape[0] - 512, 512), 0:128] = more[0][0:512, :]
        outs[0][pl.ds(outs[0].shape[0] - 512, 512), 128:256] = more[0][512:1024, :]
    for lane in range(tmp.shape[0]):
        cols = slice(lane * 128, lane * 128 + 128)
        for n in range(12):
            for h in range(side[0]):
                v = local[n, h, :, cols].astype(F32)
                tmp[lane, pl.ds(h * side[0] * 16 + n, side[0], stride=16), :] = v
        for n in range(6):
            for h in range(side[1]):
                v = glob[n, h, :, cols].astype(F32)
                tmp[lane, pl.ds(base + h * side[1] * 8 + n, side[1], stride=8), :] = v
        at = 0
        for out, n in zip(outs, cuts):
            out[pl.ds(0, n), cols] = tmp[lane, pl.ds(at, n), :].astype(out.dtype)
            at += n


def pack(name, local, glob, side, cuts, more=()):
    c = local.shape[-1]
    rows = sum(cuts)
    extra = (512 * len(more), 0)
    return launch(
        name,
        functools.partial(pack_kernel, side, cuts),
        [(v, VM) for v in (local, glob) + more],
        [(shape((n + e, c), BF), VM) for n, e in zip(cuts, extra)],
        [pltpu.VMEM((c // 128, rows, 128), F32)],
        (0, 4 * rows * c),
    )


def unpack_kernel(side, lanes, local, glob):
    base = side[0] * side[0] * 16
    for lane in range(lanes.shape[0]):
        cols = slice(lane * 128, lane * 128 + 128)
        for n in range(12):
            for h in range(side[0]):
                v = lanes[lane, pl.ds(h * side[0] * 16 + n, side[0], stride=16), :]
                local[n, h, :, cols] = v
        for n in range(6):
            for h in range(side[1]):
                v = lanes[lane, pl.ds(base + h * side[1] * 8 + n, side[1], stride=8), :]
                glob[n, h, :, cols] = v


def unpack_whole(side, rows, local, glob, lanes):
    for lane in range(lanes.shape[0]):
        lanes[lane] = rows[:, lane * 128 : lane * 128 + 128]
    unpack_kernel(side, lanes, local, glob)


def unpack(name, rows, side):
    c = rows.shape[-1]
    return launch(
        name,
        functools.partial(unpack_whole, side),
        [(rows, VM)],
        [
            (shape((12, side[0], side[0], c)), VM),
            (shape((6, side[1], side[1], c)), VM),
        ],
        [pltpu.VMEM((c // 128,) + rows.shape[:1] + (128,), F32)],
        (0, 8 * rows.size),
    )


def pieces_kernel(at, spatial_one, expand_one, reduce_two, spatial_two, expand_two, near, late, sem):
    copies = []

    def take(src, dst, first):
        n = src.shape[0] // 32
        rows = pl.ds(pl.multiple_of(at[0] * n, 16), n)
        for j in range(src.shape[1] // 128):
            here = dst.at[pl.ds(first, n), :]
            copies.append(go(src.at[rows, pl.ds(128 * j, 128)], here, sem.at[len(copies)]))
            first += n

    take(spatial_one, near, 0)
    take(expand_one, near, 144)
    take(reduce_two, near, 208)
    take(spatial_two, late, 0)
    take(expand_two, late, 144)
    wait(copies)


def square_kernel(*refs):
    out = refs[-1]
    for i, w in enumerate(refs[:-1]):
        n = w.shape[0] // 8
        total = jnp.zeros((8, 128), F32)
        for lane in range(w.shape[1] // 128):
            cols = slice(lane * 128, lane * 128 + 128)

            def step(s, t, w=w, cols=cols, n=n):
                v = w[pl.ds(pl.multiple_of(s * n, 16), n), cols].astype(F32)
                return t + rows8(v * v)

            total = lax.fori_loop(0, 8, step, total)
        out[i] = total


PARTS = ((0, 576), (576, 224), (800, 672), (1472, 672))
TOP = 800


def wide_moments(z_ref, parts):
    z8 = jnp.zeros((8, 512), F32)
    carry = (z8, z8)
    for first, rows in parts:

        def step(s, c, first=first):
            v = z_ref[pl.ds(pl.multiple_of(first + s * 64, 16), 64), :]
            return c[0] + rows8(v), c[1] + rows8(v * v)

        carry = lax.fori_loop(0, rows // 64, step, carry)
        left = rows % 64
        if left:
            v = z_ref[pl.ds(first + rows - left, left), :]
            carry = (carry[0] + rows8(v), carry[1] + rows8(v * v))
    return carry


def first_kernel(zi, *refs):
    xs, rest = refs[:8], refs[8:]
    z1, stats, xv, zv, w, xsem, osem, ws = rest
    weight = riding_in(zi, xs[::2], w, ws)
    cin = []
    for i, (first, rows) in enumerate(PARTS):
        half, base = (0, 0) if first < TOP else (1, TOP)
        one = []
        for k in range(4):
            cols = pl.ds(pl.multiple_of(zi[k] * 256, 256), 256)
            src = xs[2 * k + half].at[pl.ds(first - base, rows), :]
            one.append(go(src, xv.at[pl.ds(first, rows), cols], xsem.at[i, k]))
        cin.append(one)
    wait(weight)
    wf = w
    out, sums = [], []
    for i, (first, rows) in enumerate(PARTS):
        here = pl.ds(first, rows)
        wait(cin[i])
        zv[here, :] = dot(xv[here, :], wf[...])
        out.append(go(zv.at[here, :], z1.at[here, :], osem.at[i]))
    put_stats(stats, [wide_moments(zv, PARTS[:1]), wide_moments(zv, PARTS[1:])])
    wait(out)


def load_taps(local, glob, i, j, stride):
    c = local.shape[-1]
    if stride == 2:
        lv = local.reshape(4, 2, 4, 2, 16, c)
        gv = glob.reshape(8, 2, 8, 2, 8, c)
        a, p, b, q = i // 2, i % 2, j // 2, j % 2
        lt = lv[a : a + 3, p, b : b + 3, q]
        gt = gv[a : a + 7, p, b : b + 7, q]
    else:
        lt = local[i : i + 3, j : j + 3]
        gt = glob[i : i + 7, j : j + 7]
    return jnp.concatenate(
        [lt.reshape(LOUT, c), gt.reshape(GOUT, c), jnp.zeros((8, c), F32)], axis=0
    )


def clear_border(ref):
    side = ref.shape[0]
    zero = jnp.zeros((side,) + ref.shape[2:], F32)
    ref[0] = zero
    ref[side - 1] = zero
    for r in range(1, side - 1):
        ref[r, 0] = zero[0]
        ref[r, side - 1] = zero[0]


def conv_tail(stride, hl, hg, weight, wf, tv, taps, ts, zv, z, zsem, stats):
    out = []
    for k in range(9):
        cols = pl.ds(k * 512, 512)
        tv[:, cols] = load_taps(hl, hg, k // 3, k % 3, stride).astype(BF)
        out.append(go(tv.at[:, cols], taps.at[:, cols], ts.at[k]))
        if k == 0:
            wait(weight)
            zv[...] = dot(tv[:, cols], wf[0:512, :])
        else:
            zv[...] += dot(tv[:, cols], wf[k * 512 : (k + 1) * 512, :])
    out.append(go(zv, z, zsem))
    put_stats(stats, moments(zv))
    wait(out)


def second_kernel(st, norms, z1, near, taps, z2, stats, sums, zin, hl, hg, w, tv, zv, xs, ws, ts, zsem):
    lines_in(z1, zin, xs)
    weight = bundle_in(near, 0, w, ws)
    total = added(st)
    sums[...] = total
    gb = mid_gb(norms, 0)
    cs = [coefs(total, k, M_IN[k], gb) for k in (0, 1)]
    clear_border(hl)
    clear_border(hg)

    def body(group, s, start, rows, carry):
        _, _, a, sh = cs[group]
        line_wait(z1, zin, xs, group, s, start, rows)
        i = lax.broadcasted_iota(jnp.int32, (rows, 512), 0)
        ok = (i & 15) < 12 if group == 0 else (i & 7) < 6
        h = jnp.where(ok, act(zin[pl.ds(start, rows), :] * a + sh), 0.0)
        if group == 0:
            hl[s + 1, 1:7] = h.reshape(6, 16, 512)
        else:
            hg[s + 1, 1:15] = h.reshape(14, 8, 512)
        return carry

    wide_sweep(body, 0)
    conv_tail(2, hl, hg, weight, w.reshape(4608, 512), tv, taps, ts, zv, z2, zsem.at[0], stats)


def fifth_kernel(st, norms, z4, late, taps, z5, stats, sums, zin, hl, hg, w, tv, zv, xs, ws, ts, zsem):
    cin = go(z4, zin, xs.at[0])
    weight = bundle_in(late, 0, w, ws)
    total = added(st)
    sums[...] = total
    gb = mid_gb(norms, 2)
    cs = [coefs(total, k, M_OUT[k], gb) for k in (0, 1)]
    clear_border(hl)
    clear_border(hg)
    cin.wait()
    for group, (first, side, rows) in enumerate(((0, 3, 48), (144, 7, 56))):
        _, _, a, sh = cs[group]
        i = lax.broadcasted_iota(jnp.int32, (rows, 512), 0)
        ok = (i & 15) < 12 if group == 0 else (i & 7) < 6

        def step(s, carry, group=group, first=first, rows=rows, a=a, sh=sh, ok=ok):
            v = zin[pl.ds(pl.multiple_of(first + s * rows, 8), rows), :]
            h = jnp.where(ok, act(v * a + sh), 0.0)
            if group == 0:
                hl[s + 1, 1:4] = h.reshape(3, 16, 512)
            else:
                hg[s + 1, 1:8] = h.reshape(7, 8, 512)
            return carry

        lax.fori_loop(0, side, step, 0)
    conv_tail(1, hl, hg, weight, w.reshape(4608, 512), tv, taps, ts, zv, z5, zsem.at[0], stats)


def conv_call(name, kernel, ins, rows, sides, n, flops):
    sl, sg = sides
    return launch(
        name,
        kernel,
        ins,
        [
            (shape((ROUT, 4608), BF), ANY),
            (shape((ROUT, 512)), ANY),
            (shape((32, 4, 512)), FAR),
            (shape((4, 512)), VM),
        ],
        [
            pltpu.VMEM((rows, 512), F32),
            pltpu.VMEM((sl, sl, 16, 512), F32),
            pltpu.VMEM((sg, sg, 8, 512), F32),
            pltpu.VMEM((32, 144, 512), BF),
            pltpu.VMEM((ROUT, 4608), BF),
            pltpu.VMEM((ROUT, 512), F32),
            sems(n),
            sems(13),
            sems(9),
            sems(1),
        ],
        (flops, 20_000_000),
    )


def expand_kernel(which, at, st, norms, z, bundle, h, zo, stats, sums, zin, hv, zv, w, wsem, hsem, zsem, isem):
    cin = go(z, zin, isem.at[0])
    weight = bundle_out_in(bundle, at, w.reshape(32, 16, 2048), wsem)
    total = added(st)
    sums[...] = total
    gb = mid_gb(norms, which)
    cs = [coefs(total, k, M_OUT[k], gb) for k in (0, 1)]
    cin.wait()

    def body(group, start, rows, carry):
        _, _, a, sh = cs[group]
        v = act(zin[pl.ds(start, rows), :] * a + sh)
        hv[pl.ds(start, rows), :] = jnp.where(keep(rows, 512, group, start), v, 0.0).astype(BF)
        return carry

    sweep(body, 0)
    out = [go(hv, h, hsem.at[0])]
    wait(weight)
    for n in range(4):
        cols = quarter(n)
        zv[:, cols] = dot(hv[...], w[:, cols])
        out.append(go(zv.at[:, cols], zo.at[:, cols], zsem.at[n]))
        put_stats(stats, moments(zv, cols), cols)
    wait(out)


def expand_call(name, which, at, st, norms, z, bundle):
    return launch(
        name,
        functools.partial(expand_kernel, which, at),
        [(st, NEAR), (norms, VM), (z, ANY), (bundle, ANY)],
        [
            (shape((ROUT, 512), BF), ANY),
            (shape((ROUT, 2048)), ANY),
            (shape((4, 2048)), VM),
            (shape((4, 512)), VM),
        ],
        [
            pltpu.VMEM((ROUT, 512), F32),
            pltpu.VMEM((ROUT, 512), BF),
            pltpu.VMEM((ROUT, 2048), F32),
            pltpu.VMEM((512, 2048), BF),
            sems(16),
            sems(1),
            sems(4),
            sems(1),
        ],
        (2 * 544 * 512 * 2048, 9_000_000),
    )


def skip_kernel(zi, *refs):
    x, srcs, rest = refs[:8], refs[8:21], refs[21:]
    xe, zs, stats, xv, ev, tmp, zv, w, xs, ws, es, os = rest
    xin = [
        [
            go(x[2 * k].at[pl.ds(0, TOP), :], xv.at[k, pl.ds(0, TOP), :], xs.at[k, 0]),
            go(x[2 * k + 1], xv.at[k, pl.ds(TOP, RIN - TOP), :], xs.at[k, 1]),
        ]
        for k in range(4)
    ]
    weight = halves_in(zi, srcs, w, ws)
    tmp[pl.ds(536, 8), :] = jnp.zeros((8, 256), F32)
    for k in range(4):
        wait(xin[k])
        for r in range(3):
            v = xv[k, pl.ds(r * 192, 96), :].astype(F32).reshape(3, 2, 16, 256)[:, 0]
            tmp[pl.ds(r * 48, 48), :] = v.reshape(48, 256)
        for r in range(7):
            v = xv[k, pl.ds(576 + r * 224, 112), :].astype(F32).reshape(7, 2, 8, 256)[:, 0]
            tmp[pl.ds(144 + r * 56, 56), :] = v.reshape(56, 256)
        at = pl.multiple_of(zi[k] * 256, 256)
        ev[:, pl.ds(at, 256)] = tmp[...].astype(BF)
    out = [go(ev, xe, es.at[0])]
    wait(weight)
    for n in range(4):
        cols = quarter(n)
        zv[:, cols] = dot(ev[...], w[:, cols])
        out.append(go(zv.at[:, cols], zs.at[:, cols], os.at[n]))
        put_stats(stats, moments(zv, cols), cols)
    wait(out)


def middle_kernel(st3, norms, z3, zs, late, mid, h3, z4, stats, sum3, sums, z3v, zsv, hv, zv, w, ins, ws, os, hs, zsem):
    cin = []
    for n in range(4):
        cols = quarter(n)
        cin.append(
            [go(z3.at[:, cols], z3v.at[:, cols], ins.at[0, n]), go(zs.at[:, cols], zsv.at[:, cols], ins.at[1, n])]
        )
    weight = bundle_in(late, 208, w, ws)
    wf = w.reshape(2048, 512)
    out = []
    for n in range(4):
        cols = quarter(n)
        both = added(st3, cols)
        s3, ss = both[0:4], both[4:8]
        sum3[:, cols] = s3
        sums[:, cols] = ss
        cs = []
        for k in (0, 1):
            _, _, a3, b3 = coefs(s3, k, M_OUT[k], out_gb(norms, 0, n))
            _, _, a5, b5 = coefs(ss, k, M_OUT[k], out_gb(norms, 1, n))
            cs.append((a3, a5, b3 + b5))
        wait(cin[n])

        def body(group, start, rows, carry, cols=cols, cs=cs):
            a3, a5, b = cs[group]
            here = (pl.ds(start, rows), cols)
            v = act(z3v[here] * a3 + zsv[here] * a5 + b)
            v = jnp.where(keep(rows, 512, group, start), v, 0.0)
            z3v[here] = v
            hv[here] = v.astype(BF)
            return carry

        sweep(body, 0)
        out.append(go(z3v.at[:, cols], mid.at[:, cols], os.at[n]))
        out.append(go(hv.at[:, cols], h3.at[:, cols], hs.at[n]))
        if n == 0:
            wait(weight)
            zv[...] = dot(hv[:, cols], wf[0:512, :])
        else:
            zv[...] += dot(hv[:, cols], wf[n * 512 : (n + 1) * 512, :])
    out.append(go(zv, z4, zsem.at[0]))
    put_stats(stats, moments(zv))
    wait(out)


def last_kernel(zi, st, norms, z6, mid, *refs):
    cots, rest = refs[:8], refs[8:]
    out, dv6, stats, sums, zv, mv, cv, ov, ins, os = rest
    cin = []
    for k in range(4):
        cols = pl.ds(pl.multiple_of(zi[k] * 512, 512), 512)
        cin.append(
            [
                go(z6.at[:, cols], zv.at[k], ins.at[0, k]),
                go(mid.at[:, cols], mv.at[k], ins.at[1, k]),
                go(cots[2 * k], cv.at[k, pl.ds(0, 272), :], ins.at[2, k]),
                go(cots[2 * k + 1], cv.at[k, pl.ds(272, 272), :], ins.at[3, k]),
            ]
        )
    sums[...] = added(st)
    done_out = []
    for k in range(4):
        cols = pl.ds(pl.multiple_of(zi[k] * 512, 512), 512)
        total = sums[:, cols]
        gb = out_gb(norms, 2, zi[k])
        cs = [coefs(total, j, M_OUT[j], gb) for j in (0, 1)]
        wait(cin[k])

        def body(group, start, rows, carry, cs=cs, k=k):
            m, _, a, sh = cs[group]
            here = pl.ds(start, rows)
            z = zv[k, here, :]
            v = z * a + sh + mv[k, here, :]
            if k == 0:
                ov[here, :] = act(v)
            d = slope(v) * cv[k, here, :].astype(F32)
            mv[k, here, :] = d
            return carry[0] + rows8(d), carry[1] + rows8(d * (z - m))

        done = sweep(body, two(512))
        done_out.append(go(mv.at[k], dv6.at[:, cols], os.at[k]))
        if k == 0:
            done_out.append(go(ov, out, os.at[4]))
        done = [(s, q * cs[j][1]) for j, (s, q) in enumerate(done)]
        put_stats(stats, done, cols)
    wait(done_out)


def grads_out(ref, grads, cols=slice(None)):
    ref[0:1, cols] = grads[0:1] + grads[2:3]
    ref[1:2, cols] = grads[1:2] + grads[3:4]


def slope_rows(dy, z, cs):
    def body(group, start, rows, carry):
        m, _, a, sh = cs[group]
        here = (pl.ds(start, rows), slice(None))
        v = z[here]
        d = jnp.where(keep(rows, 512, group, start), slope(v * a + sh) * dy[here], 0.0)
        dy[here] = d
        return carry[0] + rows8(d), carry[1] + rows8(d * (v - m))

    return [(s, q * cs[j][1]) for j, (s, q) in enumerate(sweep(body, two(512)))]


def norm_rows(dy, z, cs, cols, dz):
    def body(group, start, rows, carry):
        a, c1, c0 = cs[group]
        here = (pl.ds(start, rows), cols)
        d = a * dy[here] - c1 * z[here] - c0
        dz[here] = jnp.where(keep(rows, 512, group, start), d, 0.0).astype(dz.dtype)
        return carry

    sweep(body, 0)


def all_coefs(sums, gb):
    return [coefs(sums, k, M_OUT[k], gb) for k in (0, 1)]


def all_back(sums, grads, gb, members=M_OUT):
    return [back_coefs(sums, grads, k, members[k], gb) for k in (0, 1)]


def own_cols(dst, src, zi, width):
    at = pl.multiple_of(zi[0] * width, width)
    dst[...] = src[:, pl.ds(at, width)].astype(dst.dtype)


def back_six_kernel(zi, stb, norms, sum6, sum5, z6, dv6, z5, late, own, dv5, stats, grad, zv, dv, z5v, acc, dz, w, ins, i5, ws, os):
    cin = []
    for n in range(4):
        cols = quarter(n)
        cin.append(
            [go(z6.at[:, cols], zv.at[:, cols], ins.at[0, n]), go(dv6.at[:, cols], dv.at[:, cols], ins.at[1, n])]
        )
    weight = bundle_out_in(late, 144, w.reshape(32, 16, 2048), ws)
    c5 = go(z5, z5v, i5.at[0])
    for n in range(4):
        cols = quarter(n)
        grads = added(stb, cols)
        grads_out(grad, grads, cols)
        cs = all_back(sum6[:, cols], grads, out_gb(norms, 2, n))
        wait(cin[n])
        norm_rows(dv, zv, cs, cols, dz)
        if n == 0:
            wait(weight)
            acc[...] = dot_t(dz[:, cols], w[:, cols])
        else:
            acc[...] += dot_t(dz[:, cols], w[:, cols])
    own_cols(own, dz, zi, 512)
    c5.wait()
    done = slope_rows(acc, z5v, all_coefs(sum5[...], mid_gb(norms, 3)))
    out = go(acc, dv5, os.at[0])
    put_stats(stats, done)
    out.wait()


def pad_back(dzl, dzg, dz, at):
    dzl[...] = jnp.zeros_like(dzl)
    dzg[...] = jnp.zeros_like(dzg)
    for r in range(3):
        dzl[at + r, at : at + 3] = dz[pl.ds(48 * r, 48), :].reshape(3, 16, 512)
    for r in range(7):
        dzg[at + r, at : at + 7] = dz[pl.ds(144 + 56 * r, 56), :].reshape(7, 8, 512)


def back_five_kernel(zi, stb, norms, sum5, sum4, z5, dv5, z4, late, own, dv4, stats, grad, zv, dv, z4v, acc, dz, dzl, dzg, w, ins, ws, os):
    cin = [go(z5, zv, ins.at[0]), go(dv5, dv, ins.at[1])]
    weight = bundle_in(late, 0, w, ws)
    c4 = go(z4, z4v, ins.at[2])
    grads = added(stb)
    grads_out(grad, grads)
    cs = all_back(sum5[...], grads, mid_gb(norms, 3))
    wait(cin)
    norm_rows(dv, zv, cs, slice(None), dv)
    own_cols(own, dv, zi, 128)
    pad_back(dzl, dzg, dv, 1)
    wait(weight)
    wf = w.reshape(4608, 512)
    for k in range(9):
        dz[...] = load_taps(dzl, dzg, 2 - k // 3, 2 - k % 3, 1).astype(BF)
        part = dot_t(dz[...], wf[k * 512 : (k + 1) * 512, :])
        if k == 0:
            acc[...] = part
        else:
            acc[...] += part
    c4.wait()
    done = slope_rows(acc, z4v, all_coefs(sum4[...], mid_gb(norms, 2)))
    out = go(acc, dv4, os.at[0])
    put_stats(stats, done)
    out.wait()


def back_four_kernel(zi, stb, norms, sum4, sum3, sums, z4, dv4, dv6, z3, zs, late, own, dpre, stats, grad, zv, dv, d6, z3v, zsv, dz, w, in4, ins, ws, os):
    cin = [go(z4, zv, in4.at[0]), go(dv4, dv, in4.at[1])]
    weight = bundle_in(late, 208, w, ws)
    wide = []
    for n in range(4):
        cols = quarter(n)
        wide.append(
            [
                go(src.at[:, cols], dst.at[:, cols], ins.at[i, n])
                for i, (src, dst) in enumerate(((dv6, d6), (z3, z3v), (zs, zsv)))
            ]
        )
    grads = added(stb)
    grads_out(grad, grads)
    cs4 = all_back(sum4[...], grads, mid_gb(norms, 2))
    wait(cin)
    norm_rows(dv, zv, cs4, slice(None), dz)
    own_cols(own, dz, zi, 128)
    wait(weight)
    wf = w.reshape(2048, 512)
    z8 = jnp.zeros((8, 512), F32)
    out = []
    for n in range(4):
        cols = quarter(n)
        s3, ss = sum3[:, cols], sums[:, cols]
        cs = []
        for k in (0, 1):
            m3, i3, a3, b3 = coefs(s3, k, M_OUT[k], out_gb(norms, 0, n))
            ms, is_, a5, b5 = coefs(ss, k, M_OUT[k], out_gb(norms, 1, n))
            cs.append((a3, a5, b3 + b5, m3, ms, i3, is_))
        zv[...] = dot_t(dz[...], wf[n * 512 : (n + 1) * 512, :])
        wait(wide[n])

        def body(group, start, rows, carry, cols=cols, cs=cs):
            a3, a5, b, m3, ms, _, _ = cs[group]
            here = (pl.ds(start, rows), cols)
            u, v = z3v[here], zsv[here]
            d = slope(u * a3 + v * a5 + b) * (zv[pl.ds(start, rows), :] + d6[here])
            d = jnp.where(keep(rows, 512, group, start), d, 0.0)
            d6[here] = d
            return (
                carry[0] + rows8(d),
                carry[1] + rows8(d * (u - m3)),
                carry[2] + rows8(d * (v - ms)),
            )

        done = sweep(body, (z8, z8, z8))
        out.append(go(d6.at[:, cols], dpre.at[:, cols], os.at[n]))
        done = [(s, p * cs[j][5], q * cs[j][6]) for j, (s, p, q) in enumerate(done)]
        put_stats(stats, done, cols)
    wait(out)


def pick(grads, rows):
    return jnp.concatenate([grads[r : r + 1] for r in rows], axis=0)


def back_three_kernel(zi, stb, norms, sum3, sum2, z3, dpre, z2, bundle, own, dv2, stats, grad, gsum, zv, dv, z2v, acc, dz, w, ins, i2, ws, os):
    cin = []
    for n in range(4):
        cols = quarter(n)
        cin.append(
            [go(z3.at[:, cols], zv.at[:, cols], ins.at[0, n]), go(dpre.at[:, cols], dv.at[:, cols], ins.at[1, n])]
        )
    weight = bundle_out_in(bundle, 144, w.reshape(32, 16, 2048), ws)
    c2 = go(z2, z2v, i2.at[0])
    for n in range(4):
        cols = quarter(n)
        grads = added(stb, cols)
        gsum[:, cols] = pick(grads, (0, 2, 3, 5))
        grads = pick(grads, (0, 1, 3, 4))
        grads_out(grad, grads, cols)
        cs = all_back(sum3[:, cols], grads, out_gb(norms, 0, n))
        wait(cin[n])
        norm_rows(dv, zv, cs, cols, dz)
        if n == 0:
            wait(weight)
            acc[...] = dot_t(dz[:, cols], w[:, cols])
        else:
            acc[...] += dot_t(dz[:, cols], w[:, cols])
    own_cols(own, dz, zi, 512)
    c2.wait()
    done = slope_rows(acc, z2v, all_coefs(sum2[...], mid_gb(norms, 1)))
    out = go(acc, dv2, os.at[0])
    put_stats(stats, done)
    out.wait()


def back_skip_kernel(zi, norms, gsum, sums, zs, dpre, *refs):
    srcs, rest = refs[:13], refs[13:]
    own, skip, grad, zv, dv, dz, w, ins, ws = rest
    cin = []
    for n in range(4):
        cols = quarter(n)
        cin.append(
            [go(zs.at[:, cols], zv.at[:, cols], ins.at[0, n]), go(dpre.at[:, cols], dv.at[:, cols], ins.at[1, n])]
        )
    mine = pl.ds(pl.multiple_of(zi[0] * 256, 256), 256)
    cols = [pl.ds(pl.multiple_of(zi[k] * 512, 512), 512) for k in range(4)]
    weight = [go(srcs[0].at[mine, :], w.at[:, cols[0]], ws.at[0])]
    which = jnp.where(zi[0] // 2 == zi[4], 0, 2) + zi[0] % 2
    for v in range(4):

        @pl.when(which == v)
        def _(v=v):
            for k in (1, 2, 3):
                go(srcs[1 + 6 * (v // 2) + 2 * (k - 1) + v % 2], w.at[:, cols[k]], ws.at[k])

    for n in range(4):
        here = quarter(n)
        grads = gsum[:, here]
        grads_out(grad, grads, here)
        cs = all_back(sums[:, here], grads, out_gb(norms, 1, n))
        wait(cin[n])
        norm_rows(dv, zv, cs, here, dz)
    own_cols(own, dz, zi, 512)
    wait(weight)
    for k in (1, 2, 3):
        pltpu.make_async_copy(srcs[1], w.at[:, cols[k]], ws.at[k]).wait()
    skip[...] = dot_t(dz[...], w[...])


def back_two_kernel(zi, stb, norms, sum2, sum1, z2, dv2, z1, near, *refs):
    (own, dv1, stats, grad, zv, dv, dz, acc, dzl, dzg, w, z1v, ins, ws, os) = refs
    cin = [go(z2, zv, ins.at[0]), go(dv2, dv, ins.at[1])]
    weight = bundle_in(near, 0, w, ws)
    c1 = go(z1, z1v, ins.at[2])
    grads = added(stb)
    grads_out(grad, grads)
    cs = all_back(sum2[...], grads, mid_gb(norms, 1))
    wait(cin)
    norm_rows(dv, zv, cs, slice(None), dv)
    own_cols(own, dv, zi, 128)
    pad_back(dzl, dzg, dv, 0)
    wait(weight)
    wf = w.reshape(4608, 512)
    gb1 = mid_gb(norms, 0)
    c1s = [coefs(sum1[...], k, M_IN[k], gb1) for k in (0, 1)]
    reach = (((1, 0),), ((2, 0), (0, 1)))
    z8 = jnp.zeros((8, 512), F32)
    totals = [(z8, z8), (z8, z8)]
    out = []
    for p in (0, 1):
        for q in (0, 1):
            first = True
            for i, di in reach[p]:
                for j, dj in reach[q]:
                    k = 3 * i + j
                    dz[...] = load_taps(dzl, dzg, di, dj, 1).astype(BF)
                    part = dot_t(dz[...], wf[k * 512 : (k + 1) * 512, :])
                    if first:
                        acc[...] = part
                    else:
                        acc[...] += part
                    first = False
            if p == 0 and q == 0:
                c1.wait()
            for group, (base, side, n, from_row) in enumerate(((0, 3, 16, 0), (576, 7, 8, 144))):
                m, _, a, sh = c1s[group]
                rows = side * n
                i_ = lax.broadcasted_iota(jnp.int32, (rows, 512), 0)
                okay = (i_ & 15) < 12 if group == 0 else (i_ & 7) < 6
                cells = z1v.at[pl.ds(base, 4 * side * side * n), :]
                cells = cells.reshape(side, 2, side, 2, n, 512)

                def step(r, carry, n=n, side=side, rows=rows, from_row=from_row, m=m, a=a, sh=sh, okay=okay, cells=cells, p=p, q=q):
                    v = cells[r, p, :, q].reshape(rows, 512)
                    g = acc[pl.ds(pl.multiple_of(from_row + r * rows, 8), rows), :]
                    d = jnp.where(okay, slope(v * a + sh) * g, 0.0)
                    cells[r, p, :, q] = d.reshape(side, n, 512)
                    return carry[0] + rows8(d), carry[1] + rows8(d * (v - m))

                totals[group] = lax.fori_loop(0, side, step, totals[group])
        for group, (first_row, steps, rows) in enumerate(LINES):
            for s in range(p, steps, 2):
                here = pl.ds(first_row + s * rows, rows)
                out.append(go(z1v.at[here, :], dv1.at[here, :], os.at[6 * group + s]))
    put_stats(stats, [(s, t * c1s[j][1]) for j, (s, t) in enumerate(totals)])
    wait(out)


def back_one_kernel(zi, stb, norms, sum1, z1, dv1, own, dz1, grad, zv, dv, dzv, is0, is1, os):
    lines_in(z1, zv, is0)
    lines_in(dv1, dv, is1)
    grads = added(stb)
    grads_out(grad, grads)
    cs = all_back(sum1[...], grads, mid_gb(norms, 0), M_IN)

    def body(group, s, start, rows, carry):
        a, c1, c0 = cs[group]
        line_wait(z1, zv, is0, group, s, start, rows)
        line_wait(dv1, dv, is1, group, s, start, rows)
        here = (pl.ds(start, rows), slice(None))
        i = lax.broadcasted_iota(jnp.int32, (rows, 512), 0)
        ok = (i & 15) < 12 if group == 0 else (i & 7) < 6
        d = a * dv[here] - c1 * zv[here] - c0
        dzv[here] = jnp.where(ok, d, 0.0).astype(BF)
        return carry

    wide_sweep(body, 0)
    out = go(dzv, dz1, os.at[0])
    own_cols(own, dzv, zi, 128)
    out.wait()


def image_kernel(zi, dz1, t0, t1, t2, t3, skip, local, glob, img, w, ws):
    wait(riding_in(zi, (t0, t1, t2, t3), w, ws))
    mine = w[pl.ds(pl.multiple_of(zi[0] * 256, 256), 256), :]
    for lane in range(2):
        cols = slice(lane * 128, lane * 128 + 128)
        img[lane] = dot_t(dz1[...], mine[lane * 128 : lane * 128 + 128])
        lv = img.at[lane, pl.ds(0, LIN)].reshape(3, 2, 3, 2, 16, 128)
        gv = img.at[lane, pl.ds(LIN, GIN)].reshape(7, 2, 7, 2, 8, 128)
        lv[:, 0, :, 0] += skip[pl.ds(0, LOUT), cols].reshape(3, 3, 16, 128)
        gv[:, 0, :, 0] += skip[pl.ds(LOUT, GOUT), cols].reshape(7, 7, 8, 128)
    unpack_kernel((6, 14), img, local, glob)


def flipped(a, bt):
    return dot(bt, a).T.astype(BF)


def halves_out(zi, a, bt, width, held, give, at):
    for c, dst in enumerate((held, give)):
        half = zi[4] if c == 0 else 1 - zi[4]
        begin = pl.multiple_of(half * width, width)
        for k in range(0, width, 256):
            n = min(256, width - k)
            v = flipped(a[:, pl.ds(pl.multiple_of(begin + k, 128), n)], bt)
            for j in range(v.shape[1] // 128):
                row = at + j * width + k
                dst[row : row + n, :] = v[:, 128 * j : 128 * (j + 1)]


def grad_kernel(widths, zi, *refs):
    held, give = refs[-2:]
    at = 0
    for i, width in enumerate(widths):
        a, b = refs[2 * i], refs[2 * i + 1]
        bt = b[...].astype(F32).T.astype(BF)
        halves_out(zi, a, bt, width, held, give, at)
        at += width * b.shape[1] // 128


def grad_call(name, zi, pairs):
    widths = [a.shape[1] // 2 for a, _ in pairs]
    rows = sum(a.shape[1] * b.shape[1] // 256 for a, b in pairs)
    return launch(
        name,
        functools.partial(grad_kernel, widths),
        [(zi, SM)] + [(v, VM) for pair in pairs for v in pair],
        [(shape((rows, 128), BF), VM)] * 2,
        (),
        (4 * ROUT * rows * 128, 7_000_000),
    )


def first_grad_kernel(zi, *refs):
    xs, (o1, held, give) = refs[:8], refs[8:]
    bt = o1[...].astype(F32).T.astype(BF)
    for k in range(4):
        v = dot(bt[:, :768], xs[2 * k][0:768, :]) + dot(bt[:, 896:], xs[2 * k + 1][96:, :])
        edge = jnp.concatenate([xs[2 * k][768:800, :], xs[2 * k + 1][0:96, :]], axis=0)
        v = v + dot(bt[:, 768:896], edge)
        v = v.T.astype(BF)
        mine = zi[4] == k // 2
        rows = slice((k % 2) * 256, (k % 2) * 256 + 256)

        @pl.when(mine)
        def _():
            held[rows, :] = v

        @pl.when(jnp.logical_not(mine))
        def _():
            give[rows, :] = v


SPANS = (
    (6, 0, 1024),
    (5, 1024, 3328),
    (4, 3328, 4352),
    (2, 4352, 5376),
    (3, 5376, 7424),
), ((1, 0, 2304), (0, 2304, 2816))


def slice_kernel(at, some, rest, out):
    squares = [jnp.zeros((1, 128), F32)] * 8
    first = 0
    for src, spans in zip((some, rest), SPANS):
        n = src.shape[1]
        v = src[0].astype(F32)
        for p in range(1, 16):
            v = v + src[p].astype(F32)
        out[first : first + n, :] = v.astype(BF)
        first += n
        v = v * v
        row = lax.broadcasted_iota(jnp.int32, (n, 128), 0) + at[0] * n
        for i, lo, hi in spans:
            squares[i] = row1(jnp.where((row >= lo) & (row < hi), v, 0.0))
    left = jnp.concatenate(squares + squares, axis=0)
    for k in range(3):
        part = left.astype(BF)
        out[first + 16 * k : first + 16 * k + 16, :] = part
        left = left - part.astype(F32)


def spill_kernel(other, zi, src, *refs):
    refs = refs[7:] if other else refs
    outs, (v6, v5, v4, v3, vs, v2, v1, fa, fb, ins, sem) = refs[:7], refs[7:]
    cin = [
        go(src.at[:, pl.ds(0, 464), :], fa.reshape(16, 464, 128), ins.at[0]),
        go(src.at[:, pl.ds(464, 176), :], fb.reshape(16, 176, 128), ins.at[1]),
    ]
    c = 1 - zi[4] if other else zi[4]
    copies = []
    plan = (
        (v5, 1, fa, 1024, 2304, 1),
        (vs, 4, fa, 5376, 512, 4),
        (v6, 0, fa, 0, 256, 4),
        (v4, 2, fa, 3328, 1024, 1),
        (v3, 3, fa, 4352, 256, 4),
        (v2, 5, fb, 0, 2304, 1),
    )
    cin[0].wait()
    for dst, i, flat, at, n, blocks in plan:
        if i == 5:
            cin[1].wait()
        for j in range(blocks):
            dst[:, 128 * j : 128 * (j + 1)] = flat[at + j * n : at + (j + 1) * n, :].astype(F32)
        rows = pl.ds(pl.multiple_of(c * n, n), n)
        copies.append(go(dst, outs[i].at[rows, :], sem.at[i]))
    for k in range(2):
        v1[256 * k : 256 * (k + 1), :] = fb[2304 + 256 * k : 2560 + 256 * k, :].astype(F32)
        rows = pl.ds(pl.multiple_of(zi[2 * c + k] * 256, 256), 256)
        copies.append(go(v1.at[pl.ds(256 * k, 256), :], outs[6].at[rows, :], sem.at[6 + k]))
    wait(copies)


GRADS = ((512, 512), (4608, 128), (2048, 128), (512, 512), (1024, 512), (4608, 128), (1024, 128))


def spill(name, zi, src, before):
    other = bool(before)
    return pl.pallas_call(
        functools.partial(spill_kernel, other),
        name=name,
        out_shape=tuple(pltpu.HBM(d, F32) for d in GRADS),
        in_specs=[SM, ANY] + [ANY] * len(before),
        out_specs=tuple(ANY for _ in GRADS),
        scratch_shapes=[pltpu.VMEM((r // 2, c), F32) for r, c in GRADS]
        + [pltpu.VMEM((7424, 128), BF), pltpu.VMEM((2816, 128), BF), sems(2), sems(8)],
        input_output_aliases={2 + i: i for i in range(len(before))},
        compiler_params=pltpu.CompilerParams(vmem_limit_bytes=50 * 1024 * 1024),
        cost_estimate=pl.CostEstimate(flops=0, bytes_accessed=8_000_000, transcendentals=0),
    )(zi, src, *before)


def ring(n, k):
    return [(i, (i + k) % n) for i in range(n)]


def spread(v, axes, n):
    return lax.all_to_all(jnp.broadcast_to(v[None], (n,) + v.shape), axes, 0, 0)


def share(v):
    v = v + lax.ppermute(v, "c", ring(2, 1))
    return spread(v, PLANE, 16)


def tell(v):
    return lax.all_to_all(v, BATCH, 0, 0)


def tie(*vs):
    return lax.optimization_barrier(vs)


def plane_index():
    return lax.axis_index("y") * 4 + lax.axis_index("x")


def piece(shard, index):
    n = shard.shape[0] // 32
    return lax.dynamic_slice_in_dim(shard, index * n, n, 0)


def swap(v):
    return lax.ppermute(v, "c", ring(2, 1))


def around(parts):
    left = [lax.ppermute(v, "z", ring(4, 1)) for v in parts]
    right = [lax.ppermute(v, "z", ring(4, 3)) for v in parts]
    left[0], left[1], right[0], right[1] = tie(*left, *right)
    far = [lax.ppermute(left[0], "z", ring(4, 1)), lax.ppermute(right[1], "z", ring(4, 3))]
    return right, far, left


def after(v, *first):
    return tie(v, *first)[0]


def add_halves(held, give):
    return (held.astype(F32) + swap(give).astype(F32)).astype(BF)


def body(
    image_global,
    image_local,
    cotangent_global,
    cotangent_local,
    reduce_one,
    spatial_one,
    expand_one,
    shortcut,
    reduce_two,
    spatial_two,
    expand_two,
    factors_mid,
    factors_out,
    shifts_mid,
    shifts_out,
):
    zi = lax.axis_index("z")
    ci = lax.axis_index("c")
    where = jnp.stack([zi, (zi + 1) % 4, (zi + 2) % 4, (zi + 3) % 4, ci]).astype(jnp.int32)
    flat2, flat5 = spatial_one.reshape(-1, 128), spatial_two.reshape(-1, 128)
    own = [reduce_one, flat2, expand_one, shortcut, reduce_two, flat5, expand_two]

    x = pack(
        "pack_image", image_local, image_global, (6, 14), (TOP, RIN - TOP), (reduce_one,)
    )
    x_right, x_far, x_left = around(x)
    xs = tuple(x) + tuple(x_right) + tuple(x_far) + tuple(x_left)

    norms = jnp.concatenate(
        [factors_mid, shifts_mid, factors_out.reshape(12, 128), shifts_out.reshape(12, 128)]
    )
    norms = after(norms, x[0])
    high = lax.reduce_precision(norms, 8, 7)
    middle = lax.reduce_precision(norms - high, 8, 7)
    low = norms - high - middle
    norms = spread(jnp.concatenate([v.astype(BF) for v in (high, middle, low)]), "z", 4)
    norms = norms[:, 0:32].astype(F32) + norms[:, 32:64].astype(F32) + norms[:, 64:96].astype(F32)

    xs = tuple(after(v, norms) for v in xs)

    near, late = launch(
        "pieces",
        pieces_kernel,
        [((plane_index() * 2 + ci).reshape(1).astype(jnp.int32), SM)]
        + [(after(v, x[0]), ANY) for v in (flat2, expand_one, reduce_two, flat5, expand_two)],
        [(shape((272, 128), BF), VM), (shape((208, 128), BF), VM)],
        [sems(14)],
    )
    near = lax.all_gather(near, EVERY, axis=0).reshape(32, 4, 272, 128)
    late = lax.all_gather(late, EVERY, axis=0).reshape(32, 4, 208, 128)

    cot = pack("pack_cotangent", cotangent_local, cotangent_global, (3, 7), (272, 272))
    c_right, c_far, c_left = around(cot)
    cots = tuple(cot) + tuple(c_right) + tuple(c_far) + tuple(c_left)
    square = launch(
        "weight_squares",
        square_kernel,
        [(w, VM) for w in own],
        [(shape((7, 8, 128)), VM)],
        (),
        (0, 6_000_000),
    )[0]

    mid_stats = (shape((32, 4, 512)), FAR)
    out_stats = (shape((4, 2048)), VM)
    narrow, wide = (shape((ROUT, 512)), ANY), (shape((ROUT, 2048)), ANY)
    z1, s1 = launch(
        "reduce_one",
        first_kernel,
        [(where, SM)] + [(v, ANY) for v in xs],
        [(shape((RIN, 512)), ANY), mid_stats],
        [
            pltpu.VMEM((RIN, 1024), BF),
            pltpu.VMEM((RIN, 512), F32),
            pltpu.VMEM((1024, 512), BF),
            sems(4, 4),
            sems(4),
            sems(8),
        ],
        (2 * RIN * 1024 * 512, 10_000_000),
    )
    parts = [lax.dynamic_slice_in_dim(shortcut, ci * 512 + 256 * i, 256, 0) for i in (0, 1)]
    st1 = tell(s1)
    p_right, p_far, p_left = around([after(v, st1) for v in parts])
    skips = tuple(p_right) + tuple(p_far) + tuple(p_left)
    skips = (shortcut,) + skips + tuple(swap(v) for v in skips)
    t1, z2, s2, sum1 = conv_call(
        "spatial_one",
        second_kernel,
        [(st1, NEAR), (norms, VM), (z1, ANY), (near, ANY)],
        RIN,
        (8, 16),
        20,
        40_000_000_000,
    )
    st2 = tell(s2)
    xe, zs, ss = launch(
        "shortcut",
        skip_kernel,
        [(where, SM)] + [(v, ANY) for v in xs + skips],
        [(shape((ROUT, 1024), BF), ANY), wide, out_stats],
        [
            pltpu.VMEM((4, RIN, 256), BF),
            pltpu.VMEM((ROUT, 1024), BF),
            pltpu.VMEM((ROUT, 256), F32),
            pltpu.VMEM((ROUT, 2048), F32),
            pltpu.VMEM((1024, 2048), BF),
            sems(4, 2),
            sems(16),
            sems(1),
            sems(4),
        ],
        (2 * ROUT * 1024 * 2048, 14_000_000),
    )
    h2, z3, s3, sum2 = expand_call(
        "expand_one", 1, 144, st2, norms, z2, near
    )
    st3 = share(jnp.concatenate([s3, ss]))
    mid, h3, z4, s4, sum3, sums = launch(
        "reduce_two",
        middle_kernel,
        [(st3, NEAR), (norms, VM), (z3, ANY), (zs, ANY), (near, ANY)],
        [wide, (shape((ROUT, 2048), BF), ANY), narrow, mid_stats, out_stats, out_stats],
        [
            pltpu.VMEM((ROUT, 2048), F32),
            pltpu.VMEM((ROUT, 2048), F32),
            pltpu.VMEM((ROUT, 2048), BF),
            pltpu.VMEM((ROUT, 512), F32),
            pltpu.VMEM((32, 64, 512), BF),
            sems(2, 4),
            sems(4),
            sems(4),
            sems(4),
            sems(1),
        ],
        (2 * ROUT * 2048 * 512, 20_000_000),
    )
    st4 = tell(s4)
    st4, square = tie(st4, square)
    t4, z5, s5, sum4 = conv_call(
        "spatial_two",
        fifth_kernel,
        [(st4, NEAR), (norms, VM), (z4, ANY), (late, ANY)],
        ROUT,
        (5, 9),
        1,
        2 * 544 * 4608 * 512,
    )
    st5 = tell(s5)
    h5, z6, s6, sum5 = expand_call("expand_two", 3, 144, st5, norms, z5, late)
    st6 = share(s6)
    out, dv6, b6, sum6 = launch(
        "output",
        last_kernel,
        [(where, SM), (st6, NEAR), (norms, VM)] + [(v, ANY) for v in (z6, mid) + cots],
        [narrow, wide, out_stats, out_stats],
        [
            pltpu.VMEM((4, ROUT, 512), F32),
            pltpu.VMEM((4, ROUT, 512), F32),
            pltpu.VMEM((4, ROUT, 512), BF),
            pltpu.VMEM((ROUT, 512), F32),
            sems(4, 4),
            sems(5),
        ],
        (0, 20_000_000),
    )
    output_local, output_global = unpack("unpack_output", out, (3, 7))
    bt6 = share(b6)
    bt6, output_local, output_global = tie(bt6, output_local, output_global)

    wide_in = [pltpu.VMEM((ROUT, 2048), F32), pltpu.VMEM((ROUT, 2048), F32)]
    flat = [pltpu.VMEM((ROUT, 512), F32)]
    mid_grad, out_grad = (shape((2, 512)), VM), (shape((2, 2048)), VM)
    own_mid, own_out = (shape((ROUT, 128), BF), VM), (shape((ROUT, 512), BF), VM)
    o6, dv5, b5, gr6 = launch(
        "back_expand_two",
        back_six_kernel,
        [(where, SM), (bt6, NEAR), (norms, VM), (sum6, VM), (sum5, VM)]
        + [(v, ANY) for v in (z6, dv6, z5, late)],
        [own_out, narrow, mid_stats, out_grad],
        wide_in
        + flat * 2
        + [
            pltpu.VMEM((ROUT, 2048), BF),
            pltpu.VMEM((512, 2048), BF),
            sems(2, 4),
            sems(1),
            sems(16),
            sems(1),
        ],
        (2 * ROUT * 2048 * 512, 14_000_000),
    )
    bt5 = tell(b5)
    gw6 = grad_call("grad_expand_two", where, [(h5, o6)])
    bt5, *gw6 = tie(bt5, *gw6)
    conv_weight = [pltpu.VMEM((32, 144, 512), BF)]
    o5, dv4, b4, gr5 = launch(
        "back_spatial_two",
        back_five_kernel,
        [(where, SM), (bt5, NEAR), (norms, VM), (sum5, VM), (sum4, VM)]
        + [(v, ANY) for v in (z5, dv5, z4, late)],
        [own_mid, narrow, mid_stats, mid_grad],
        flat * 4
        + [
            pltpu.VMEM((ROUT, 512), BF),
            pltpu.VMEM((5, 5, 16, 512), F32),
            pltpu.VMEM((9, 9, 8, 512), F32),
        ]
        + conv_weight
        + [sems(3), sems(4), sems(1)],
        (2 * ROUT * 4608 * 512, 10_000_000),
    )
    bt4 = tell(b4)
    gw5 = grad_call("grad_spatial_two", where, [(t4, o5)])
    bt4, *gw5 = tie(bt4, *gw5)
    o4, dpre, b3, gr4 = launch(
        "back_reduce_two",
        back_four_kernel,
        [(where, SM), (bt4, NEAR), (norms, VM), (sum4, VM), (sum3, VM), (sums, VM)]
        + [(v, ANY) for v in (z4, dv4, dv6, z3, zs, near)],
        [own_mid, wide, (shape((6, 2048)), VM), mid_grad],
        flat * 2
        + wide_in
        + wide_in[:1]
        + [
            pltpu.VMEM((ROUT, 512), BF),
            pltpu.VMEM((32, 64, 512), BF),
            sems(2),
            sems(3, 4),
            sems(4),
            sems(4),
        ],
        (2 * ROUT * 2048 * 512, 22_000_000),
    )
    bt3 = share(b3)
    gw4 = grad_call("grad_reduce_two", where, [(h3, o4)])
    bt3, *gw4 = tie(bt3, *gw4)
    o3, dv2, b2, gr3, gsum = launch(
        "back_expand_one",
        back_three_kernel,
        [(where, SM), (bt3, NEAR), (norms, VM), (sum3, VM), (sum2, VM)]
        + [(v, ANY) for v in (z3, dpre, z2, near)],
        [own_out, narrow, mid_stats, out_grad, out_stats],
        wide_in
        + flat * 2
        + [
            pltpu.VMEM((ROUT, 2048), BF),
            pltpu.VMEM((512, 2048), BF),
            sems(2, 4),
            sems(1),
            sems(16),
            sems(1),
        ],
        (2 * ROUT * 2048 * 512, 16_000_000),
    )
    bt2 = tell(b2)
    o_s, skip, grs = launch(
        "back_shortcut",
        back_skip_kernel,
        [(where, SM), (norms, VM), (gsum, VM), (sums, VM)]
        + [(v, ANY) for v in (zs, dpre) + skips],
        [own_out, (shape((ROUT, 256)), VM), out_grad],
        wide_in
        + [pltpu.VMEM((ROUT, 2048), BF), pltpu.VMEM((256, 2048), BF), sems(2, 4), sems(16)],
        (2 * ROUT * 2048 * 256, 10_000_000),
    )
    pair = grad_call("grad_pair", where, [(h2, o3), (xe, o_s)])
    bt2, skip, *pair = tie(bt2, skip, *pair)
    o2, dv1, b1, gr2 = launch(
        "back_spatial_one",
        back_two_kernel,
        [(where, SM), (bt2, NEAR), (norms, VM), (sum2, VM), (sum1, VM)]
        + [(v, ANY) for v in (z2, dv2, z1, near)],
        [own_mid, (shape((RIN, 512)), ANY), mid_stats, mid_grad],
        flat * 2
        + [
            pltpu.VMEM((ROUT, 512), BF),
            pltpu.VMEM((ROUT, 512), F32),
            pltpu.VMEM((4, 4, 16, 512), F32),
            pltpu.VMEM((8, 8, 8, 512), F32),
        ]
        + conv_weight
        + [pltpu.VMEM((RIN, 512), F32), sems(3), sems(4), sems(20)],
        (2 * ROUT * 4608 * 512, 20_000_000),
    )
    bt1 = tell(b1)
    conv = grad_call("grad_spatial_one", where, [(t1, o2)])
    some = jnp.concatenate([add_halves(*v) for v in (gw6, gw5, gw4, pair)]).reshape(16, 464, 128)
    bt1, some, *conv = tie(bt1, some, *conv)
    some = lax.all_to_all(some, PLANE, 0, 0)
    o1, dz1, gr1 = launch(
        "back_reduce_one",
        back_one_kernel,
        [(where, SM), (bt1, NEAR), (norms, VM), (sum1, VM), (z1, ANY), (dv1, ANY)],
        [(shape((RIN, 128), BF), VM), (shape((RIN, 512), BF), ANY), mid_grad],
        [
            pltpu.VMEM((RIN, 512), F32),
            pltpu.VMEM((RIN, 512), F32),
            pltpu.VMEM((RIN, 512), BF),
            sems(20),
            sems(20),
            sems(1),
        ],
        (0, 12_000_000),
    )
    first = launch(
        "grad_reduce_one",
        first_grad_kernel,
        [(where, SM)] + [(v, VM) for v in xs + (o1,)],
        [(shape((512, 128), BF), VM)] * 2,
        (),
        (2 * RIN * 1024 * 128, 6_000_000),
    )
    rest = jnp.concatenate([add_halves(*conv), add_halves(*first)]).reshape(16, 176, 128)
    some, rest = tie(some, rest)
    rest = lax.all_to_all(rest, PLANE, 0, 0)
    slice_ = launch(
        "slice",
        slice_kernel,
        [(plane_index().reshape(1).astype(jnp.int32), SM), (some, VM), (rest, VM)],
        [(shape((688, 128), BF), VM)],
        (),
        (0, 3_000_000),
    )[0]
    dimage_local, dimage_global = launch(
        "image_grad",
        image_kernel,
        [(where, SM), (dz1, VM)] + [(v, ANY) for v in xs[::2]] + [(skip, VM)],
        [(shape((12, 6, 6, 256)), VM), (shape((6, 14, 14, 256)), VM)],
        [pltpu.VMEM((2, RIN, 128), F32), pltpu.VMEM((1024, 512), BF), sems(8)],
        (2 * RIN * 512 * 256, 8_000_000),
    )
    slice_, dimage_local, dimage_global = tie(slice_, dimage_local, dimage_global)
    held = spread(slice_, PLANE, 16)
    given = swap(held)
    grads = spill("grads_kept", where, held, ())
    given, *grads = tie(given, *grads)
    t6, t5, t4w, t3, ts, t2, t1w = spill("grads_given", where, given, grads)

    def squares(v):
        v = v[:, 640:688].astype(F32).reshape(16, 3, 16, 128)[:, :, :8]
        return jnp.sum(v, axis=(0, 1, 3))

    grad_sq = squares(held) + squares(given)
    weight_sq = jnp.pad(jnp.sum(square, axis=(1, 2)), (0, 1))
    sq = jnp.concatenate([weight_sq[None], grad_sq[None]])
    sq = sq + lax.ppermute(sq, "z", ring(4, 2))
    sq = (sq + lax.ppermute(sq, "z", ring(4, 1)))[:, :7]
    weight_norm = jnp.sqrt(sq[0])
    ratios = weight_norm / (jnp.sqrt(sq[1]) / 12864.0 + DECAY * weight_norm)

    def cut_own(v, n):
        return lax.dynamic_slice_in_dim(v, zi * n, n, 2)

    mids = cut_own(jnp.stack([gr1, gr2, gr4, gr5]), 128)
    wides = cut_own(jnp.stack([gr3, grs, gr6]), 512)
    return (
        output_global,
        output_local,
        dimage_global,
        dimage_local,
        t1w,
        t2.reshape(spatial_one.shape),
        t3,
        ts,
        t4w,
        t5.reshape(spatial_two.shape),
        t6,
        mids[:, 1],
        wides[:, 1],
        mids[:, 0],
        wides[:, 0],
        ratios,
    )


def solution(mesh):
    fine = Mesh(np.asarray(mesh.devices).reshape(4, 4, 2, 4), EVERY)
    crops = P(BATCH, None, None, "z")
    mat = P(None, "z")
    conv = P(None, None, None, "z")
    weights = (mat, conv, mat, mat, mat, conv, mat)
    return jax.shard_map(
        body,
        mesh=fine,
        in_specs=(crops,) * 4 + weights + (mat,) * 4,
        out_specs=(crops,) * 4 + weights + (mat,) * 4 + (P(),),
        check_vma=False,
    )
```

```python
import functools
import math

import jax
import jax.numpy as jnp
import numpy as np
from jax import lax
from jax.experimental import pallas as pl
from jax.experimental.pallas import tpu as pltpu
from jax.sharding import Mesh, PartitionSpec as P

EPS = 1e-05
DECAY = 5e-05
BATCH = ("y", "x", "c")
PLANE = ("y", "x")
EVERY = ("y", "x", "c", "z")
BF = jnp.bfloat16
F32 = jnp.float32
SLOPE = math.sqrt(2.0 / math.pi)
CUBE = 0.044715

LIN, GIN, RIN = 576, 1568, 2144
LOUT, GOUT, ROUT = 144, 392, 544
M_IN = (36 * 12 * 32.0, 196 * 6 * 32.0)
M_OUT = (9 * 12 * 32.0, 49 * 6 * 32.0)
ANY = pl.BlockSpec(memory_space=pltpu.HBM)
VM = pl.BlockSpec(memory_space=pltpu.VMEM)
NEAR = "near"
FAR = "far"
SM = pl.BlockSpec(memory_space=pltpu.SMEM)


def shape(dims, dtype=F32):
    return jax.ShapeDtypeStruct(dims, dtype)


def launch(name, body, ins, outs, scratch=(), cost=(0, 0)):
    def placed(a, s):
        if s is VM or s is SM:
            return a
        return pltpu.with_memory_space_constraint(a, pltpu.VMEM if s is NEAR else pltpu.HBM)

    return pl.pallas_call(
        body,
        name=name,
        out_shape=tuple(pltpu.HBM(o.shape, o.dtype) if s is not VM else o for o, s in outs),
        in_specs=[VM if s is NEAR else s for _, s in ins],
        out_specs=tuple(VM if s is FAR else s for _, s in outs),
        scratch_shapes=list(scratch),
        compiler_params=pltpu.CompilerParams(vmem_limit_bytes=50 * 1024 * 1024),
        cost_estimate=pl.CostEstimate(flops=cost[0], bytes_accessed=cost[1], transcendentals=0),
    )(*[placed(a, s) for a, s in ins])


def sems(*dims):
    return pltpu.SemaphoreType.DMA(dims)


def go(src, dst, sem):
    c = pltpu.make_async_copy(src, dst, sem)
    c.start()
    return c


def wait(copies):
    for c in copies:
        c.wait()


def quarter(n):
    return pl.ds(n * 512, 512)


def act(v):
    t = jnp.tanh(v * (SLOPE + (SLOPE * CUBE) * (v * v)))
    h = 0.5 * v
    return h + h * t


def slope(v):
    s = v * v
    t = jnp.tanh(v * (SLOPE + (SLOPE * CUBE) * s))
    p = 0.5 + 0.5 * t
    return p + p * (1.0 - t) * (v * (SLOPE + (3.0 * SLOPE * CUBE) * s))


def rows8(v):
    return jnp.sum(v.reshape(-1, 8, v.shape[-1]), axis=0)


def row1(v):
    return jnp.sum(v, axis=0, keepdims=True)


def coefs(sums, k, members, gb):
    g, b = gb
    m = sums[2 * k : 2 * k + 1] / members
    inv = lax.rsqrt(sums[2 * k + 1 : 2 * k + 2] / members - m * m + EPS)
    a = inv * g
    return m, inv, a, b - m * a


def back_coefs(sums, grads, k, members, gb):
    m, inv, a, _ = coefs(sums, k, members, gb)
    c1 = a * inv * (grads[2 * k + 1 : 2 * k + 2] / members)
    return a, c1, a * (grads[2 * k : 2 * k + 1] / members) - m * c1


def mid_gb(norms, i):
    return [
        jnp.concatenate([norms[z, r : r + 1, :] for z in range(4)], axis=1) for r in (i, 4 + i)
    ]


def out_gb(norms, i, z):
    return [
        jnp.concatenate([norms[z, r + l : r + l + 1, :] for l in range(4)], axis=1)
        for r in (8 + 4 * i, 20 + 4 * i)
    ]


def keep(rows, width, group, start):
    i = lax.broadcasted_iota(jnp.int32, (rows, width), 0)
    if group == 0:
        return (i & 15) < 12
    return ((i & 7) < 6) & (i + start < LOUT + GOUT)


def sweep(body, init):
    done = []
    for group, (first, steps, rows) in enumerate(((0, 1, 144), (144, 5, 80))):

        def step(s, carry, group=group, first=first, rows=rows):
            return body(group, pl.multiple_of(first + s * rows, 16), rows, carry)

        done.append(lax.fori_loop(0, steps, step, init))
    return done


LINES = ((0, 6, 96), (576, 14, 112))


def wide_sweep(body, init):
    done = []
    for group, (first, steps, rows) in enumerate(LINES):

        def step(s, carry, group=group, first=first, rows=rows):
            return body(group, s, pl.multiple_of(first + s * rows, 16), rows, carry)

        done.append(lax.fori_loop(0, steps, step, init))
    return done


def lines_in(src, dst, sem):
    for group, (first, steps, rows) in enumerate(LINES):
        for s in range(steps):
            here = pl.ds(first + s * rows, rows)
            go(src.at[here, :], dst.at[here, :], sem.at[6 * group + s])


def line_wait(src, dst, sem, group, s, start, rows):
    here = pl.ds(start, rows)
    pltpu.make_async_copy(src.at[here, :], dst.at[here, :], sem.at[6 * group + s]).wait()


def two(width):
    z = jnp.zeros((8, width), F32)
    return (z, z)


def put_stats(out, done, cols=None):
    rows = jnp.concatenate([row1(s) for group in done for s in group], axis=0)
    if cols is None:
        for p in range(out.shape[0]):
            out[p] = rows
    else:
        out[:, cols] = rows


def moments(z_ref, cols=slice(None)):
    def body(group, start, rows, carry):
        v = z_ref[pl.ds(start, rows), cols]
        return carry[0] + rows8(v), carry[1] + rows8(v * v)

    return sweep(body, two(512))


def added(st, cols=None):
    return jnp.sum(st[...] if cols is None else st[:, :, cols], axis=0)


def dot(a, b):
    return jnp.dot(a, b, preferred_element_type=F32)


def dot_t(a, b):
    return lax.dot_general(a, b, (((1,), (1,)), ((), ())), preferred_element_type=F32)


def riding_in(zi, tops, w, sem):
    return [
        go(
            tops[k].at[pl.ds(TOP, 512), pl.ds(128 * i, 128)],
            w.at[pl.ds(512 * i, 512), pl.ds(pl.multiple_of(zi[k] * 128, 128), 128)],
            sem.at[2 * k + i],
        )
        for k in range(4)
        for i in (0, 1)
    ]


def bundle_in(bundle, at, w, sem):
    n = w.shape[1]
    return [
        go(bundle.at[:, z, pl.ds(at, n), :], w.at[:, :, pl.ds(z * 128, 128)], sem.at[z])
        for z in range(4)
    ]


def bundle_out_in(bundle, at, w, sem):
    n = w.shape[1]
    return [
        go(
            bundle.at[:, z, pl.ds(at + n * j, n), :],
            w.at[:, :, pl.ds(z * 512 + j * 128, 128)],
            sem.at[4 * z + j],
        )
        for z in range(4)
        for j in range(4)
    ]


def pack_kernel(side, cuts, local, glob, *refs):
    more, outs, tmp = refs[: -1 - len(cuts)], refs[-1 - len(cuts) : -1], refs[-1]
    tmp[...] = jnp.zeros_like(tmp)
    base = side[0] * side[0] * 16
    if more:
        outs[0][pl.ds(outs[0].shape[0] - 512, 512), 0:128] = more[0][0:512, :]
        outs[0][pl.ds(outs[0].shape[0] - 512, 512), 128:256] = more[0][512:1024, :]
    for lane in range(tmp.shape[0]):
        cols = slice(lane * 128, lane * 128 + 128)
        for n in range(12):
            for h in range(side[0]):
                v = local[n, h, :, cols].astype(F32)
                tmp[lane, pl.ds(h * side[0] * 16 + n, side[0], stride=16), :] = v
        for n in range(6):
            for h in range(side[1]):
                v = glob[n, h, :, cols].astype(F32)
                tmp[lane, pl.ds(base + h * side[1] * 8 + n, side[1], stride=8), :] = v
        at = 0
        for out, n in zip(outs, cuts):
            out[pl.ds(0, n), cols] = tmp[lane, pl.ds(at, n), :].astype(out.dtype)
            at += n


def pack(name, local, glob, side, cuts, more=()):
    c = local.shape[-1]
    rows = sum(cuts)
    extra = (512 * len(more), 0)
    return launch(
        name,
        functools.partial(pack_kernel, side, cuts),
        [(v, VM) for v in (local, glob) + more],
        [(shape((n + e, c), BF), VM) for n, e in zip(cuts, extra)],
        [pltpu.VMEM((c // 128, rows, 128), F32)],
        (0, 4 * rows * c),
    )


def unpack_kernel(side, lanes, local, glob):
    base = side[0] * side[0] * 16
    for lane in range(lanes.shape[0]):
        cols = slice(lane * 128, lane * 128 + 128)
        for n in range(12):
            for h in range(side[0]):
                v = lanes[lane, pl.ds(h * side[0] * 16 + n, side[0], stride=16), :]
                local[n, h, :, cols] = v
        for n in range(6):
            for h in range(side[1]):
                v = lanes[lane, pl.ds(base + h * side[1] * 8 + n, side[1], stride=8), :]
                glob[n, h, :, cols] = v


def unpack_whole(side, rows, local, glob, lanes):
    for lane in range(lanes.shape[0]):
        lanes[lane] = rows[:, lane * 128 : lane * 128 + 128]
    unpack_kernel(side, lanes, local, glob)


def unpack(name, rows, side):
    c = rows.shape[-1]
    return launch(
        name,
        functools.partial(unpack_whole, side),
        [(rows, VM)],
        [
            (shape((12, side[0], side[0], c)), VM),
            (shape((6, side[1], side[1], c)), VM),
        ],
        [pltpu.VMEM((c // 128,) + rows.shape[:1] + (128,), F32)],
        (0, 8 * rows.size),
    )


def pieces_kernel(at, spatial_one, expand_one, shortcut, reduce_two, spatial_two, expand_two, near, late, sem):
    copies = []

    def take(src, dst, first):
        n = src.shape[0] // 32
        rows = pl.ds(pl.multiple_of(at[0] * n, 16), n)
        for j in range(src.shape[1] // 128):
            here = dst.at[pl.ds(first, n), :]
            copies.append(go(src.at[rows, pl.ds(128 * j, 128)], here, sem.at[len(copies)]))
            first += n

    take(spatial_one, near, 0)
    take(expand_one, near, 144)
    take(shortcut, near, 208)
    take(reduce_two, near, 336)
    take(spatial_two, late, 0)
    take(expand_two, late, 144)
    wait(copies)


def square_kernel(*refs):
    out = refs[-1]
    for i, w in enumerate(refs[:-1]):
        n = w.shape[0] // 8
        total = jnp.zeros((8, 128), F32)
        for lane in range(w.shape[1] // 128):
            cols = slice(lane * 128, lane * 128 + 128)

            def step(s, t, w=w, cols=cols, n=n):
                v = w[pl.ds(pl.multiple_of(s * n, 16), n), cols].astype(F32)
                return t + rows8(v * v)

            total = lax.fori_loop(0, 8, step, total)
        out[i] = total


PARTS = ((0, 576), (576, 224), (800, 672), (1472, 672))
TOP = 800


def wide_moments(z_ref, parts):
    z8 = jnp.zeros((8, 512), F32)
    carry = (z8, z8)
    for first, rows in parts:

        def step(s, c, first=first):
            v = z_ref[pl.ds(pl.multiple_of(first + s * 64, 16), 64), :]
            return c[0] + rows8(v), c[1] + rows8(v * v)

        carry = lax.fori_loop(0, rows // 64, step, carry)
        left = rows % 64
        if left:
            v = z_ref[pl.ds(first + rows - left, left), :]
            carry = (carry[0] + rows8(v), carry[1] + rows8(v * v))
    return carry


def first_kernel(zi, *refs):
    xs, rest = refs[:8], refs[8:]
    z1, stats, xv, zv, w, xsem, osem, ws = rest
    weight = riding_in(zi, xs[::2], w, ws)
    cin = []
    for i, (first, rows) in enumerate(PARTS):
        half, base = (0, 0) if first < TOP else (1, TOP)
        one = []
        for k in range(4):
            cols = pl.ds(pl.multiple_of(zi[k] * 256, 256), 256)
            src = xs[2 * k + half].at[pl.ds(first - base, rows), :]
            one.append(go(src, xv.at[pl.ds(first, rows), cols], xsem.at[i, k]))
        cin.append(one)
    wait(weight)
    wf = w
    out, sums = [], []
    for i, (first, rows) in enumerate(PARTS):
        here = pl.ds(first, rows)
        wait(cin[i])
        zv[here, :] = dot(xv[here, :], wf[...])
        out.append(go(zv.at[here, :], z1.at[here, :], osem.at[i]))
    put_stats(stats, [wide_moments(zv, PARTS[:1]), wide_moments(zv, PARTS[1:])])
    wait(out)


def load_taps(local, glob, i, j, stride):
    c = local.shape[-1]
    if stride == 2:
        lv = local.reshape(4, 2, 4, 2, 16, c)
        gv = glob.reshape(8, 2, 8, 2, 8, c)
        a, p, b, q = i // 2, i % 2, j // 2, j % 2
        lt = lv[a : a + 3, p, b : b + 3, q]
        gt = gv[a : a + 7, p, b : b + 7, q]
    else:
        lt = local[i : i + 3, j : j + 3]
        gt = glob[i : i + 7, j : j + 7]
    return jnp.concatenate(
        [lt.reshape(LOUT, c), gt.reshape(GOUT, c), jnp.zeros((8, c), F32)], axis=0
    )


def clear_border(ref):
    side = ref.shape[0]
    zero = jnp.zeros((side,) + ref.shape[2:], F32)
    ref[0] = zero
    ref[side - 1] = zero
    for r in range(1, side - 1):
        ref[r, 0] = zero[0]
        ref[r, side - 1] = zero[0]


def conv_tail(stride, hl, hg, weight, wf, tv, taps, ts, zv, z, zsem, stats):
    out = []
    for k in range(9):
        cols = pl.ds(k * 512, 512)
        tv[:, cols] = load_taps(hl, hg, k // 3, k % 3, stride).astype(BF)
        out.append(go(tv.at[:, cols], taps.at[:, cols], ts.at[k]))
        if k == 0:
            wait(weight)
            zv[...] = dot(tv[:, cols], wf[0:512, :])
        else:
            zv[...] += dot(tv[:, cols], wf[k * 512 : (k + 1) * 512, :])
    out.append(go(zv, z, zsem))
    put_stats(stats, moments(zv))
    wait(out)


def second_kernel(st, norms, z1, near, taps, z2, stats, sums, zin, hl, hg, w, tv, zv, xs, ws, ts, zsem):
    lines_in(z1, zin, xs)
    weight = bundle_in(near, 0, w, ws)
    total = added(st)
    sums[...] = total
    gb = mid_gb(norms, 0)
    cs = [coefs(total, k, M_IN[k], gb) for k in (0, 1)]
    clear_border(hl)
    clear_border(hg)

    def body(group, s, start, rows, carry):
        _, _, a, sh = cs[group]
        line_wait(z1, zin, xs, group, s, start, rows)
        i = lax.broadcasted_iota(jnp.int32, (rows, 512), 0)
        ok = (i & 15) < 12 if group == 0 else (i & 7) < 6
        h = jnp.where(ok, act(zin[pl.ds(start, rows), :] * a + sh), 0.0)
        if group == 0:
            hl[s + 1, 1:7] = h.reshape(6, 16, 512)
        else:
            hg[s + 1, 1:15] = h.reshape(14, 8, 512)
        return carry

    wide_sweep(body, 0)
    conv_tail(2, hl, hg, weight, w.reshape(4608, 512), tv, taps, ts, zv, z2, zsem.at[0], stats)


def fifth_kernel(st, norms, z4, late, taps, z5, stats, sums, zin, hl, hg, w, tv, zv, xs, ws, ts, zsem):
    cin = go(z4, zin, xs.at[0])
    weight = bundle_in(late, 0, w, ws)
    total = added(st)
    sums[...] = total
    gb = mid_gb(norms, 2)
    cs = [coefs(total, k, M_OUT[k], gb) for k in (0, 1)]
    clear_border(hl)
    clear_border(hg)
    cin.wait()
    for group, (first, side, rows) in enumerate(((0, 3, 48), (144, 7, 56))):
        _, _, a, sh = cs[group]
        i = lax.broadcasted_iota(jnp.int32, (rows, 512), 0)
        ok = (i & 15) < 12 if group == 0 else (i & 7) < 6

        def step(s, carry, group=group, first=first, rows=rows, a=a, sh=sh, ok=ok):
            v = zin[pl.ds(pl.multiple_of(first + s * rows, 8), rows), :]
            h = jnp.where(ok, act(v * a + sh), 0.0)
            if group == 0:
                hl[s + 1, 1:4] = h.reshape(3, 16, 512)
            else:
                hg[s + 1, 1:8] = h.reshape(7, 8, 512)
            return carry

        lax.fori_loop(0, side, step, 0)
    conv_tail(1, hl, hg, weight, w.reshape(4608, 512), tv, taps, ts, zv, z5, zsem.at[0], stats)


def conv_call(name, kernel, ins, rows, sides, n, flops):
    sl, sg = sides
    return launch(
        name,
        kernel,
        ins,
        [
            (shape((ROUT, 4608), BF), ANY),
            (shape((ROUT, 512)), ANY),
            (shape((32, 4, 512)), FAR),
            (shape((4, 512)), VM),
        ],
        [
            pltpu.VMEM((rows, 512), F32),
            pltpu.VMEM((sl, sl, 16, 512), F32),
            pltpu.VMEM((sg, sg, 8, 512), F32),
            pltpu.VMEM((32, 144, 512), BF),
            pltpu.VMEM((ROUT, 4608), BF),
            pltpu.VMEM((ROUT, 512), F32),
            sems(n),
            sems(13),
            sems(9),
            sems(1),
        ],
        (flops, 20_000_000),
    )


def expand_kernel(which, at, st, norms, z, bundle, h, zo, stats, sums, zin, hv, zv, w, wsem, hsem, zsem, isem):
    cin = go(z, zin, isem.at[0])
    weight = bundle_out_in(bundle, at, w.reshape(32, 16, 2048), wsem)
    total = added(st)
    sums[...] = total
    gb = mid_gb(norms, which)
    cs = [coefs(total, k, M_OUT[k], gb) for k in (0, 1)]
    cin.wait()

    def body(group, start, rows, carry):
        _, _, a, sh = cs[group]
        v = act(zin[pl.ds(start, rows), :] * a + sh)
        hv[pl.ds(start, rows), :] = jnp.where(keep(rows, 512, group, start), v, 0.0).astype(BF)
        return carry

    sweep(body, 0)
    out = [go(hv, h, hsem.at[0])]
    wait(weight)
    for n in range(4):
        cols = quarter(n)
        zv[:, cols] = dot(hv[...], w[:, cols])
        out.append(go(zv.at[:, cols], zo.at[:, cols], zsem.at[n]))
        put_stats(stats, moments(zv, cols), cols)
    wait(out)


def expand_call(name, which, at, st, norms, z, bundle):
    return launch(
        name,
        functools.partial(expand_kernel, which, at),
        [(st, NEAR), (norms, VM), (z, ANY), (bundle, ANY)],
        [
            (shape((ROUT, 512), BF), ANY),
            (shape((ROUT, 2048)), ANY),
            (shape((4, 2048)), VM),
            (shape((4, 512)), VM),
        ],
        [
            pltpu.VMEM((ROUT, 512), F32),
            pltpu.VMEM((ROUT, 512), BF),
            pltpu.VMEM((ROUT, 2048), F32),
            pltpu.VMEM((512, 2048), BF),
            sems(16),
            sems(1),
            sems(4),
            sems(1),
        ],
        (2 * 544 * 512 * 2048, 9_000_000),
    )


def skip_kernel(zi, *refs):
    x, bundle, rest = refs[:8], refs[8], refs[9:]
    xe, zs, stats, xv, ev, tmp, zv, w, xs, ws, es, os = rest
    xin = [
        [
            go(x[2 * k].at[pl.ds(0, TOP), :], xv.at[k, pl.ds(0, TOP), :], xs.at[k, 0]),
            go(x[2 * k + 1], xv.at[k, pl.ds(TOP, RIN - TOP), :], xs.at[k, 1]),
        ]
        for k in range(4)
    ]
    weight = bundle_out_in(bundle, 208, w.reshape(32, 32, 2048), ws)
    tmp[pl.ds(536, 8), :] = jnp.zeros((8, 256), F32)
    for k in range(4):
        wait(xin[k])
        for r in range(3):
            v = xv[k, pl.ds(r * 192, 96), :].astype(F32).reshape(3, 2, 16, 256)[:, 0]
            tmp[pl.ds(r * 48, 48), :] = v.reshape(48, 256)
        for r in range(7):
            v = xv[k, pl.ds(576 + r * 224, 112), :].astype(F32).reshape(7, 2, 8, 256)[:, 0]
            tmp[pl.ds(144 + r * 56, 56), :] = v.reshape(56, 256)
        at = pl.multiple_of(zi[k] * 256, 256)
        ev[:, pl.ds(at, 256)] = tmp[...].astype(BF)
    out = [go(ev, xe, es.at[0])]
    wait(weight)
    for n in range(4):
        cols = quarter(n)
        zv[:, cols] = dot(ev[...], w[:, cols])
        out.append(go(zv.at[:, cols], zs.at[:, cols], os.at[n]))
        put_stats(stats, moments(zv, cols), cols)
    wait(out)


def middle_kernel(st3, norms, z3, zs, late, mid, h3, z4, stats, sum3, sums, z3v, zsv, hv, zv, w, ins, ws, os, hs, zsem):
    cin = []
    for n in range(4):
        cols = quarter(n)
        cin.append(
            [go(z3.at[:, cols], z3v.at[:, cols], ins.at[0, n]), go(zs.at[:, cols], zsv.at[:, cols], ins.at[1, n])]
        )
    weight = bundle_in(late, 336, w, ws)
    wf = w.reshape(2048, 512)
    out = []
    for n in range(4):
        cols = quarter(n)
        both = added(st3, cols)
        s3, ss = both[0:4], both[4:8]
        sum3[:, cols] = s3
        sums[:, cols] = ss
        cs = []
        for k in (0, 1):
            _, _, a3, b3 = coefs(s3, k, M_OUT[k], out_gb(norms, 0, n))
            _, _, a5, b5 = coefs(ss, k, M_OUT[k], out_gb(norms, 1, n))
            cs.append((a3, a5, b3 + b5))
        wait(cin[n])

        def body(group, start, rows, carry, cols=cols, cs=cs):
            a3, a5, b = cs[group]
            here = (pl.ds(start, rows), cols)
            v = act(z3v[here] * a3 + zsv[here] * a5 + b)
            v = jnp.where(keep(rows, 512, group, start), v, 0.0)
            z3v[here] = v
            hv[here] = v.astype(BF)
            return carry

        sweep(body, 0)
        out.append(go(z3v.at[:, cols], mid.at[:, cols], os.at[n]))
        out.append(go(hv.at[:, cols], h3.at[:, cols], hs.at[n]))
        if n == 0:
            wait(weight)
            zv[...] = dot(hv[:, cols], wf[0:512, :])
        else:
            zv[...] += dot(hv[:, cols], wf[n * 512 : (n + 1) * 512, :])
    out.append(go(zv, z4, zsem.at[0]))
    put_stats(stats, moments(zv))
    wait(out)


def last_kernel(zi, st, norms, z6, mid, *refs):
    cots, rest = refs[:8], refs[8:]
    out, dv6, stats, sums, zv, mv, cv, ov, ins, os = rest
    cin = []
    for k in range(4):
        cols = pl.ds(pl.multiple_of(zi[k] * 512, 512), 512)
        cin.append(
            [
                go(z6.at[:, cols], zv.at[k], ins.at[0, k]),
                go(mid.at[:, cols], mv.at[k], ins.at[1, k]),
                go(cots[2 * k], cv.at[k, pl.ds(0, 272), :], ins.at[2, k]),
                go(cots[2 * k + 1], cv.at[k, pl.ds(272, 272), :], ins.at[3, k]),
            ]
        )
    sums[...] = added(st)
    done_out = []
    for k in range(4):
        cols = pl.ds(pl.multiple_of(zi[k] * 512, 512), 512)
        total = sums[:, cols]
        gb = out_gb(norms, 2, zi[k])
        cs = [coefs(total, j, M_OUT[j], gb) for j in (0, 1)]
        wait(cin[k])

        def body(group, start, rows, carry, cs=cs, k=k):
            m, _, a, sh = cs[group]
            here = pl.ds(start, rows)
            z = zv[k, here, :]
            v = z * a + sh + mv[k, here, :]
            if k == 0:
                ov[here, :] = act(v)
            d = slope(v) * cv[k, here, :].astype(F32)
            mv[k, here, :] = d
            return carry[0] + rows8(d), carry[1] + rows8(d * (z - m))

        done = sweep(body, two(512))
        done_out.append(go(mv.at[k], dv6.at[:, cols], os.at[k]))
        if k == 0:
            done_out.append(go(ov, out, os.at[4]))
        done = [(s, q * cs[j][1]) for j, (s, q) in enumerate(done)]
        put_stats(stats, done, cols)
    wait(done_out)


def grads_out(ref, grads, cols=slice(None)):
    ref[0:1, cols] = grads[0:1] + grads[2:3]
    ref[1:2, cols] = grads[1:2] + grads[3:4]


def slope_rows(dy, z, cs):
    def body(group, start, rows, carry):
        m, _, a, sh = cs[group]
        here = (pl.ds(start, rows), slice(None))
        v = z[here]
        d = jnp.where(keep(rows, 512, group, start), slope(v * a + sh) * dy[here], 0.0)
        dy[here] = d
        return carry[0] + rows8(d), carry[1] + rows8(d * (v - m))

    return [(s, q * cs[j][1]) for j, (s, q) in enumerate(sweep(body, two(512)))]


def norm_rows(dy, z, cs, cols, dz):
    def body(group, start, rows, carry):
        a, c1, c0 = cs[group]
        here = (pl.ds(start, rows), cols)
        d = a * dy[here] - c1 * z[here] - c0
        dz[here] = jnp.where(keep(rows, 512, group, start), d, 0.0).astype(dz.dtype)
        return carry

    sweep(body, 0)


def all_coefs(sums, gb):
    return [coefs(sums, k, M_OUT[k], gb) for k in (0, 1)]


def all_back(sums, grads, gb, members=M_OUT):
    return [back_coefs(sums, grads, k, members[k], gb) for k in (0, 1)]


def own_cols(dst, src, zi, width):
    at = pl.multiple_of(zi[0] * width, width)
    dst[...] = src[:, pl.ds(at, width)].astype(dst.dtype)


def back_six_kernel(zi, stb, norms, sum6, sum5, z6, dv6, z5, late, own, dv5, stats, grad, zv, dv, z5v, acc, dz, w, ins, i5, ws, os):
    cin = []
    for n in range(4):
        cols = quarter(n)
        cin.append(
            [go(z6.at[:, cols], zv.at[:, cols], ins.at[0, n]), go(dv6.at[:, cols], dv.at[:, cols], ins.at[1, n])]
        )
    weight = bundle_out_in(late, 144, w.reshape(32, 16, 2048), ws)
    c5 = go(z5, z5v, i5.at[0])
    for n in range(4):
        cols = quarter(n)
        grads = added(stb, cols)
        grads_out(grad, grads, cols)
        cs = all_back(sum6[:, cols], grads, out_gb(norms, 2, n))
        wait(cin[n])
        norm_rows(dv, zv, cs, cols, dz)
        if n == 0:
            wait(weight)
            acc[...] = dot_t(dz[:, cols], w[:, cols])
        else:
            acc[...] += dot_t(dz[:, cols], w[:, cols])
    own_cols(own, dz, zi, 512)
    c5.wait()
    done = slope_rows(acc, z5v, all_coefs(sum5[...], mid_gb(norms, 3)))
    out = go(acc, dv5, os.at[0])
    put_stats(stats, done)
    out.wait()


def pad_back(dzl, dzg, dz, at):
    dzl[...] = jnp.zeros_like(dzl)
    dzg[...] = jnp.zeros_like(dzg)
    for r in range(3):
        dzl[at + r, at : at + 3] = dz[pl.ds(48 * r, 48), :].reshape(3, 16, 512)
    for r in range(7):
        dzg[at + r, at : at + 7] = dz[pl.ds(144 + 56 * r, 56), :].reshape(7, 8, 512)


def back_five_kernel(zi, stb, norms, sum5, sum4, z5, dv5, z4, late, own, dv4, stats, grad, zv, dv, z4v, acc, dz, dzl, dzg, w, ins, ws, os):
    cin = [go(z5, zv, ins.at[0]), go(dv5, dv, ins.at[1])]
    weight = bundle_in(late, 0, w, ws)
    c4 = go(z4, z4v, ins.at[2])
    grads = added(stb)
    grads_out(grad, grads)
    cs = all_back(sum5[...], grads, mid_gb(norms, 3))
    wait(cin)
    norm_rows(dv, zv, cs, slice(None), dv)
    own_cols(own, dv, zi, 128)
    pad_back(dzl, dzg, dv, 1)
    wait(weight)
    wf = w.reshape(4608, 512)
    for k in range(9):
        dz[...] = load_taps(dzl, dzg, 2 - k // 3, 2 - k % 3, 1).astype(BF)
        part = dot_t(dz[...], wf[k * 512 : (k + 1) * 512, :])
        if k == 0:
            acc[...] = part
        else:
            acc[...] += part
    c4.wait()
    done = slope_rows(acc, z4v, all_coefs(sum4[...], mid_gb(norms, 2)))
    out = go(acc, dv4, os.at[0])
    put_stats(stats, done)
    out.wait()


def back_four_kernel(zi, stb, norms, sum4, sum3, sums, z4, dv4, dv6, z3, zs, late, own, dpre, stats, grad, zv, dv, d6, z3v, zsv, dz, w, in4, ins, ws, os):
    cin = [go(z4, zv, in4.at[0]), go(dv4, dv, in4.at[1])]
    weight = bundle_in(late, 336, w, ws)
    wide = []
    for n in range(4):
        cols = quarter(n)
        wide.append(
            [
                go(src.at[:, cols], dst.at[:, cols], ins.at[i, n])
                for i, (src, dst) in enumerate(((dv6, d6), (z3, z3v), (zs, zsv)))
            ]
        )
    grads = added(stb)
    grads_out(grad, grads)
    cs4 = all_back(sum4[...], grads, mid_gb(norms, 2))
    wait(cin)
    norm_rows(dv, zv, cs4, slice(None), dz)
    own_cols(own, dz, zi, 128)
    wait(weight)
    wf = w.reshape(2048, 512)
    z8 = jnp.zeros((8, 512), F32)
    out = []
    for n in range(4):
        cols = quarter(n)
        s3, ss = sum3[:, cols], sums[:, cols]
        cs = []
        for k in (0, 1):
            m3, i3, a3, b3 = coefs(s3, k, M_OUT[k], out_gb(norms, 0, n))
            ms, is_, a5, b5 = coefs(ss, k, M_OUT[k], out_gb(norms, 1, n))
            cs.append((a3, a5, b3 + b5, m3, ms, i3, is_))
        zv[...] = dot_t(dz[...], wf[n * 512 : (n + 1) * 512, :])
        wait(wide[n])

        def body(group, start, rows, carry, cols=cols, cs=cs):
            a3, a5, b, m3, ms, _, _ = cs[group]
            here = (pl.ds(start, rows), cols)
            u, v = z3v[here], zsv[here]
            d = slope(u * a3 + v * a5 + b) * (zv[pl.ds(start, rows), :] + d6[here])
            d = jnp.where(keep(rows, 512, group, start), d, 0.0)
            d6[here] = d
            return (
                carry[0] + rows8(d),
                carry[1] + rows8(d * (u - m3)),
                carry[2] + rows8(d * (v - ms)),
            )

        done = sweep(body, (z8, z8, z8))
        out.append(go(d6.at[:, cols], dpre.at[:, cols], os.at[n]))
        done = [(s, p * cs[j][5], q * cs[j][6]) for j, (s, p, q) in enumerate(done)]
        put_stats(stats, done, cols)
    wait(out)


def pick(grads, rows):
    return jnp.concatenate([grads[r : r + 1] for r in rows], axis=0)


def back_three_kernel(zi, stb, norms, sum3, sum2, z3, dpre, z2, bundle, own, dv2, stats, grad, gsum, zv, dv, z2v, acc, dz, w, ins, i2, ws, os):
    cin = []
    for n in range(4):
        cols = quarter(n)
        cin.append(
            [go(z3.at[:, cols], zv.at[:, cols], ins.at[0, n]), go(dpre.at[:, cols], dv.at[:, cols], ins.at[1, n])]
        )
    weight = bundle_out_in(bundle, 144, w.reshape(32, 16, 2048), ws)
    c2 = go(z2, z2v, i2.at[0])
    for n in range(4):
        cols = quarter(n)
        grads = added(stb, cols)
        gsum[:, cols] = pick(grads, (0, 2, 3, 5))
        grads = pick(grads, (0, 1, 3, 4))
        grads_out(grad, grads, cols)
        cs = all_back(sum3[:, cols], grads, out_gb(norms, 0, n))
        wait(cin[n])
        norm_rows(dv, zv, cs, cols, dz)
        if n == 0:
            wait(weight)
            acc[...] = dot_t(dz[:, cols], w[:, cols])
        else:
            acc[...] += dot_t(dz[:, cols], w[:, cols])
    own_cols(own, dz, zi, 512)
    c2.wait()
    done = slope_rows(acc, z2v, all_coefs(sum2[...], mid_gb(norms, 1)))
    out = go(acc, dv2, os.at[0])
    put_stats(stats, done)
    out.wait()


def back_skip_kernel(zi, norms, gsum, sums, zs, dpre, bundle, own, skip, grad, zv, dv, dz, w, ins, ws):
    cin = []
    for n in range(4):
        cols = quarter(n)
        cin.append(
            [go(zs.at[:, cols], zv.at[:, cols], ins.at[0, n]), go(dpre.at[:, cols], dv.at[:, cols], ins.at[1, n])]
        )
    wv = w.reshape(8, 32, 2048)
    weight = [
        go(
            bundle.at[pl.ds(zi[0] * 8, 8), z, pl.ds(208 + 32 * j, 32), :],
            wv.at[:, :, pl.ds(z * 512 + j * 128, 128)],
            ws.at[4 * z + j],
        )
        for z in range(4)
        for j in range(4)
    ]
    for n in range(4):
        here = quarter(n)
        grads = gsum[:, here]
        grads_out(grad, grads, here)
        cs = all_back(sums[:, here], grads, out_gb(norms, 1, n))
        wait(cin[n])
        norm_rows(dv, zv, cs, here, dz)
    own_cols(own, dz, zi, 512)
    wait(weight)
    skip[...] = dot_t(dz[...], w[...])


def back_two_kernel(zi, stb, norms, sum2, sum1, z2, dv2, z1, near, *refs):
    (own, dv1, stats, grad, zv, dv, dz, acc, dzl, dzg, w, z1v, ins, ws, os) = refs
    cin = [go(z2, zv, ins.at[0]), go(dv2, dv, ins.at[1])]
    weight = bundle_in(near, 0, w, ws)
    c1 = go(z1, z1v, ins.at[2])
    grads = added(stb)
    grads_out(grad, grads)
    cs = all_back(sum2[...], grads, mid_gb(norms, 1))
    wait(cin)
    norm_rows(dv, zv, cs, slice(None), dv)
    own_cols(own, dv, zi, 128)
    pad_back(dzl, dzg, dv, 0)
    for i in range(4):
        dz[i] = load_taps(dzl, dzg, i // 2, i % 2, 1).astype(BF)
    wait(weight)
    wf = w.reshape(4608, 512)
    gb1 = mid_gb(norms, 0)
    c1s = [coefs(sum1[...], k, M_IN[k], gb1) for k in (0, 1)]
    reach = (((1, 0),), ((2, 0), (0, 1)))
    z8 = jnp.zeros((8, 512), F32)
    totals = [(z8, z8), (z8, z8)]
    out = []
    for p in (0, 1):
        for q in (0, 1):
            first = True
            for i, di in reach[p]:
                for j, dj in reach[q]:
                    k = 3 * i + j
                    part = dot_t(dz[2 * di + dj], wf[k * 512 : (k + 1) * 512, :])
                    if first:
                        acc[...] = part
                    else:
                        acc[...] += part
                    first = False
            if p == 0 and q == 0:
                c1.wait()
            for group, (base, side, n, from_row) in enumerate(((0, 3, 16, 0), (576, 7, 8, 144))):
                m, _, a, sh = c1s[group]
                rows = side * n
                i_ = lax.broadcasted_iota(jnp.int32, (rows, 512), 0)
                okay = (i_ & 15) < 12 if group == 0 else (i_ & 7) < 6
                cells = z1v.at[pl.ds(base, 4 * side * side * n), :]
                cells = cells.reshape(side, 2, side, 2, n, 512)

                def step(r, carry, n=n, side=side, rows=rows, from_row=from_row, m=m, a=a, sh=sh, okay=okay, cells=cells, p=p, q=q):
                    v = cells[r, p, :, q].reshape(rows, 512)
                    g = acc[pl.ds(pl.multiple_of(from_row + r * rows, 8), rows), :]
                    d = jnp.where(okay, slope(v * a + sh) * g, 0.0)
                    cells[r, p, :, q] = d.reshape(side, n, 512)
                    return carry[0] + rows8(d), carry[1] + rows8(d * (v - m))

                totals[group] = lax.fori_loop(0, side, step, totals[group])
        for group, (first_row, steps, rows) in enumerate(LINES):
            for s in range(p, steps, 2):
                here = pl.ds(first_row + s * rows, rows)
                out.append(go(z1v.at[here, :], dv1.at[here, :], os.at[6 * group + s]))
    put_stats(stats, [(s, t * c1s[j][1]) for j, (s, t) in enumerate(totals)])
    wait(out)


def back_one_kernel(zi, stb, norms, sum1, z1, dv1, own, dz1, grad, zv, dv, dzv, is0, is1, os):
    lines_in(z1, zv, is0)
    lines_in(dv1, dv, is1)
    grads = added(stb)
    grads_out(grad, grads)
    cs = all_back(sum1[...], grads, mid_gb(norms, 0), M_IN)

    def body(group, s, start, rows, carry):
        a, c1, c0 = cs[group]
        line_wait(z1, zv, is0, group, s, start, rows)
        line_wait(dv1, dv, is1, group, s, start, rows)
        here = (pl.ds(start, rows), slice(None))
        i = lax.broadcasted_iota(jnp.int32, (rows, 512), 0)
        ok = (i & 15) < 12 if group == 0 else (i & 7) < 6
        d = a * dv[here] - c1 * zv[here] - c0
        dzv[here] = jnp.where(ok, d, 0.0).astype(BF)
        return carry

    wide_sweep(body, 0)
    out = go(dzv, dz1, os.at[0])
    own_cols(own, dzv, zi, 128)
    out.wait()


def image_kernel(zi, dz1, t0, t1, t2, t3, skip, local, glob, img, w, ws):
    wait(riding_in(zi, (t0, t1, t2, t3), w, ws))
    mine = w[pl.ds(pl.multiple_of(zi[0] * 256, 256), 256), :]
    for lane in range(2):
        cols = slice(lane * 128, lane * 128 + 128)
        img[lane] = dot_t(dz1[...], mine[lane * 128 : lane * 128 + 128])
        lv = img.at[lane, pl.ds(0, LIN)].reshape(3, 2, 3, 2, 16, 128)
        gv = img.at[lane, pl.ds(LIN, GIN)].reshape(7, 2, 7, 2, 8, 128)
        lv[:, 0, :, 0] += skip[pl.ds(0, LOUT), cols].reshape(3, 3, 16, 128)
        gv[:, 0, :, 0] += skip[pl.ds(LOUT, GOUT), cols].reshape(7, 7, 8, 128)
    unpack_kernel((6, 14), img, local, glob)


def flipped(a, bt):
    return dot(bt, a).T.astype(BF)


def halves_out(zi, a, bt, width, held, give, at):
    for c, dst in enumerate((held, give)):
        half = zi[4] if c == 0 else 1 - zi[4]
        begin = pl.multiple_of(half * width, width)
        for k in range(0, width, 256):
            n = min(256, width - k)
            v = flipped(a[:, pl.ds(pl.multiple_of(begin + k, 128), n)], bt)
            for j in range(v.shape[1] // 128):
                row = at + j * width + k
                dst[row : row + n, :] = v[:, 128 * j : 128 * (j + 1)]


def grad_kernel(widths, zi, *refs):
    held, give = refs[-2:]
    at = 0
    for i, width in enumerate(widths):
        a, b = refs[2 * i], refs[2 * i + 1]
        bt = b[...].astype(F32).T.astype(BF)
        halves_out(zi, a, bt, width, held, give, at)
        at += width * b.shape[1] // 128


def grad_call(name, zi, pairs):
    widths = [a.shape[1] // 2 for a, _ in pairs]
    rows = sum(a.shape[1] * b.shape[1] // 256 for a, b in pairs)
    return launch(
        name,
        functools.partial(grad_kernel, widths),
        [(zi, SM)] + [(v, VM) for pair in pairs for v in pair],
        [(shape((rows, 128), BF), VM)] * 2,
        (),
        (4 * ROUT * rows * 128, 7_000_000),
    )


def first_grad_kernel(zi, *refs):
    xs, (o1, held, give) = refs[:8], refs[8:]
    bt = o1[...].astype(F32).T.astype(BF)
    for k in range(4):
        v = dot(bt[:, :768], xs[2 * k][0:768, :]) + dot(bt[:, 896:], xs[2 * k + 1][96:, :])
        edge = jnp.concatenate([xs[2 * k][768:800, :], xs[2 * k + 1][0:96, :]], axis=0)
        v = v + dot(bt[:, 768:896], edge)
        v = v.T.astype(BF)
        mine = zi[4] == k // 2
        rows = slice((k % 2) * 256, (k % 2) * 256 + 256)

        @pl.when(mine)
        def _():
            held[rows, :] = v

        @pl.when(jnp.logical_not(mine))
        def _():
            give[rows, :] = v


SPANS = (
    (6, 0, 1024),
    (5, 1024, 3328),
    (4, 3328, 4352),
    (2, 4352, 5376),
    (3, 5376, 7424),
), ((1, 0, 2304), (0, 2304, 2816))


def slice_kernel(spans, at, src, *refs):
    out = refs[0] if spans is SPANS[0] else refs[1]
    squares = [jnp.zeros((1, 128), F32)] * 8
    n = src.shape[1]
    v = src[0].astype(F32)
    for p in range(1, 16):
        v = v + src[p].astype(F32)
    out[0:n, :] = v.astype(BF)
    v = v * v
    row = lax.broadcasted_iota(jnp.int32, (n, 128), 0) + at[0] * n
    for i, lo, hi in spans:
        squares[i] = row1(jnp.where((row >= lo) & (row < hi), v, 0.0))
    left = jnp.concatenate(squares, axis=0)
    if spans is SPANS[0]:
        refs[1][...] = left
        return
    left = left + refs[0][...]
    left = jnp.concatenate([left, left], axis=0)
    for k in range(3):
        part = left.astype(BF)
        out[n + 16 * k : n + 16 * k + 16, :] = part
        left = left - part.astype(F32)


def spill_kernel(other, zi, places, a0, a1, a2, a3, b, *refs):
    refs = refs[7:] if other else refs
    outs, (v6, v5, v4, v3, vs, v2, v1, fa, fb, ins, sem) = refs[:7], refs[7:]
    cin = []
    for j, a in enumerate((a0, a1, a2, a3)):
        for k in range(4):
            dst = fa.at[pl.ds(pl.multiple_of(places[4 * j + k] * 464, 16), 464), :]
            cin.append(go(a.at[pl.ds(464 * k, 464), :], dst, ins.at[4 * j + k]))
    last = go(b.at[:, pl.ds(0, 176), :], fb.reshape(16, 176, 128), ins.at[16])
    c = 1 - zi[4] if other else zi[4]
    copies = []
    plan = (
        (v5, 1, fa, 1024, 2304, 1),
        (vs, 4, fa, 5376, 512, 4),
        (v6, 0, fa, 0, 256, 4),
        (v4, 2, fa, 3328, 1024, 1),
        (v3, 3, fa, 4352, 256, 4),
        (v2, 5, fb, 0, 2304, 1),
    )
    wait(cin)
    for dst, i, flat, at, n, blocks in plan:
        if i == 5:
            last.wait()
        for j in range(blocks):
            dst[:, 128 * j : 128 * (j + 1)] = flat[at + j * n : at + (j + 1) * n, :].astype(F32)
        rows = pl.ds(pl.multiple_of(c * n, n), n)
        copies.append(go(dst, outs[i].at[rows, :], sem.at[i]))
    for k in range(2):
        v1[256 * k : 256 * (k + 1), :] = fb[2304 + 256 * k : 2560 + 256 * k, :].astype(F32)
        rows = pl.ds(pl.multiple_of(zi[2 * c + k] * 256, 256), 256)
        copies.append(go(v1.at[pl.ds(256 * k, 256), :], outs[6].at[rows, :], sem.at[6 + k]))
    wait(copies)


GRADS = ((512, 512), (4608, 128), (2048, 128), (512, 512), (1024, 512), (4608, 128), (1024, 128))


def spill(name, zi, places, srcs, before):
    other = bool(before)
    return pl.pallas_call(
        functools.partial(spill_kernel, other),
        name=name,
        out_shape=tuple(pltpu.HBM(d, F32) for d in GRADS),
        in_specs=[SM, SM] + [ANY] * (5 + len(before)),
        out_specs=tuple(ANY for _ in GRADS),
        scratch_shapes=[pltpu.VMEM((r // 2, c), F32) for r, c in GRADS]
        + [pltpu.VMEM((7424, 128), BF), pltpu.VMEM((2816, 128), BF), sems(17), sems(8)],
        input_output_aliases={7 + i: i for i in range(len(before))},
        compiler_params=pltpu.CompilerParams(vmem_limit_bytes=50 * 1024 * 1024),
        cost_estimate=pl.CostEstimate(flops=0, bytes_accessed=8_000_000, transcendentals=0),
    )(zi, places, *srcs, *before)


def ring(n, k):
    return [(i, (i + k) % n) for i in range(n)]


def spread(v, axes, n):
    return lax.all_to_all(jnp.broadcast_to(v[None], (n,) + v.shape), axes, 0, 0)


def share(v):
    v = v + lax.ppermute(v, "c", ring(2, 1))
    return spread(v, PLANE, 16)


def tell(v):
    return lax.all_to_all(v, BATCH, 0, 0)


def tie(*vs):
    return lax.optimization_barrier(vs)


def plane_index():
    return lax.axis_index("y") * 4 + lax.axis_index("x")


def piece(shard, index):
    n = shard.shape[0] // 32
    return lax.dynamic_slice_in_dim(shard, index * n, n, 0)


def swap(v):
    return lax.ppermute(v, "c", ring(2, 1))


def around(parts):
    left = [lax.ppermute(v, "z", ring(4, 1)) for v in parts]
    right = [lax.ppermute(v, "z", ring(4, 3)) for v in parts]
    left[0], left[1], right[0], right[1] = tie(*left, *right)
    far = [lax.ppermute(left[0], "z", ring(4, 1)), lax.ppermute(right[1], "z", ring(4, 3))]
    return right, far, left


def after(v, *first):
    return tie(v, *first)[0]


def add_halves(held, give):
    return (held.astype(F32) + swap(give).astype(F32)).astype(BF)


def body(
    image_global,
    image_local,
    cotangent_global,
    cotangent_local,
    reduce_one,
    spatial_one,
    expand_one,
    shortcut,
    reduce_two,
    spatial_two,
    expand_two,
    factors_mid,
    factors_out,
    shifts_mid,
    shifts_out,
):
    zi = lax.axis_index("z")
    ci = lax.axis_index("c")
    where = jnp.stack([zi, (zi + 1) % 4, (zi + 2) % 4, (zi + 3) % 4, ci]).astype(jnp.int32)
    flat2, flat5 = spatial_one.reshape(-1, 128), spatial_two.reshape(-1, 128)
    own = [reduce_one, flat2, expand_one, shortcut, reduce_two, flat5, expand_two]

    x = pack(
        "pack_image", image_local, image_global, (6, 14), (TOP, RIN - TOP), (reduce_one,)
    )
    x_right, x_far, x_left = around(x)
    xs = tuple(x) + tuple(x_right) + tuple(x_far) + tuple(x_left)

    norms = jnp.concatenate(
        [factors_mid, shifts_mid, factors_out.reshape(12, 128), shifts_out.reshape(12, 128)]
    )
    norms = after(norms, x[0])
    high = lax.reduce_precision(norms, 8, 7)
    middle = lax.reduce_precision(norms - high, 8, 7)
    low = norms - high - middle
    norms = spread(jnp.concatenate([v.astype(BF) for v in (high, middle, low)]), "z", 4)
    norms = norms[:, 0:32].astype(F32) + norms[:, 32:64].astype(F32) + norms[:, 64:96].astype(F32)

    xs = tuple(after(v, norms) for v in xs)

    near, late = launch(
        "pieces",
        pieces_kernel,
        [((plane_index() * 2 + ci).reshape(1).astype(jnp.int32), SM)]
        + [(after(v, x[0]), ANY) for v in (flat2, expand_one, shortcut, reduce_two, flat5, expand_two)],
        [(shape((400, 128), BF), VM), (shape((208, 128), BF), VM)],
        [sems(15)],
    )
    near = lax.all_gather(near, EVERY, axis=0).reshape(32, 4, 400, 128)
    late = lax.all_gather(late, EVERY, axis=0).reshape(32, 4, 208, 128)

    cot = pack("pack_cotangent", cotangent_local, cotangent_global, (3, 7), (272, 272))
    c_right, c_far, c_left = around(cot)
    cots = tuple(cot) + tuple(c_right) + tuple(c_far) + tuple(c_left)
    square = launch(
        "weight_squares",
        square_kernel,
        [(w, VM) for w in own],
        [(shape((7, 8, 128)), VM)],
        (),
        (0, 6_000_000),
    )[0]

    mid_stats = (shape((32, 4, 512)), FAR)
    out_stats = (shape((4, 2048)), VM)
    narrow, wide = (shape((ROUT, 512)), ANY), (shape((ROUT, 2048)), ANY)
    z1, s1 = launch(
        "reduce_one",
        first_kernel,
        [(where, SM)] + [(v, ANY) for v in xs],
        [(shape((RIN, 512)), ANY), mid_stats],
        [
            pltpu.VMEM((RIN, 1024), BF),
            pltpu.VMEM((RIN, 512), F32),
            pltpu.VMEM((1024, 512), BF),
            sems(4, 4),
            sems(4),
            sems(8),
        ],
        (2 * RIN * 1024 * 512, 10_000_000),
    )
    st1 = tell(s1)
    t1, z2, s2, sum1 = conv_call(
        "spatial_one",
        second_kernel,
        [(st1, NEAR), (norms, VM), (z1, ANY), (near, ANY)],
        RIN,
        (8, 16),
        20,
        40_000_000_000,
    )
    st2 = tell(s2)
    xe, zs, ss = launch(
        "shortcut",
        skip_kernel,
        [(where, SM)] + [(v, ANY) for v in xs + (near,)],
        [(shape((ROUT, 1024), BF), ANY), wide, out_stats],
        [
            pltpu.VMEM((4, RIN, 256), BF),
            pltpu.VMEM((ROUT, 1024), BF),
            pltpu.VMEM((ROUT, 256), F32),
            pltpu.VMEM((ROUT, 2048), F32),
            pltpu.VMEM((1024, 2048), BF),
            sems(4, 2),
            sems(16),
            sems(1),
            sems(4),
        ],
        (2 * ROUT * 1024 * 2048, 14_000_000),
    )
    h2, z3, s3, sum2 = expand_call(
        "expand_one", 1, 144, st2, norms, z2, near
    )
    st3 = share(jnp.concatenate([s3, ss]))
    mid, h3, z4, s4, sum3, sums = launch(
        "reduce_two",
        middle_kernel,
        [(st3, NEAR), (norms, VM), (z3, ANY), (zs, ANY), (near, ANY)],
        [wide, (shape((ROUT, 2048), BF), ANY), narrow, mid_stats, out_stats, out_stats],
        [
            pltpu.VMEM((ROUT, 2048), F32),
            pltpu.VMEM((ROUT, 2048), F32),
            pltpu.VMEM((ROUT, 2048), BF),
            pltpu.VMEM((ROUT, 512), F32),
            pltpu.VMEM((32, 64, 512), BF),
            sems(2, 4),
            sems(4),
            sems(4),
            sems(4),
            sems(1),
        ],
        (2 * ROUT * 2048 * 512, 20_000_000),
    )
    st4 = tell(s4)
    st4, square = tie(st4, square)
    t4, z5, s5, sum4 = conv_call(
        "spatial_two",
        fifth_kernel,
        [(st4, NEAR), (norms, VM), (z4, ANY), (late, ANY)],
        ROUT,
        (5, 9),
        1,
        2 * 544 * 4608 * 512,
    )
    st5 = tell(s5)
    h5, z6, s6, sum5 = expand_call("expand_two", 3, 144, st5, norms, z5, late)
    st6 = share(s6)
    out, dv6, b6, sum6 = launch(
        "output",
        last_kernel,
        [(where, SM), (st6, NEAR), (norms, VM)] + [(v, ANY) for v in (z6, mid) + cots],
        [narrow, wide, out_stats, out_stats],
        [
            pltpu.VMEM((4, ROUT, 512), F32),
            pltpu.VMEM((4, ROUT, 512), F32),
            pltpu.VMEM((4, ROUT, 512), BF),
            pltpu.VMEM((ROUT, 512), F32),
            sems(4, 4),
            sems(5),
        ],
        (0, 20_000_000),
    )
    output_local, output_global = unpack("unpack_output", out, (3, 7))
    bt6 = share(b6)
    bt6, output_local, output_global = tie(bt6, output_local, output_global)

    wide_in = [pltpu.VMEM((ROUT, 2048), F32), pltpu.VMEM((ROUT, 2048), F32)]
    flat = [pltpu.VMEM((ROUT, 512), F32)]
    mid_grad, out_grad = (shape((2, 512)), VM), (shape((2, 2048)), VM)
    own_mid, own_out = (shape((ROUT, 128), BF), VM), (shape((ROUT, 512), BF), VM)
    o6, dv5, b5, gr6 = launch(
        "back_expand_two",
        back_six_kernel,
        [(where, SM), (bt6, NEAR), (norms, VM), (sum6, VM), (sum5, VM)]
        + [(v, ANY) for v in (z6, dv6, z5, late)],
        [own_out, narrow, mid_stats, out_grad],
        wide_in
        + flat * 2
        + [
            pltpu.VMEM((ROUT, 2048), BF),
            pltpu.VMEM((512, 2048), BF),
            sems(2, 4),
            sems(1),
            sems(16),
            sems(1),
        ],
        (2 * ROUT * 2048 * 512, 14_000_000),
    )
    bt5 = tell(b5)
    gw6 = grad_call("grad_expand_two", where, [(h5, o6)])
    bt5, *gw6 = tie(bt5, *gw6)
    conv_weight = [pltpu.VMEM((32, 144, 512), BF)]
    o5, dv4, b4, gr5 = launch(
        "back_spatial_two",
        back_five_kernel,
        [(where, SM), (bt5, NEAR), (norms, VM), (sum5, VM), (sum4, VM)]
        + [(v, ANY) for v in (z5, dv5, z4, late)],
        [own_mid, narrow, mid_stats, mid_grad],
        flat * 4
        + [
            pltpu.VMEM((ROUT, 512), BF),
            pltpu.VMEM((5, 5, 16, 512), F32),
            pltpu.VMEM((9, 9, 8, 512), F32),
        ]
        + conv_weight
        + [sems(3), sems(4), sems(1)],
        (2 * ROUT * 4608 * 512, 10_000_000),
    )
    bt4 = tell(b4)
    gw5 = grad_call("grad_spatial_two", where, [(t4, o5)])
    bt4, *gw5 = tie(bt4, *gw5)
    o4, dpre, b3, gr4 = launch(
        "back_reduce_two",
        back_four_kernel,
        [(where, SM), (bt4, NEAR), (norms, VM), (sum4, VM), (sum3, VM), (sums, VM)]
        + [(v, ANY) for v in (z4, dv4, dv6, z3, zs, near)],
        [own_mid, wide, (shape((6, 2048)), VM), mid_grad],
        flat * 2
        + wide_in
        + wide_in[:1]
        + [
            pltpu.VMEM((ROUT, 512), BF),
            pltpu.VMEM((32, 64, 512), BF),
            sems(2),
            sems(3, 4),
            sems(4),
            sems(4),
        ],
        (2 * ROUT * 2048 * 512, 22_000_000),
    )
    bt3 = share(b3)
    gw4 = grad_call("grad_reduce_two", where, [(h3, o4)])
    bt3, *gw4 = tie(bt3, *gw4)
    o3, dv2, b2, gr3, gsum = launch(
        "back_expand_one",
        back_three_kernel,
        [(where, SM), (bt3, NEAR), (norms, VM), (sum3, VM), (sum2, VM)]
        + [(v, ANY) for v in (z3, dpre, z2, near)],
        [own_out, narrow, mid_stats, out_grad, out_stats],
        wide_in
        + flat * 2
        + [
            pltpu.VMEM((ROUT, 2048), BF),
            pltpu.VMEM((512, 2048), BF),
            sems(2, 4),
            sems(1),
            sems(16),
            sems(1),
        ],
        (2 * ROUT * 2048 * 512, 16_000_000),
    )
    bt2 = tell(b2)
    o_s, skip, grs = launch(
        "back_shortcut",
        back_skip_kernel,
        [(where, SM), (norms, VM), (gsum, VM), (sums, VM)]
        + [(v, ANY) for v in (zs, dpre, near)],
        [own_out, (shape((ROUT, 256)), VM), out_grad],
        wide_in
        + [pltpu.VMEM((ROUT, 2048), BF), pltpu.VMEM((256, 2048), BF), sems(2, 4), sems(16)],
        (2 * ROUT * 2048 * 256, 10_000_000),
    )
    pair = grad_call("grad_pair", where, [(h2, o3), (xe, o_s)])
    bt2, skip, *pair = tie(bt2, skip, *pair)
    o2, dv1, b1, gr2 = launch(
        "back_spatial_one",
        back_two_kernel,
        [(where, SM), (bt2, NEAR), (norms, VM), (sum2, VM), (sum1, VM)]
        + [(v, ANY) for v in (z2, dv2, z1, near)],
        [own_mid, (shape((RIN, 512)), ANY), mid_stats, mid_grad],
        flat * 2
        + [
            pltpu.VMEM((4, ROUT, 512), BF),
            pltpu.VMEM((ROUT, 512), F32),
            pltpu.VMEM((4, 4, 16, 512), F32),
            pltpu.VMEM((8, 8, 8, 512), F32),
        ]
        + conv_weight
        + [pltpu.VMEM((RIN, 512), F32), sems(3), sems(4), sems(20)],
        (2 * ROUT * 4608 * 512, 20_000_000),
    )
    bt1 = tell(b1)
    conv = grad_call("grad_spatial_one", where, [(t1, o2)])
    some = jnp.concatenate([add_halves(*v) for v in (gw6, gw5, gw4, pair)]).reshape(16, 464, 128)
    bt1, some, *conv = tie(bt1, some, *conv)
    some = lax.all_to_all(some, PLANE, 0, 0)
    o1, dz1, gr1 = launch(
        "back_reduce_one",
        back_one_kernel,
        [(where, SM), (bt1, NEAR), (norms, VM), (sum1, VM), (z1, ANY), (dv1, ANY)],
        [(shape((RIN, 128), BF), VM), (shape((RIN, 512), BF), ANY), mid_grad],
        [
            pltpu.VMEM((RIN, 512), F32),
            pltpu.VMEM((RIN, 512), F32),
            pltpu.VMEM((RIN, 512), BF),
            sems(20),
            sems(20),
            sems(1),
        ],
        (0, 12_000_000),
    )
    first = launch(
        "grad_reduce_one",
        first_grad_kernel,
        [(where, SM)] + [(v, VM) for v in xs + (o1,)],
        [(shape((512, 128), BF), VM)] * 2,
        (),
        (2 * RIN * 1024 * 128, 6_000_000),
    )
    rest = jnp.concatenate([add_halves(*conv), add_halves(*first)]).reshape(16, 176, 128)
    some, rest = tie(some, rest)
    rest = lax.all_to_all(rest, PLANE, 0, 0)
    here = plane_index().reshape(1).astype(jnp.int32)
    some, squares_ = launch(
        "slice_some",
        functools.partial(slice_kernel, SPANS[0]),
        [(here, SM), (some, VM)],
        [(shape((464, 128), BF), VM), (shape((8, 128)), VM)],
        (),
        (0, 2_000_000),
    )
    some = [some] + [lax.ppermute(some, "x", ring(4, k)) for k in (1, 2, 3)]
    rest, *some = tie(rest, *some)
    rest = launch(
        "slice_rest",
        functools.partial(slice_kernel, SPANS[1]),
        [(here, SM), (rest, VM), (squares_, VM)],
        [(shape((224, 128), BF), VM)],
        (),
        (0, 1_000_000),
    )[0]
    dimage_local, dimage_global = launch(
        "image_grad",
        image_kernel,
        [(where, SM), (dz1, VM)] + [(v, ANY) for v in xs[::2]] + [(skip, VM)],
        [(shape((12, 6, 6, 256)), VM), (shape((6, 14, 14, 256)), VM)],
        [pltpu.VMEM((2, RIN, 128), F32), pltpu.VMEM((1024, 512), BF), sems(8)],
        (2 * RIN * 512 * 256, 8_000_000),
    )
    rest, dimage_local, dimage_global = tie(rest, dimage_local, dimage_global)
    some = jnp.concatenate(some)
    some = [some] + [lax.ppermute(some, "y", ring(4, k)) for k in (1, 2, 3)]
    yi, xi = lax.axis_index("y"), lax.axis_index("x")
    places = jnp.stack([(yi - j) % 4 * 4 + (xi - k) % 4 for j in range(4) for k in range(4)])
    places = places.astype(jnp.int32)
    rest = spread(rest, PLANE, 16)
    rest, *some = tie(rest, *some)
    grads = spill("grads_kept", where, places, (*some, rest), ())
    given = swap(rest)
    others = [swap(v) for v in some]
    t6, t5, t4w, t3, ts, t2, t1w = spill("grads_given", where, places, (*others, given), grads)

    def squares(v):
        v = v[:, 176:224].astype(F32).reshape(16, 3, 16, 128)[:, :, :8]
        return jnp.sum(v, axis=(0, 1, 3))

    grad_sq = squares(rest) + squares(given)
    weight_sq = jnp.pad(jnp.sum(square, axis=(1, 2)), (0, 1))
    sq = jnp.concatenate([weight_sq[None], grad_sq[None]])
    sq = sq + lax.ppermute(sq, "z", ring(4, 2))
    sq = (sq + lax.ppermute(sq, "z", ring(4, 1)))[:, :7]
    weight_norm = jnp.sqrt(sq[0])
    ratios = weight_norm / (jnp.sqrt(sq[1]) / 12864.0 + DECAY * weight_norm)

    def cut_own(v, n):
        return lax.dynamic_slice_in_dim(v, zi * n, n, 2)

    mids = cut_own(jnp.stack([gr1, gr2, gr4, gr5]), 128)
    wides = cut_own(jnp.stack([gr3, grs, gr6]), 512)
    return (
        output_global,
        output_local,
        dimage_global,
        dimage_local,
        t1w,
        t2.reshape(spatial_one.shape),
        t3,
        ts,
        t4w,
        t5.reshape(spatial_two.shape),
        t6,
        mids[:, 1],
        wides[:, 1],
        mids[:, 0],
        wides[:, 0],
        ratios,
    )


def solution(mesh):
    fine = Mesh(np.asarray(mesh.devices).reshape(4, 4, 2, 4), EVERY)
    crops = P(BATCH, None, None, "z")
    mat = P(None, "z")
    conv = P(None, None, None, "z")
    weights = (mat, conv, mat, mat, mat, conv, mat)
    return jax.shard_map(
        body,
        mesh=fine,
        in_specs=(crops,) * 4 + weights + (mat,) * 4,
        out_specs=(crops,) * 4 + weights + (mat,) * 4 + (P(),),
        check_vma=False,
    )
```

```python
import functools
import math

import jax
import jax.numpy as jnp
import numpy as np
from jax import lax
from jax.experimental import pallas as pl
from jax.experimental.pallas import tpu as pltpu
from jax.sharding import Mesh, PartitionSpec as P

EPS = 1e-05
DECAY = 5e-05
BATCH = ("y", "x", "c")
PLANE = ("y", "x")
EVERY = ("y", "x", "c", "z")
BF = jnp.bfloat16
F32 = jnp.float32
SLOPE = math.sqrt(2.0 / math.pi)
CUBE = 0.044715

LIN, GIN, RIN = 576, 1568, 2144
LOUT, GOUT, ROUT = 144, 392, 544
M_IN = (36 * 12 * 32.0, 196 * 6 * 32.0)
M_OUT = (9 * 12 * 32.0, 49 * 6 * 32.0)
ANY = pl.BlockSpec(memory_space=pltpu.HBM)
VM = pl.BlockSpec(memory_space=pltpu.VMEM)
NEAR = "near"
FAR = "far"
SM = pl.BlockSpec(memory_space=pltpu.SMEM)


def shape(dims, dtype=F32):
    return jax.ShapeDtypeStruct(dims, dtype)


def launch(name, body, ins, outs, scratch=(), cost=(0, 0)):
    def placed(a, s):
        if s is VM or s is SM:
            return a
        return pltpu.with_memory_space_constraint(a, pltpu.VMEM if s is NEAR else pltpu.HBM)

    return pl.pallas_call(
        body,
        name=name,
        out_shape=tuple(pltpu.HBM(o.shape, o.dtype) if s is not VM else o for o, s in outs),
        in_specs=[VM if s is NEAR else s for _, s in ins],
        out_specs=tuple(VM if s is FAR else s for _, s in outs),
        scratch_shapes=list(scratch),
        compiler_params=pltpu.CompilerParams(vmem_limit_bytes=50 * 1024 * 1024),
        cost_estimate=pl.CostEstimate(flops=cost[0], bytes_accessed=cost[1], transcendentals=0),
    )(*[placed(a, s) for a, s in ins])


def sems(*dims):
    return pltpu.SemaphoreType.DMA(dims)


def go(src, dst, sem):
    c = pltpu.make_async_copy(src, dst, sem)
    c.start()
    return c


def wait(copies):
    for c in copies:
        c.wait()


def quarter(n):
    return pl.ds(n * 512, 512)


def act(v):
    t = jnp.tanh(v * (SLOPE + (SLOPE * CUBE) * (v * v)))
    h = 0.5 * v
    return h + h * t


def slope(v):
    s = v * v
    t = jnp.tanh(v * (SLOPE + (SLOPE * CUBE) * s))
    p = 0.5 + 0.5 * t
    return p + p * (1.0 - t) * (v * (SLOPE + (3.0 * SLOPE * CUBE) * s))


def rows8(v):
    return jnp.sum(v.reshape(-1, 8, v.shape[-1]), axis=0)


def row1(v):
    return jnp.sum(v, axis=0, keepdims=True)


def coefs(sums, k, members, gb):
    g, b = gb
    m = sums[2 * k : 2 * k + 1] / members
    inv = lax.rsqrt(sums[2 * k + 1 : 2 * k + 2] / members - m * m + EPS)
    a = inv * g
    return m, inv, a, b - m * a


def back_coefs(sums, grads, k, members, gb):
    m, inv, a, _ = coefs(sums, k, members, gb)
    c1 = a * inv * (grads[2 * k + 1 : 2 * k + 2] / members)
    return a, c1, a * (grads[2 * k : 2 * k + 1] / members) - m * c1


def mid_gb(norms, i):
    return [
        jnp.concatenate([norms[z, r : r + 1, :] for z in range(4)], axis=1) for r in (i, 4 + i)
    ]


def out_gb(norms, i, z):
    return [
        jnp.concatenate([norms[z, r + l : r + l + 1, :] for l in range(4)], axis=1)
        for r in (8 + 4 * i, 20 + 4 * i)
    ]


def keep(rows, width, group, start):
    i = lax.broadcasted_iota(jnp.int32, (rows, width), 0)
    if group == 0:
        return (i & 15) < 12
    return ((i & 7) < 6) & (i + start < LOUT + GOUT)


def sweep(body, init):
    done = []
    for group, (first, steps, rows) in enumerate(((0, 1, 144), (144, 5, 80))):

        def step(s, carry, group=group, first=first, rows=rows):
            return body(group, pl.multiple_of(first + s * rows, 16), rows, carry)

        done.append(lax.fori_loop(0, steps, step, init))
    return done


LINES = ((0, 6, 96), (576, 14, 112))


def wide_sweep(body, init):
    done = []
    for group, (first, steps, rows) in enumerate(LINES):

        def step(s, carry, group=group, first=first, rows=rows):
            return body(group, s, pl.multiple_of(first + s * rows, 16), rows, carry)

        done.append(lax.fori_loop(0, steps, step, init))
    return done


def lines_in(src, dst, sem):
    for group, (first, steps, rows) in enumerate(LINES):
        for s in range(steps):
            here = pl.ds(first + s * rows, rows)
            go(src.at[here, :], dst.at[here, :], sem.at[6 * group + s])


def line_wait(src, dst, sem, group, s, start, rows):
    here = pl.ds(start, rows)
    pltpu.make_async_copy(src.at[here, :], dst.at[here, :], sem.at[6 * group + s]).wait()


def two(width):
    z = jnp.zeros((8, width), F32)
    return (z, z)


def put_stats(out, done, cols=None):
    rows = jnp.concatenate([row1(s) for group in done for s in group], axis=0)
    if cols is None:
        for p in range(out.shape[0]):
            out[p] = rows
    else:
        out[:, cols] = rows


def moments(z_ref, cols=slice(None)):
    def body(group, start, rows, carry):
        v = z_ref[pl.ds(start, rows), cols]
        return carry[0] + rows8(v), carry[1] + rows8(v * v)

    return sweep(body, two(512))


def added(st, cols=None):
    return jnp.sum(st[...] if cols is None else st[:, :, cols], axis=0)


def dot(a, b):
    return jnp.dot(a, b, preferred_element_type=F32)


def dot_t(a, b):
    return lax.dot_general(a, b, (((1,), (1,)), ((), ())), preferred_element_type=F32)


def riding_in(zi, tops, w, sem):
    return [
        go(
            tops[k].at[pl.ds(TOP, 512), pl.ds(128 * i, 128)],
            w.at[pl.ds(512 * i, 512), pl.ds(pl.multiple_of(zi[k] * 128, 128), 128)],
            sem.at[2 * k + i],
        )
        for k in range(4)
        for i in (0, 1)
    ]


def bundle_in(bundle, at, w, sem):
    n = w.shape[1]
    return [
        go(bundle.at[:, z, pl.ds(at, n), :], w.at[:, :, pl.ds(z * 128, 128)], sem.at[z])
        for z in range(4)
    ]


def bundle_out_in(bundle, at, w, sem):
    n = w.shape[1]
    return [
        go(
            bundle.at[:, z, pl.ds(at + n * j, n), :],
            w.at[:, :, pl.ds(z * 512 + j * 128, 128)],
            sem.at[4 * z + j],
        )
        for z in range(4)
        for j in range(4)
    ]


def pack_kernel(side, cuts, local, glob, *refs):
    more, outs, tmp = refs[: -1 - len(cuts)], refs[-1 - len(cuts) : -1], refs[-1]
    tmp[...] = jnp.zeros_like(tmp)
    base = side[0] * side[0] * 16
    if more:
        outs[0][pl.ds(outs[0].shape[0] - 512, 512), 0:128] = more[0][0:512, :]
        outs[0][pl.ds(outs[0].shape[0] - 512, 512), 128:256] = more[0][512:1024, :]
    for lane in range(tmp.shape[0]):
        cols = slice(lane * 128, lane * 128 + 128)
        for n in range(12):
            for h in range(side[0]):
                v = local[n, h, :, cols].astype(F32)
                tmp[lane, pl.ds(h * side[0] * 16 + n, side[0], stride=16), :] = v
        for n in range(6):
            for h in range(side[1]):
                v = glob[n, h, :, cols].astype(F32)
                tmp[lane, pl.ds(base + h * side[1] * 8 + n, side[1], stride=8), :] = v
        at = 0
        for out, n in zip(outs, cuts):
            out[pl.ds(0, n), cols] = tmp[lane, pl.ds(at, n), :].astype(out.dtype)
            at += n


def pack(name, local, glob, side, cuts, more=()):
    c = local.shape[-1]
    rows = sum(cuts)
    extra = (512 * len(more), 0)
    return launch(
        name,
        functools.partial(pack_kernel, side, cuts),
        [(v, VM) for v in (local, glob) + more],
        [(shape((n + e, c), BF), VM) for n, e in zip(cuts, extra)],
        [pltpu.VMEM((c // 128, rows, 128), F32)],
        (0, 4 * rows * c),
    )


def unpack_kernel(side, lanes, local, glob):
    base = side[0] * side[0] * 16
    for lane in range(lanes.shape[0]):
        cols = slice(lane * 128, lane * 128 + 128)
        for n in range(12):
            for h in range(side[0]):
                v = lanes[lane, pl.ds(h * side[0] * 16 + n, side[0], stride=16), :]
                local[n, h, :, cols] = v
        for n in range(6):
            for h in range(side[1]):
                v = lanes[lane, pl.ds(base + h * side[1] * 8 + n, side[1], stride=8), :]
                glob[n, h, :, cols] = v


def unpack_whole(side, rows, local, glob, lanes):
    for lane in range(lanes.shape[0]):
        lanes[lane] = rows[:, lane * 128 : lane * 128 + 128]
    unpack_kernel(side, lanes, local, glob)


def unpack(name, rows, side):
    c = rows.shape[-1]
    return launch(
        name,
        functools.partial(unpack_whole, side),
        [(rows, VM)],
        [
            (shape((12, side[0], side[0], c)), VM),
            (shape((6, side[1], side[1], c)), VM),
        ],
        [pltpu.VMEM((c // 128,) + rows.shape[:1] + (128,), F32)],
        (0, 8 * rows.size),
    )


def pieces_kernel(at, spatial_one, expand_one, shortcut, reduce_two, spatial_two, expand_two, near, late, sem):
    copies = []

    def take(src, dst, first):
        n = src.shape[0] // 32
        rows = pl.ds(pl.multiple_of(at[0] * n, 16), n)
        for j in range(src.shape[1] // 128):
            here = dst.at[pl.ds(first, n), :]
            copies.append(go(src.at[rows, pl.ds(128 * j, 128)], here, sem.at[len(copies)]))
            first += n

    take(spatial_one, near, 0)
    take(expand_one, near, 144)
    take(shortcut, near, 208)
    take(reduce_two, near, 336)
    take(spatial_two, late, 0)
    take(expand_two, late, 144)
    wait(copies)


def square_kernel(*refs):
    out = refs[-1]
    for i, w in enumerate(refs[:-1]):
        n = w.shape[0] // 8
        total = jnp.zeros((8, 128), F32)
        for lane in range(w.shape[1] // 128):
            cols = slice(lane * 128, lane * 128 + 128)

            def step(s, t, w=w, cols=cols, n=n):
                v = w[pl.ds(pl.multiple_of(s * n, 16), n), cols].astype(F32)
                return t + rows8(v * v)

            total = lax.fori_loop(0, 8, step, total)
        out[i] = total


PARTS = ((0, 576), (576, 224), (800, 672), (1472, 672))
TOP = 800


def wide_moments(z_ref, parts):
    z8 = jnp.zeros((8, 512), F32)
    carry = (z8, z8)
    for first, rows in parts:

        def step(s, c, first=first):
            v = z_ref[pl.ds(pl.multiple_of(first + s * 64, 16), 64), :]
            return c[0] + rows8(v), c[1] + rows8(v * v)

        carry = lax.fori_loop(0, rows // 64, step, carry)
        left = rows % 64
        if left:
            v = z_ref[pl.ds(first + rows - left, left), :]
            carry = (carry[0] + rows8(v), carry[1] + rows8(v * v))
    return carry


def first_kernel(zi, *refs):
    xs, rest = refs[:8], refs[8:]
    z1, stats, xv, zv, w, xsem, osem, ws = rest
    weight = riding_in(zi, xs[::2], w, ws)
    cin = []
    for i, (first, rows) in enumerate(PARTS):
        half, base = (0, 0) if first < TOP else (1, TOP)
        one = []
        for k in range(4):
            cols = pl.ds(pl.multiple_of(zi[k] * 256, 256), 256)
            src = xs[2 * k + half].at[pl.ds(first - base, rows), :]
            one.append(go(src, xv.at[pl.ds(first, rows), cols], xsem.at[i, k]))
        cin.append(one)
    wait(weight)
    wf = w
    out, sums = [], []
    for i, (first, rows) in enumerate(PARTS):
        here = pl.ds(first, rows)
        wait(cin[i])
        zv[here, :] = dot(xv[here, :], wf[...])
        out.append(go(zv.at[here, :], z1.at[here, :], osem.at[i]))
    put_stats(stats, [wide_moments(zv, PARTS[:1]), wide_moments(zv, PARTS[1:])])
    wait(out)


def load_taps(local, glob, i, j, stride):
    c = local.shape[-1]
    if stride == 2:
        lv = local.reshape(4, 2, 4, 2, 16, c)
        gv = glob.reshape(8, 2, 8, 2, 8, c)
        a, p, b, q = i // 2, i % 2, j // 2, j % 2
        lt = lv[a : a + 3, p, b : b + 3, q]
        gt = gv[a : a + 7, p, b : b + 7, q]
    else:
        lt = local[i : i + 3, j : j + 3]
        gt = glob[i : i + 7, j : j + 7]
    return jnp.concatenate(
        [lt.reshape(LOUT, c), gt.reshape(GOUT, c), jnp.zeros((8, c), F32)], axis=0
    )


def clear_border(ref):
    side = ref.shape[0]
    zero = jnp.zeros((side,) + ref.shape[2:], F32)
    ref[0] = zero
    ref[side - 1] = zero
    for r in range(1, side - 1):
        ref[r, 0] = zero[0]
        ref[r, side - 1] = zero[0]


def conv_tail(stride, hl, hg, weight, wf, tv, taps, ts, zv, z, zsem, stats):
    out = []
    for k in range(9):
        cols = pl.ds(k * 512, 512)
        tv[:, cols] = load_taps(hl, hg, k // 3, k % 3, stride).astype(BF)
        out.append(go(tv.at[:, cols], taps.at[:, cols], ts.at[k]))
        if k == 0:
            wait(weight)
            zv[...] = dot(tv[:, cols], wf[0:512, :])
        else:
            zv[...] += dot(tv[:, cols], wf[k * 512 : (k + 1) * 512, :])
    out.append(go(zv, z, zsem))
    put_stats(stats, moments(zv))
    wait(out)


def second_kernel(st, norms, z1, near, taps, z2, stats, sums, zin, hl, hg, w, tv, zv, xs, ws, ts, zsem):
    lines_in(z1, zin, xs)
    weight = bundle_in(near, 0, w, ws)
    total = added(st)
    sums[...] = total
    gb = mid_gb(norms, 0)
    cs = [coefs(total, k, M_IN[k], gb) for k in (0, 1)]
    clear_border(hl)
    clear_border(hg)

    def body(group, s, start, rows, carry):
        _, _, a, sh = cs[group]
        line_wait(z1, zin, xs, group, s, start, rows)
        i = lax.broadcasted_iota(jnp.int32, (rows, 512), 0)
        ok = (i & 15) < 12 if group == 0 else (i & 7) < 6
        h = jnp.where(ok, act(zin[pl.ds(start, rows), :] * a + sh), 0.0)
        if group == 0:
            hl[s + 1, 1:7] = h.reshape(6, 16, 512)
        else:
            hg[s + 1, 1:15] = h.reshape(14, 8, 512)
        return carry

    wide_sweep(body, 0)
    conv_tail(2, hl, hg, weight, w.reshape(4608, 512), tv, taps, ts, zv, z2, zsem.at[0], stats)


def fifth_kernel(st, norms, z4, late, taps, z5, stats, sums, zin, hl, hg, w, tv, zv, xs, ws, ts, zsem):
    cin = go(z4, zin, xs.at[0])
    weight = bundle_in(late, 0, w, ws)
    total = added(st)
    sums[...] = total
    gb = mid_gb(norms, 2)
    cs = [coefs(total, k, M_OUT[k], gb) for k in (0, 1)]
    clear_border(hl)
    clear_border(hg)
    cin.wait()
    for group, (first, side, rows) in enumerate(((0, 3, 48), (144, 7, 56))):
        _, _, a, sh = cs[group]
        i = lax.broadcasted_iota(jnp.int32, (rows, 512), 0)
        ok = (i & 15) < 12 if group == 0 else (i & 7) < 6

        def step(s, carry, group=group, first=first, rows=rows, a=a, sh=sh, ok=ok):
            v = zin[pl.ds(pl.multiple_of(first + s * rows, 8), rows), :]
            h = jnp.where(ok, act(v * a + sh), 0.0)
            if group == 0:
                hl[s + 1, 1:4] = h.reshape(3, 16, 512)
            else:
                hg[s + 1, 1:8] = h.reshape(7, 8, 512)
            return carry

        lax.fori_loop(0, side, step, 0)
    conv_tail(1, hl, hg, weight, w.reshape(4608, 512), tv, taps, ts, zv, z5, zsem.at[0], stats)


def conv_call(name, kernel, ins, rows, sides, n, flops):
    sl, sg = sides
    return launch(
        name,
        kernel,
        ins,
        [
            (shape((ROUT, 4608), BF), ANY),
            (shape((ROUT, 512)), ANY),
            (shape((32, 4, 512)), FAR),
            (shape((4, 512)), VM),
        ],
        [
            pltpu.VMEM((rows, 512), F32),
            pltpu.VMEM((sl, sl, 16, 512), F32),
            pltpu.VMEM((sg, sg, 8, 512), F32),
            pltpu.VMEM((32, 144, 512), BF),
            pltpu.VMEM((ROUT, 4608), BF),
            pltpu.VMEM((ROUT, 512), F32),
            sems(n),
            sems(13),
            sems(9),
            sems(1),
        ],
        (flops, 20_000_000),
    )


def expand_kernel(which, at, st, norms, z, bundle, h, zo, stats, sums, zin, hv, zv, w, wsem, hsem, zsem, isem):
    cin = go(z, zin, isem.at[0])
    weight = bundle_out_in(bundle, at, w.reshape(32, 16, 2048), wsem)
    total = added(st)
    sums[...] = total
    gb = mid_gb(norms, which)
    cs = [coefs(total, k, M_OUT[k], gb) for k in (0, 1)]
    cin.wait()

    def body(group, start, rows, carry):
        _, _, a, sh = cs[group]
        v = act(zin[pl.ds(start, rows), :] * a + sh)
        hv[pl.ds(start, rows), :] = jnp.where(keep(rows, 512, group, start), v, 0.0).astype(BF)
        return carry

    sweep(body, 0)
    out = [go(hv, h, hsem.at[0])]
    wait(weight)
    for n in range(4):
        cols = quarter(n)
        zv[:, cols] = dot(hv[...], w[:, cols])
        out.append(go(zv.at[:, cols], zo.at[:, cols], zsem.at[n]))
        put_stats(stats, moments(zv, cols), cols)
    wait(out)


def expand_call(name, which, at, st, norms, z, bundle):
    return launch(
        name,
        functools.partial(expand_kernel, which, at),
        [(st, NEAR), (norms, VM), (z, ANY), (bundle, ANY)],
        [
            (shape((ROUT, 512), BF), ANY),
            (shape((ROUT, 2048)), ANY),
            (shape((4, 2048)), VM),
            (shape((4, 512)), VM),
        ],
        [
            pltpu.VMEM((ROUT, 512), F32),
            pltpu.VMEM((ROUT, 512), BF),
            pltpu.VMEM((ROUT, 2048), F32),
            pltpu.VMEM((512, 2048), BF),
            sems(16),
            sems(1),
            sems(4),
            sems(1),
        ],
        (2 * 544 * 512 * 2048, 9_000_000),
    )


def skip_kernel(zi, *refs):
    x, bundle, rest = refs[:8], refs[8], refs[9:]
    xe, zs, stats, xv, ev, tmp, zv, w, xs, ws, es, os = rest
    xin = [
        [
            go(x[2 * k].at[pl.ds(0, TOP), :], xv.at[k, pl.ds(0, TOP), :], xs.at[k, 0]),
            go(x[2 * k + 1], xv.at[k, pl.ds(TOP, RIN - TOP), :], xs.at[k, 1]),
        ]
        for k in range(4)
    ]
    weight = bundle_out_in(bundle, 208, w.reshape(32, 32, 2048), ws)
    tmp[pl.ds(536, 8), :] = jnp.zeros((8, 256), F32)
    for k in range(4):
        wait(xin[k])
        for r in range(3):
            v = xv[k, pl.ds(r * 192, 96), :].astype(F32).reshape(3, 2, 16, 256)[:, 0]
            tmp[pl.ds(r * 48, 48), :] = v.reshape(48, 256)
        for r in range(7):
            v = xv[k, pl.ds(576 + r * 224, 112), :].astype(F32).reshape(7, 2, 8, 256)[:, 0]
            tmp[pl.ds(144 + r * 56, 56), :] = v.reshape(56, 256)
        at = pl.multiple_of(zi[k] * 256, 256)
        ev[:, pl.ds(at, 256)] = tmp[...].astype(BF)
    out = [go(ev, xe, es.at[0])]
    wait(weight)
    for n in range(4):
        cols = quarter(n)
        zv[:, cols] = dot(ev[...], w[:, cols])
        out.append(go(zv.at[:, cols], zs.at[:, cols], os.at[n]))
        put_stats(stats, moments(zv, cols), cols)
    wait(out)


def middle_kernel(st3, norms, z3, zs, late, mid, h3, z4, stats, sum3, sums, z3v, zsv, hv, zv, w, ins, ws, os, hs, zsem):
    cin = []
    for n in range(4):
        cols = quarter(n)
        cin.append(
            [go(z3.at[:, cols], z3v.at[:, cols], ins.at[0, n]), go(zs.at[:, cols], zsv.at[:, cols], ins.at[1, n])]
        )
    weight = bundle_in(late, 336, w, ws)
    wf = w.reshape(2048, 512)
    out = []
    for n in range(4):
        cols = quarter(n)
        both = added(st3, cols)
        s3, ss = both[0:4], both[4:8]
        sum3[:, cols] = s3
        sums[:, cols] = ss
        cs = []
        for k in (0, 1):
            _, _, a3, b3 = coefs(s3, k, M_OUT[k], out_gb(norms, 0, n))
            _, _, a5, b5 = coefs(ss, k, M_OUT[k], out_gb(norms, 1, n))
            cs.append((a3, a5, b3 + b5))
        wait(cin[n])

        def body(group, start, rows, carry, cols=cols, cs=cs):
            a3, a5, b = cs[group]
            here = (pl.ds(start, rows), cols)
            v = act(z3v[here] * a3 + zsv[here] * a5 + b)
            v = jnp.where(keep(rows, 512, group, start), v, 0.0)
            z3v[here] = v
            hv[here] = v.astype(BF)
            return carry

        sweep(body, 0)
        out.append(go(z3v.at[:, cols], mid.at[:, cols], os.at[n]))
        out.append(go(hv.at[:, cols], h3.at[:, cols], hs.at[n]))
        if n == 0:
            wait(weight)
            zv[...] = dot(hv[:, cols], wf[0:512, :])
        else:
            zv[...] += dot(hv[:, cols], wf[n * 512 : (n + 1) * 512, :])
    out.append(go(zv, z4, zsem.at[0]))
    put_stats(stats, moments(zv))
    wait(out)


def last_kernel(zi, st, norms, z6, mid, *refs):
    cots, rest = refs[:8], refs[8:]
    out, dv6, stats, sums, zv, mv, cv, ov, ins, os = rest
    cin = []
    for k in range(4):
        cols = pl.ds(pl.multiple_of(zi[k] * 512, 512), 512)
        cin.append(
            [
                go(z6.at[:, cols], zv.at[k], ins.at[0, k]),
                go(mid.at[:, cols], mv.at[k], ins.at[1, k]),
                go(cots[2 * k], cv.at[k, pl.ds(0, 272), :], ins.at[2, k]),
                go(cots[2 * k + 1], cv.at[k, pl.ds(272, 272), :], ins.at[3, k]),
            ]
        )
    sums[...] = added(st)
    done_out = []
    for k in range(4):
        cols = pl.ds(pl.multiple_of(zi[k] * 512, 512), 512)
        total = sums[:, cols]
        gb = out_gb(norms, 2, zi[k])
        cs = [coefs(total, j, M_OUT[j], gb) for j in (0, 1)]
        wait(cin[k])

        def body(group, start, rows, carry, cs=cs, k=k):
            m, _, a, sh = cs[group]
            here = pl.ds(start, rows)
            z = zv[k, here, :]
            v = z * a + sh + mv[k, here, :]
            if k == 0:
                ov[here, :] = act(v)
            d = slope(v) * cv[k, here, :].astype(F32)
            mv[k, here, :] = d
            return carry[0] + rows8(d), carry[1] + rows8(d * (z - m))

        done = sweep(body, two(512))
        done_out.append(go(mv.at[k], dv6.at[:, cols], os.at[k]))
        if k == 0:
            done_out.append(go(ov, out, os.at[4]))
        done = [(s, q * cs[j][1]) for j, (s, q) in enumerate(done)]
        put_stats(stats, done, cols)
    wait(done_out)


def grads_out(ref, grads, cols=slice(None)):
    ref[0:1, cols] = grads[0:1] + grads[2:3]
    ref[1:2, cols] = grads[1:2] + grads[3:4]


def slope_rows(dy, z, cs):
    def body(group, start, rows, carry):
        m, _, a, sh = cs[group]
        here = (pl.ds(start, rows), slice(None))
        v = z[here]
        d = jnp.where(keep(rows, 512, group, start), slope(v * a + sh) * dy[here], 0.0)
        dy[here] = d
        return carry[0] + rows8(d), carry[1] + rows8(d * (v - m))

    return [(s, q * cs[j][1]) for j, (s, q) in enumerate(sweep(body, two(512)))]


def norm_rows(dy, z, cs, cols, dz):
    def body(group, start, rows, carry):
        a, c1, c0 = cs[group]
        here = (pl.ds(start, rows), cols)
        d = a * dy[here] - c1 * z[here] - c0
        dz[here] = jnp.where(keep(rows, 512, group, start), d, 0.0).astype(dz.dtype)
        return carry

    sweep(body, 0)


def all_coefs(sums, gb):
    return [coefs(sums, k, M_OUT[k], gb) for k in (0, 1)]


def all_back(sums, grads, gb, members=M_OUT):
    return [back_coefs(sums, grads, k, members[k], gb) for k in (0, 1)]


def own_cols(dst, src, zi, width):
    at = pl.multiple_of(zi[0] * width, width)
    dst[...] = src[:, pl.ds(at, width)].astype(dst.dtype)


def back_six_kernel(zi, stb, norms, sum6, sum5, z6, dv6, z5, late, own, dv5, stats, grad, zv, dv, z5v, acc, dz, w, ins, i5, ws, os):
    cin = []
    for n in range(4):
        cols = quarter(n)
        cin.append(
            [go(z6.at[:, cols], zv.at[:, cols], ins.at[0, n]), go(dv6.at[:, cols], dv.at[:, cols], ins.at[1, n])]
        )
    weight = bundle_out_in(late, 144, w.reshape(32, 16, 2048), ws)
    c5 = go(z5, z5v, i5.at[0])
    for n in range(4):
        cols = quarter(n)
        grads = added(stb, cols)
        grads_out(grad, grads, cols)
        cs = all_back(sum6[:, cols], grads, out_gb(norms, 2, n))
        wait(cin[n])
        norm_rows(dv, zv, cs, cols, dz)
        if n == 0:
            wait(weight)
            acc[...] = dot_t(dz[:, cols], w[:, cols])
        else:
            acc[...] += dot_t(dz[:, cols], w[:, cols])
    own_cols(own, dz, zi, 512)
    c5.wait()
    done = slope_rows(acc, z5v, all_coefs(sum5[...], mid_gb(norms, 3)))
    out = go(acc, dv5, os.at[0])
    put_stats(stats, done)
    out.wait()


def pad_back(dzl, dzg, dz, at):
    dzl[...] = jnp.zeros_like(dzl)
    dzg[...] = jnp.zeros_like(dzg)
    for r in range(3):
        dzl[at + r, at : at + 3] = dz[pl.ds(48 * r, 48), :].reshape(3, 16, 512)
    for r in range(7):
        dzg[at + r, at : at + 7] = dz[pl.ds(144 + 56 * r, 56), :].reshape(7, 8, 512)


def back_five_kernel(zi, stb, norms, sum5, sum4, z5, dv5, z4, late, own, dv4, stats, grad, zv, dv, z4v, acc, dz, dzl, dzg, w, ins, ws, os):
    cin = [go(z5, zv, ins.at[0]), go(dv5, dv, ins.at[1])]
    weight = bundle_in(late, 0, w, ws)
    c4 = go(z4, z4v, ins.at[2])
    grads = added(stb)
    grads_out(grad, grads)
    cs = all_back(sum5[...], grads, mid_gb(norms, 3))
    wait(cin)
    norm_rows(dv, zv, cs, slice(None), dv)
    own_cols(own, dv, zi, 128)
    pad_back(dzl, dzg, dv, 1)
    wait(weight)
    wf = w.reshape(4608, 512)
    for k in range(9):
        dz[...] = load_taps(dzl, dzg, 2 - k // 3, 2 - k % 3, 1).astype(BF)
        part = dot_t(dz[...], wf[k * 512 : (k + 1) * 512, :])
        if k == 0:
            acc[...] = part
        else:
            acc[...] += part
    c4.wait()
    done = slope_rows(acc, z4v, all_coefs(sum4[...], mid_gb(norms, 2)))
    out = go(acc, dv4, os.at[0])
    put_stats(stats, done)
    out.wait()


def back_four_kernel(zi, stb, norms, sum4, sum3, sums, z4, dv4, dv6, z3, zs, late, own, dpre, stats, grad, zv, dv, d6, z3v, zsv, dz, w, in4, ins, ws, os):
    cin = [go(z4, zv, in4.at[0]), go(dv4, dv, in4.at[1])]
    weight = bundle_in(late, 336, w, ws)
    wide = []
    for n in range(4):
        cols = quarter(n)
        wide.append(
            [
                go(src.at[:, cols], dst.at[:, cols], ins.at[i, n])
                for i, (src, dst) in enumerate(((dv6, d6), (z3, z3v), (zs, zsv)))
            ]
        )
    grads = added(stb)
    grads_out(grad, grads)
    cs4 = all_back(sum4[...], grads, mid_gb(norms, 2))
    wait(cin)
    norm_rows(dv, zv, cs4, slice(None), dz)
    own_cols(own, dz, zi, 128)
    wait(weight)
    wf = w.reshape(2048, 512)
    z8 = jnp.zeros((8, 512), F32)
    out = []
    for n in range(4):
        cols = quarter(n)
        s3, ss = sum3[:, cols], sums[:, cols]
        cs = []
        for k in (0, 1):
            m3, i3, a3, b3 = coefs(s3, k, M_OUT[k], out_gb(norms, 0, n))
            ms, is_, a5, b5 = coefs(ss, k, M_OUT[k], out_gb(norms, 1, n))
            cs.append((a3, a5, b3 + b5, m3, ms, i3, is_))
        zv[...] = dot_t(dz[...], wf[n * 512 : (n + 1) * 512, :])
        wait(wide[n])

        def body(group, start, rows, carry, cols=cols, cs=cs):
            a3, a5, b, m3, ms, _, _ = cs[group]
            here = (pl.ds(start, rows), cols)
            u, v = z3v[here], zsv[here]
            d = slope(u * a3 + v * a5 + b) * (zv[pl.ds(start, rows), :] + d6[here])
            d = jnp.where(keep(rows, 512, group, start), d, 0.0)
            d6[here] = d
            return (
                carry[0] + rows8(d),
                carry[1] + rows8(d * (u - m3)),
                carry[2] + rows8(d * (v - ms)),
            )

        done = sweep(body, (z8, z8, z8))
        out.append(go(d6.at[:, cols], dpre.at[:, cols], os.at[n]))
        done = [(s, p * cs[j][5], q * cs[j][6]) for j, (s, p, q) in enumerate(done)]
        put_stats(stats, done, cols)
    wait(out)


def pick(grads, rows):
    return jnp.concatenate([grads[r : r + 1] for r in rows], axis=0)


def back_three_kernel(zi, stb, norms, sum3, sum2, z3, dpre, z2, bundle, own, dv2, stats, grad, gsum, zv, dv, z2v, acc, dz, w, ins, i2, ws, os):
    cin = []
    for n in range(4):
        cols = quarter(n)
        cin.append(
            [go(z3.at[:, cols], zv.at[:, cols], ins.at[0, n]), go(dpre.at[:, cols], dv.at[:, cols], ins.at[1, n])]
        )
    weight = bundle_out_in(bundle, 144, w.reshape(32, 16, 2048), ws)
    c2 = go(z2, z2v, i2.at[0])
    for n in range(4):
        cols = quarter(n)
        grads = added(stb, cols)
        gsum[:, cols] = pick(grads, (0, 2, 3, 5))
        grads = pick(grads, (0, 1, 3, 4))
        grads_out(grad, grads, cols)
        cs = all_back(sum3[:, cols], grads, out_gb(norms, 0, n))
        wait(cin[n])
        norm_rows(dv, zv, cs, cols, dz)
        if n == 0:
            wait(weight)
            acc[...] = dot_t(dz[:, cols], w[:, cols])
        else:
            acc[...] += dot_t(dz[:, cols], w[:, cols])
    own_cols(own, dz, zi, 512)
    c2.wait()
    done = slope_rows(acc, z2v, all_coefs(sum2[...], mid_gb(norms, 1)))
    out = go(acc, dv2, os.at[0])
    put_stats(stats, done)
    out.wait()


def back_skip_kernel(zi, norms, gsum, sums, zs, dpre, bundle, own, skip, grad, zv, dv, dz, w, ins, ws):
    cin = []
    for n in range(4):
        cols = quarter(n)
        cin.append(
            [go(zs.at[:, cols], zv.at[:, cols], ins.at[0, n]), go(dpre.at[:, cols], dv.at[:, cols], ins.at[1, n])]
        )
    wv = w.reshape(8, 32, 2048)
    weight = [
        go(
            bundle.at[pl.ds(zi[0] * 8, 8), z, pl.ds(208 + 32 * j, 32), :],
            wv.at[:, :, pl.ds(z * 512 + j * 128, 128)],
            ws.at[4 * z + j],
        )
        for z in range(4)
        for j in range(4)
    ]
    for n in range(4):
        here = quarter(n)
        grads = gsum[:, here]
        grads_out(grad, grads, here)
        cs = all_back(sums[:, here], grads, out_gb(norms, 1, n))
        wait(cin[n])
        norm_rows(dv, zv, cs, here, dz)
    own_cols(own, dz, zi, 512)
    wait(weight)
    skip[...] = dot_t(dz[...], w[...])


def back_two_kernel(zi, stb, norms, sum2, sum1, z2, dv2, z1, near, *refs):
    (own, dv1, stats, grad, zv, dv, dz, acc, dzl, dzg, w, z1v, ins, ws, os) = refs
    cin = [go(z2, zv, ins.at[0]), go(dv2, dv, ins.at[1])]
    weight = bundle_in(near, 0, w, ws)
    c1 = go(z1, z1v, ins.at[2])
    grads = added(stb)
    grads_out(grad, grads)
    cs = all_back(sum2[...], grads, mid_gb(norms, 1))
    wait(cin)
    norm_rows(dv, zv, cs, slice(None), dv)
    own_cols(own, dv, zi, 128)
    pad_back(dzl, dzg, dv, 0)
    for i in range(4):
        dz[i] = load_taps(dzl, dzg, i // 2, i % 2, 1).astype(BF)
    wait(weight)
    wf = w.reshape(4608, 512)
    gb1 = mid_gb(norms, 0)
    c1s = [coefs(sum1[...], k, M_IN[k], gb1) for k in (0, 1)]
    reach = (((1, 0),), ((2, 0), (0, 1)))
    z8 = jnp.zeros((8, 512), F32)
    totals = [(z8, z8), (z8, z8)]
    out = []
    for p in (0, 1):
        for q in (0, 1):
            first = True
            for i, di in reach[p]:
                for j, dj in reach[q]:
                    k = 3 * i + j
                    part = dot_t(dz[2 * di + dj], wf[k * 512 : (k + 1) * 512, :])
                    if first:
                        acc[...] = part
                    else:
                        acc[...] += part
                    first = False
            if p == 0 and q == 0:
                c1.wait()
            for group, (base, side, n, from_row) in enumerate(((0, 3, 16, 0), (576, 7, 8, 144))):
                m, _, a, sh = c1s[group]
                rows = side * n
                i_ = lax.broadcasted_iota(jnp.int32, (rows, 512), 0)
                okay = (i_ & 15) < 12 if group == 0 else (i_ & 7) < 6
                cells = z1v.at[pl.ds(base, 4 * side * side * n), :]
                cells = cells.reshape(side, 2, side, 2, n, 512)

                def step(r, carry, n=n, side=side, rows=rows, from_row=from_row, m=m, a=a, sh=sh, okay=okay, cells=cells, p=p, q=q):
                    v = cells[r, p, :, q].reshape(rows, 512)
                    g = acc[pl.ds(pl.multiple_of(from_row + r * rows, 8), rows), :]
                    d = jnp.where(okay, slope(v * a + sh) * g, 0.0)
                    cells[r, p, :, q] = d.reshape(side, n, 512)
                    return carry[0] + rows8(d), carry[1] + rows8(d * (v - m))

                totals[group] = lax.fori_loop(0, side, step, totals[group])
        for group, (first_row, steps, rows) in enumerate(LINES):
            for s in range(p, steps, 2):
                here = pl.ds(first_row + s * rows, rows)
                out.append(go(z1v.at[here, :], dv1.at[here, :], os.at[6 * group + s]))
    put_stats(stats, [(s, t * c1s[j][1]) for j, (s, t) in enumerate(totals)])
    wait(out)


def back_one_kernel(zi, stb, norms, sum1, z1, dv1, own, dz1, grad, zv, dv, dzv, is0, is1, os):
    lines_in(z1, zv, is0)
    lines_in(dv1, dv, is1)
    grads = added(stb)
    grads_out(grad, grads)
    cs = all_back(sum1[...], grads, mid_gb(norms, 0), M_IN)

    def body(group, s, start, rows, carry):
        a, c1, c0 = cs[group]
        line_wait(z1, zv, is0, group, s, start, rows)
        line_wait(dv1, dv, is1, group, s, start, rows)
        here = (pl.ds(start, rows), slice(None))
        i = lax.broadcasted_iota(jnp.int32, (rows, 512), 0)
        ok = (i & 15) < 12 if group == 0 else (i & 7) < 6
        d = a * dv[here] - c1 * zv[here] - c0
        dzv[here] = jnp.where(ok, d, 0.0).astype(BF)
        return carry

    wide_sweep(body, 0)
    out = go(dzv, dz1, os.at[0])
    own_cols(own, dzv, zi, 128)
    out.wait()


def image_kernel(zi, dz1, t0, t1, t2, t3, skip, local, glob, img, w, ws):
    wait(riding_in(zi, (t0, t1, t2, t3), w, ws))
    mine = w[pl.ds(pl.multiple_of(zi[0] * 256, 256), 256), :]
    for lane in range(2):
        cols = slice(lane * 128, lane * 128 + 128)
        img[lane] = dot_t(dz1[...], mine[lane * 128 : lane * 128 + 128])
        lv = img.at[lane, pl.ds(0, LIN)].reshape(3, 2, 3, 2, 16, 128)
        gv = img.at[lane, pl.ds(LIN, GIN)].reshape(7, 2, 7, 2, 8, 128)
        lv[:, 0, :, 0] += skip[pl.ds(0, LOUT), cols].reshape(3, 3, 16, 128)
        gv[:, 0, :, 0] += skip[pl.ds(LOUT, GOUT), cols].reshape(7, 7, 8, 128)
    unpack_kernel((6, 14), img, local, glob)


def flipped(a, bt):
    return dot(bt, a).T.astype(BF)


def halves_out(zi, a, bt, width, held, give, at):
    for c, dst in enumerate((held, give)):
        half = zi[4] if c == 0 else 1 - zi[4]
        begin = pl.multiple_of(half * width, width)
        for k in range(0, width, 256):
            n = min(256, width - k)
            v = flipped(a[:, pl.ds(pl.multiple_of(begin + k, 128), n)], bt)
            for j in range(v.shape[1] // 128):
                row = at + j * width + k
                dst[row : row + n, :] = v[:, 128 * j : 128 * (j + 1)]


def grad_kernel(widths, zi, *refs):
    held, give = refs[-2:]
    at = 0
    for i, width in enumerate(widths):
        a, b = refs[2 * i], refs[2 * i + 1]
        bt = b[...].astype(F32).T.astype(BF)
        halves_out(zi, a, bt, width, held, give, at)
        at += width * b.shape[1] // 128


def grad_call(name, zi, pairs):
    widths = [a.shape[1] // 2 for a, _ in pairs]
    rows = sum(a.shape[1] * b.shape[1] // 256 for a, b in pairs)
    return launch(
        name,
        functools.partial(grad_kernel, widths),
        [(zi, SM)] + [(v, VM) for pair in pairs for v in pair],
        [(shape((rows, 128), BF), VM)] * 2,
        (),
        (4 * ROUT * rows * 128, 7_000_000),
    )


def first_grad_kernel(zi, *refs):
    xs, (o1, held, give) = refs[:8], refs[8:]
    bt = o1[...].astype(F32).T.astype(BF)
    for k in range(4):
        v = dot(bt[:, :768], xs[2 * k][0:768, :]) + dot(bt[:, 896:], xs[2 * k + 1][96:, :])
        edge = jnp.concatenate([xs[2 * k][768:800, :], xs[2 * k + 1][0:96, :]], axis=0)
        v = v + dot(bt[:, 768:896], edge)
        v = v.T.astype(BF)
        mine = zi[4] == k // 2
        rows = slice((k % 2) * 256, (k % 2) * 256 + 256)

        @pl.when(mine)
        def _():
            held[rows, :] = v

        @pl.when(jnp.logical_not(mine))
        def _():
            give[rows, :] = v


SPANS = (
    (6, 0, 1024),
    (5, 1024, 3328),
    (4, 3328, 4352),
    (2, 4352, 5376),
    (3, 5376, 7424),
), ((1, 0, 2304), (0, 2304, 2816))


def slice_kernel(spans, at, src, *refs):
    out = refs[0] if spans is SPANS[0] else refs[1]
    squares = [jnp.zeros((1, 128), F32)] * 8
    n = src.shape[1]
    v = src[0].astype(F32)
    for p in range(1, 16):
        v = v + src[p].astype(F32)
    out[0:n, :] = v.astype(BF)
    v = v * v
    row = lax.broadcasted_iota(jnp.int32, (n, 128), 0) + at[0] * n
    for i, lo, hi in spans:
        squares[i] = row1(jnp.where((row >= lo) & (row < hi), v, 0.0))
    left = jnp.concatenate(squares, axis=0)
    if spans is SPANS[0]:
        refs[1][...] = left
        return
    left = left + refs[0][...]
    left = jnp.concatenate([left, left], axis=0)
    for k in range(3):
        part = left.astype(BF)
        out[n + 16 * k : n + 16 * k + 16, :] = part
        left = left - part.astype(F32)


def spill_kernel(other, zi, places, *refs):
    parts, b, refs = refs[:8], refs[8], refs[9:]
    refs = refs[7:] if other else refs
    outs, (v6, v5, v4, v3, vs, v2, v1, fa, fb, ins, sem) = refs[:7], refs[7:]
    cin = []
    for j, part in enumerate(parts):
        first, n = (0, 224) if j < 4 else (224, 240)
        for k in range(4):
            row = pl.multiple_of(places[4 * j + k] * 464 + first, 16)
            cin.append(go(part.at[pl.ds(n * k, n), :], fa.at[pl.ds(row, n), :], ins.at[4 * j + k]))
    last = go(b.at[:, pl.ds(0, 176), :], fb.reshape(16, 176, 128), ins.at[32])
    c = 1 - zi[4] if other else zi[4]
    copies = []
    plan = (
        (v5, 1, fa, 1024, 2304, 1),
        (vs, 4, fa, 5376, 512, 4),
        (v6, 0, fa, 0, 256, 4),
        (v4, 2, fa, 3328, 1024, 1),
        (v3, 3, fa, 4352, 256, 4),
        (v2, 5, fb, 0, 2304, 1),
    )
    wait(cin)
    for dst, i, flat, at, n, blocks in plan:
        if i == 5:
            last.wait()
        for j in range(blocks):
            dst[:, 128 * j : 128 * (j + 1)] = flat[at + j * n : at + (j + 1) * n, :].astype(F32)
        rows = pl.ds(pl.multiple_of(c * n, n), n)
        copies.append(go(dst, outs[i].at[rows, :], sem.at[i]))
    for k in range(2):
        v1[256 * k : 256 * (k + 1), :] = fb[2304 + 256 * k : 2560 + 256 * k, :].astype(F32)
        rows = pl.ds(pl.multiple_of(zi[2 * c + k] * 256, 256), 256)
        copies.append(go(v1.at[pl.ds(256 * k, 256), :], outs[6].at[rows, :], sem.at[6 + k]))
    wait(copies)


GRADS = ((512, 512), (4608, 128), (2048, 128), (512, 512), (1024, 512), (4608, 128), (1024, 128))


def spill(name, zi, places, srcs, before):
    other = bool(before)
    return pl.pallas_call(
        functools.partial(spill_kernel, other),
        name=name,
        out_shape=tuple(pltpu.HBM(d, F32) for d in GRADS),
        in_specs=[SM, SM] + [ANY] * (9 + len(before)),
        out_specs=tuple(ANY for _ in GRADS),
        scratch_shapes=[pltpu.VMEM((r // 2, c), F32) for r, c in GRADS]
        + [pltpu.VMEM((7424, 128), BF), pltpu.VMEM((2816, 128), BF), sems(33), sems(8)],
        input_output_aliases={11 + i: i for i in range(len(before))},
        compiler_params=pltpu.CompilerParams(vmem_limit_bytes=50 * 1024 * 1024),
        cost_estimate=pl.CostEstimate(flops=0, bytes_accessed=8_000_000, transcendentals=0),
    )(zi, places, *srcs, *before)


def ring(n, k):
    return [(i, (i + k) % n) for i in range(n)]


def spread(v, axes, n):
    return lax.all_to_all(jnp.broadcast_to(v[None], (n,) + v.shape), axes, 0, 0)


def share(v):
    v = v + lax.ppermute(v, "c", ring(2, 1))
    return spread(v, PLANE, 16)


def tell(v):
    return lax.all_to_all(v, BATCH, 0, 0)


def tie(*vs):
    return lax.optimization_barrier(vs)


def plane_index():
    return lax.axis_index("y") * 4 + lax.axis_index("x")


def piece(shard, index):
    n = shard.shape[0] // 32
    return lax.dynamic_slice_in_dim(shard, index * n, n, 0)


def swap(v):
    return lax.ppermute(v, "c", ring(2, 1))


def around(parts):
    left = [lax.ppermute(v, "z", ring(4, 1)) for v in parts]
    right = [lax.ppermute(v, "z", ring(4, 3)) for v in parts]
    left[0], left[1], right[0], right[1] = tie(*left, *right)
    far = [lax.ppermute(left[0], "z", ring(4, 1)), lax.ppermute(right[1], "z", ring(4, 3))]
    return right, far, left


def after(v, *first):
    return tie(v, *first)[0]


def add_halves(held, give):
    return (held.astype(F32) + swap(give).astype(F32)).astype(BF)


def body(
    image_global,
    image_local,
    cotangent_global,
    cotangent_local,
    reduce_one,
    spatial_one,
    expand_one,
    shortcut,
    reduce_two,
    spatial_two,
    expand_two,
    factors_mid,
    factors_out,
    shifts_mid,
    shifts_out,
):
    zi = lax.axis_index("z")
    ci = lax.axis_index("c")
    where = jnp.stack([zi, (zi + 1) % 4, (zi + 2) % 4, (zi + 3) % 4, ci]).astype(jnp.int32)
    flat2, flat5 = spatial_one.reshape(-1, 128), spatial_two.reshape(-1, 128)
    own = [reduce_one, flat2, expand_one, shortcut, reduce_two, flat5, expand_two]

    x = pack(
        "pack_image", image_local, image_global, (6, 14), (TOP, RIN - TOP), (reduce_one,)
    )
    x_right, x_far, x_left = around(x)
    xs = tuple(x) + tuple(x_right) + tuple(x_far) + tuple(x_left)

    norms = jnp.concatenate(
        [factors_mid, shifts_mid, factors_out.reshape(12, 128), shifts_out.reshape(12, 128)]
    )
    norms = after(norms, x[0])
    high = lax.reduce_precision(norms, 8, 7)
    middle = lax.reduce_precision(norms - high, 8, 7)
    low = norms - high - middle
    norms = spread(jnp.concatenate([v.astype(BF) for v in (high, middle, low)]), "z", 4)
    norms = norms[:, 0:32].astype(F32) + norms[:, 32:64].astype(F32) + norms[:, 64:96].astype(F32)

    xs = tuple(after(v, norms) for v in xs)

    near, late = launch(
        "pieces",
        pieces_kernel,
        [((plane_index() * 2 + ci).reshape(1).astype(jnp.int32), SM)]
        + [(after(v, x[0]), ANY) for v in (flat2, expand_one, shortcut, reduce_two, flat5, expand_two)],
        [(shape((400, 128), BF), VM), (shape((208, 128), BF), VM)],
        [sems(15)],
    )
    near = lax.all_gather(near, EVERY, axis=0).reshape(32, 4, 400, 128)
    late = lax.all_gather(late, EVERY, axis=0).reshape(32, 4, 208, 128)

    cot = pack("pack_cotangent", cotangent_local, cotangent_global, (3, 7), (272, 272))
    c_right, c_far, c_left = around(cot)
    cots = tuple(cot) + tuple(c_right) + tuple(c_far) + tuple(c_left)
    square = launch(
        "weight_squares",
        square_kernel,
        [(w, VM) for w in own],
        [(shape((7, 8, 128)), VM)],
        (),
        (0, 6_000_000),
    )[0]

    mid_stats = (shape((32, 4, 512)), FAR)
    out_stats = (shape((4, 2048)), VM)
    narrow, wide = (shape((ROUT, 512)), ANY), (shape((ROUT, 2048)), ANY)
    z1, s1 = launch(
        "reduce_one",
        first_kernel,
        [(where, SM)] + [(v, ANY) for v in xs],
        [(shape((RIN, 512)), ANY), mid_stats],
        [
            pltpu.VMEM((RIN, 1024), BF),
            pltpu.VMEM((RIN, 512), F32),
            pltpu.VMEM((1024, 512), BF),
            sems(4, 4),
            sems(4),
            sems(8),
        ],
        (2 * RIN * 1024 * 512, 10_000_000),
    )
    st1 = tell(s1)
    t1, z2, s2, sum1 = conv_call(
        "spatial_one",
        second_kernel,
        [(st1, NEAR), (norms, VM), (z1, ANY), (near, ANY)],
        RIN,
        (8, 16),
        20,
        40_000_000_000,
    )
    st2 = tell(s2)
    xe, zs, ss = launch(
        "shortcut",
        skip_kernel,
        [(where, SM)] + [(v, ANY) for v in xs + (near,)],
        [(shape((ROUT, 1024), BF), ANY), wide, out_stats],
        [
            pltpu.VMEM((4, RIN, 256), BF),
            pltpu.VMEM((ROUT, 1024), BF),
            pltpu.VMEM((ROUT, 256), F32),
            pltpu.VMEM((ROUT, 2048), F32),
            pltpu.VMEM((1024, 2048), BF),
            sems(4, 2),
            sems(16),
            sems(1),
            sems(4),
        ],
        (2 * ROUT * 1024 * 2048, 14_000_000),
    )
    h2, z3, s3, sum2 = expand_call(
        "expand_one", 1, 144, st2, norms, z2, near
    )
    st3 = share(jnp.concatenate([s3, ss]))
    mid, h3, z4, s4, sum3, sums = launch(
        "reduce_two",
        middle_kernel,
        [(st3, NEAR), (norms, VM), (z3, ANY), (zs, ANY), (near, ANY)],
        [wide, (shape((ROUT, 2048), BF), ANY), narrow, mid_stats, out_stats, out_stats],
        [
            pltpu.VMEM((ROUT, 2048), F32),
            pltpu.VMEM((ROUT, 2048), F32),
            pltpu.VMEM((ROUT, 2048), BF),
            pltpu.VMEM((ROUT, 512), F32),
            pltpu.VMEM((32, 64, 512), BF),
            sems(2, 4),
            sems(4),
            sems(4),
            sems(4),
            sems(1),
        ],
        (2 * ROUT * 2048 * 512, 20_000_000),
    )
    st4 = tell(s4)
    st4, square = tie(st4, square)
    t4, z5, s5, sum4 = conv_call(
        "spatial_two",
        fifth_kernel,
        [(st4, NEAR), (norms, VM), (z4, ANY), (late, ANY)],
        ROUT,
        (5, 9),
        1,
        2 * 544 * 4608 * 512,
    )
    st5 = tell(s5)
    h5, z6, s6, sum5 = expand_call("expand_two", 3, 144, st5, norms, z5, late)
    st6 = share(s6)
    out, dv6, b6, sum6 = launch(
        "output",
        last_kernel,
        [(where, SM), (st6, NEAR), (norms, VM)] + [(v, ANY) for v in (z6, mid) + cots],
        [narrow, wide, out_stats, out_stats],
        [
            pltpu.VMEM((4, ROUT, 512), F32),
            pltpu.VMEM((4, ROUT, 512), F32),
            pltpu.VMEM((4, ROUT, 512), BF),
            pltpu.VMEM((ROUT, 512), F32),
            sems(4, 4),
            sems(5),
        ],
        (0, 20_000_000),
    )
    output_local, output_global = unpack("unpack_output", out, (3, 7))
    bt6 = share(b6)
    bt6, output_local, output_global = tie(bt6, output_local, output_global)

    wide_in = [pltpu.VMEM((ROUT, 2048), F32), pltpu.VMEM((ROUT, 2048), F32)]
    flat = [pltpu.VMEM((ROUT, 512), F32)]
    mid_grad, out_grad = (shape((2, 512)), VM), (shape((2, 2048)), VM)
    own_mid, own_out = (shape((ROUT, 128), BF), VM), (shape((ROUT, 512), BF), VM)
    o6, dv5, b5, gr6 = launch(
        "back_expand_two",
        back_six_kernel,
        [(where, SM), (bt6, NEAR), (norms, VM), (sum6, VM), (sum5, VM)]
        + [(v, ANY) for v in (z6, dv6, z5, late)],
        [own_out, narrow, mid_stats, out_grad],
        wide_in
        + flat * 2
        + [
            pltpu.VMEM((ROUT, 2048), BF),
            pltpu.VMEM((512, 2048), BF),
            sems(2, 4),
            sems(1),
            sems(16),
            sems(1),
        ],
        (2 * ROUT * 2048 * 512, 14_000_000),
    )
    bt5 = tell(b5)
    gw6 = grad_call("grad_expand_two", where, [(h5, o6)])
    bt5, *gw6 = tie(bt5, *gw6)
    conv_weight = [pltpu.VMEM((32, 144, 512), BF)]
    o5, dv4, b4, gr5 = launch(
        "back_spatial_two",
        back_five_kernel,
        [(where, SM), (bt5, NEAR), (norms, VM), (sum5, VM), (sum4, VM)]
        + [(v, ANY) for v in (z5, dv5, z4, late)],
        [own_mid, narrow, mid_stats, mid_grad],
        flat * 4
        + [
            pltpu.VMEM((ROUT, 512), BF),
            pltpu.VMEM((5, 5, 16, 512), F32),
            pltpu.VMEM((9, 9, 8, 512), F32),
        ]
        + conv_weight
        + [sems(3), sems(4), sems(1)],
        (2 * ROUT * 4608 * 512, 10_000_000),
    )
    bt4 = tell(b4)
    gw5 = grad_call("grad_spatial_two", where, [(t4, o5)])
    bt4, *gw5 = tie(bt4, *gw5)
    o4, dpre, b3, gr4 = launch(
        "back_reduce_two",
        back_four_kernel,
        [(where, SM), (bt4, NEAR), (norms, VM), (sum4, VM), (sum3, VM), (sums, VM)]
        + [(v, ANY) for v in (z4, dv4, dv6, z3, zs, near)],
        [own_mid, wide, (shape((6, 2048)), VM), mid_grad],
        flat * 2
        + wide_in
        + wide_in[:1]
        + [
            pltpu.VMEM((ROUT, 512), BF),
            pltpu.VMEM((32, 64, 512), BF),
            sems(2),
            sems(3, 4),
            sems(4),
            sems(4),
        ],
        (2 * ROUT * 2048 * 512, 22_000_000),
    )
    bt3 = share(b3)
    gw4 = grad_call("grad_reduce_two", where, [(h3, o4)])
    bt3, *gw4 = tie(bt3, *gw4)
    o3, dv2, b2, gr3, gsum = launch(
        "back_expand_one",
        back_three_kernel,
        [(where, SM), (bt3, NEAR), (norms, VM), (sum3, VM), (sum2, VM)]
        + [(v, ANY) for v in (z3, dpre, z2, near)],
        [own_out, narrow, mid_stats, out_grad, out_stats],
        wide_in
        + flat * 2
        + [
            pltpu.VMEM((ROUT, 2048), BF),
            pltpu.VMEM((512, 2048), BF),
            sems(2, 4),
            sems(1),
            sems(16),
            sems(1),
        ],
        (2 * ROUT * 2048 * 512, 16_000_000),
    )
    bt2 = tell(b2)
    o_s, skip, grs = launch(
        "back_shortcut",
        back_skip_kernel,
        [(where, SM), (norms, VM), (gsum, VM), (sums, VM)]
        + [(v, ANY) for v in (zs, dpre, near)],
        [own_out, (shape((ROUT, 256)), VM), out_grad],
        wide_in
        + [pltpu.VMEM((ROUT, 2048), BF), pltpu.VMEM((256, 2048), BF), sems(2, 4), sems(16)],
        (2 * ROUT * 2048 * 256, 10_000_000),
    )
    pair = grad_call("grad_pair", where, [(h2, o3), (xe, o_s)])
    bt2, skip, *pair = tie(bt2, skip, *pair)
    o2, dv1, b1, gr2 = launch(
        "back_spatial_one",
        back_two_kernel,
        [(where, SM), (bt2, NEAR), (norms, VM), (sum2, VM), (sum1, VM)]
        + [(v, ANY) for v in (z2, dv2, z1, near)],
        [own_mid, (shape((RIN, 512)), ANY), mid_stats, mid_grad],
        flat * 2
        + [
            pltpu.VMEM((4, ROUT, 512), BF),
            pltpu.VMEM((ROUT, 512), F32),
            pltpu.VMEM((4, 4, 16, 512), F32),
            pltpu.VMEM((8, 8, 8, 512), F32),
        ]
        + conv_weight
        + [pltpu.VMEM((RIN, 512), F32), sems(3), sems(4), sems(20)],
        (2 * ROUT * 4608 * 512, 20_000_000),
    )
    bt1 = tell(b1)
    conv = grad_call("grad_spatial_one", where, [(t1, o2)])
    some = jnp.concatenate([add_halves(*v) for v in (gw6, gw5, gw4, pair)]).reshape(16, 464, 128)
    bt1, some, *conv = tie(bt1, some, *conv)
    some = lax.all_to_all(some, PLANE, 0, 0)
    o1, dz1, gr1 = launch(
        "back_reduce_one",
        back_one_kernel,
        [(where, SM), (bt1, NEAR), (norms, VM), (sum1, VM), (z1, ANY), (dv1, ANY)],
        [(shape((RIN, 128), BF), VM), (shape((RIN, 512), BF), ANY), mid_grad],
        [
            pltpu.VMEM((RIN, 512), F32),
            pltpu.VMEM((RIN, 512), F32),
            pltpu.VMEM((RIN, 512), BF),
            sems(20),
            sems(20),
            sems(1),
        ],
        (0, 12_000_000),
    )
    first = launch(
        "grad_reduce_one",
        first_grad_kernel,
        [(where, SM)] + [(v, VM) for v in xs + (o1,)],
        [(shape((512, 128), BF), VM)] * 2,
        (),
        (2 * RIN * 1024 * 128, 6_000_000),
    )
    rest = jnp.concatenate([add_halves(*conv), add_halves(*first)]).reshape(16, 176, 128)
    some, rest = tie(some, rest)
    rest = lax.all_to_all(rest, PLANE, 0, 0)
    here = plane_index().reshape(1).astype(jnp.int32)
    some, squares_ = launch(
        "slice_some",
        functools.partial(slice_kernel, SPANS[0]),
        [(here, SM), (some, VM)],
        [(shape((464, 128), BF), VM), (shape((8, 128)), VM)],
        (),
        (0, 2_000_000),
    )
    parts = [
        [v] + [lax.ppermute(v, axis, ring(4, k)) for k in (1, 2, 3)]
        for v, axis in ((some[:224], "x"), (some[224:], "y"))
    ]
    rest, *some = tie(rest, *parts[0], *parts[1])
    rest = launch(
        "slice_rest",
        functools.partial(slice_kernel, SPANS[1]),
        [(here, SM), (rest, VM), (squares_, VM)],
        [(shape((224, 128), BF), VM)],
        (),
        (0, 1_000_000),
    )[0]
    dimage_local, dimage_global = launch(
        "image_grad",
        image_kernel,
        [(where, SM), (dz1, VM)] + [(v, ANY) for v in xs[::2]] + [(skip, VM)],
        [(shape((12, 6, 6, 256)), VM), (shape((6, 14, 14, 256)), VM)],
        [pltpu.VMEM((2, RIN, 128), F32), pltpu.VMEM((1024, 512), BF), sems(8)],
        (2 * RIN * 512 * 256, 8_000_000),
    )
    rest, dimage_local, dimage_global = tie(rest, dimage_local, dimage_global)
    some = [
        w
        for v, axis in ((jnp.concatenate(some[:4]), "y"), (jnp.concatenate(some[4:]), "x"))
        for w in [v] + [lax.ppermute(v, axis, ring(4, k)) for k in (1, 2, 3)]
    ]
    yi, xi = lax.axis_index("y"), lax.axis_index("x")
    places = jnp.stack(
        [(yi - j) % 4 * 4 + (xi - k) % 4 for j in range(4) for k in range(4)]
        + [(yi - k) % 4 * 4 + (xi - j) % 4 for j in range(4) for k in range(4)]
    )
    places = places.astype(jnp.int32)
    rest = spread(rest, PLANE, 16)
    rest, *some = tie(rest, *some)
    grads = spill("grads_kept", where, places, (*some, rest), ())
    given = swap(rest)
    others = [swap(v) for v in some]
    t6, t5, t4w, t3, ts, t2, t1w = spill("grads_given", where, places, (*others, given), grads)

    def squares(v):
        v = v[:, 176:224].astype(F32).reshape(16, 3, 16, 128)[:, :, :8]
        return jnp.sum(v, axis=(0, 1, 3))

    grad_sq = squares(rest) + squares(given)
    weight_sq = jnp.pad(jnp.sum(square, axis=(1, 2)), (0, 1))
    sq = jnp.concatenate([weight_sq[None], grad_sq[None]])
    sq = sq + lax.ppermute(sq, "z", ring(4, 2))
    sq = (sq + lax.ppermute(sq, "z", ring(4, 1)))[:, :7]
    weight_norm = jnp.sqrt(sq[0])
    ratios = weight_norm / (jnp.sqrt(sq[1]) / 12864.0 + DECAY * weight_norm)

    def cut_own(v, n):
        return lax.dynamic_slice_in_dim(v, zi * n, n, 2)

    mids = cut_own(jnp.stack([gr1, gr2, gr4, gr5]), 128)
    wides = cut_own(jnp.stack([gr3, grs, gr6]), 512)
    return (
        output_global,
        output_local,
        dimage_global,
        dimage_local,
        t1w,
        t2.reshape(spatial_one.shape),
        t3,
        ts,
        t4w,
        t5.reshape(spatial_two.shape),
        t6,
        mids[:, 1],
        wides[:, 1],
        mids[:, 0],
        wides[:, 0],
        ratios,
    )


def solution(mesh):
    fine = Mesh(np.asarray(mesh.devices).reshape(4, 4, 2, 4), EVERY)
    crops = P(BATCH, None, None, "z")
    mat = P(None, "z")
    conv = P(None, None, None, "z")
    weights = (mat, conv, mat, mat, mat, conv, mat)
    return jax.shard_map(
        body,
        mesh=fine,
        in_specs=(crops,) * 4 + weights + (mat,) * 4,
        out_specs=(crops,) * 4 + weights + (mat,) * 4 + (P(),),
        check_vma=False,
    )
```

```python
import functools
import math

import jax
import jax.numpy as jnp
import numpy as np
from jax import lax
from jax.experimental import pallas as pl
from jax.experimental.pallas import tpu as pltpu
from jax.sharding import Mesh, PartitionSpec as P

EPS = 1e-05
DECAY = 5e-05
BATCH = ("y", "x", "c")
PLANE = ("y", "x")
EVERY = ("y", "x", "c", "z")
BF = jnp.bfloat16
F32 = jnp.float32
SLOPE = math.sqrt(2.0 / math.pi)
CUBE = 0.044715

LIN, GIN, RIN = 576, 1568, 2144
LOUT, GOUT, ROUT = 144, 392, 544
M_IN = (36 * 12 * 32.0, 196 * 6 * 32.0)
M_OUT = (9 * 12 * 32.0, 49 * 6 * 32.0)
ANY = pl.BlockSpec(memory_space=pltpu.HBM)
VM = pl.BlockSpec(memory_space=pltpu.VMEM)
NEAR = "near"
FAR = "far"
SM = pl.BlockSpec(memory_space=pltpu.SMEM)


def shape(dims, dtype=F32):
    return jax.ShapeDtypeStruct(dims, dtype)


def launch(name, body, ins, outs, scratch=(), cost=(0, 0)):
    def placed(a, s):
        if s is VM or s is SM:
            return a
        return pltpu.with_memory_space_constraint(a, pltpu.VMEM if s is NEAR else pltpu.HBM)

    return pl.pallas_call(
        body,
        name=name,
        out_shape=tuple(pltpu.HBM(o.shape, o.dtype) if s is not VM else o for o, s in outs),
        in_specs=[VM if s in (NEAR, FAR) else s for _, s in ins],
        out_specs=tuple(VM if s is FAR else s for _, s in outs),
        scratch_shapes=list(scratch),
        compiler_params=pltpu.CompilerParams(vmem_limit_bytes=50 * 1024 * 1024),
        cost_estimate=pl.CostEstimate(flops=cost[0], bytes_accessed=cost[1], transcendentals=0),
    )(*[placed(a, s) for a, s in ins])


def sems(*dims):
    return pltpu.SemaphoreType.DMA(dims)


def go(src, dst, sem):
    c = pltpu.make_async_copy(src, dst, sem)
    c.start()
    return c


def wait(copies):
    for c in copies:
        c.wait()


def quarter(n):
    return pl.ds(n * 512, 512)


def act(v):
    t = jnp.tanh(v * (SLOPE + (SLOPE * CUBE) * (v * v)))
    h = 0.5 * v
    return h + h * t


def slope(v):
    s = v * v
    t = jnp.tanh(v * (SLOPE + (SLOPE * CUBE) * s))
    p = 0.5 + 0.5 * t
    return p + p * (1.0 - t) * (v * (SLOPE + (3.0 * SLOPE * CUBE) * s))


def rows8(v):
    return jnp.sum(v.reshape(-1, 8, v.shape[-1]), axis=0)


def row1(v):
    return jnp.sum(v, axis=0, keepdims=True)


def coefs(sums, k, members, gb):
    g, b = gb
    m = sums[2 * k : 2 * k + 1] / members
    inv = lax.rsqrt(sums[2 * k + 1 : 2 * k + 2] / members - m * m + EPS)
    a = inv * g
    return m, inv, a, b - m * a


def back_coefs(sums, grads, k, members, gb):
    m, inv, a, _ = coefs(sums, k, members, gb)
    c1 = a * inv * (grads[2 * k + 1 : 2 * k + 2] / members)
    return a, c1, a * (grads[2 * k : 2 * k + 1] / members) - m * c1


def mid_gb(norms, i):
    return [
        jnp.concatenate([norms[z, r : r + 1, :] for z in range(4)], axis=1) for r in (i, 4 + i)
    ]


def out_gb(norms, i, z):
    return [
        jnp.concatenate([norms[z, r + l : r + l + 1, :] for l in range(4)], axis=1)
        for r in (8 + 4 * i, 20 + 4 * i)
    ]


def keep(rows, width, group, start):
    i = lax.broadcasted_iota(jnp.int32, (rows, width), 0)
    if group == 0:
        return (i & 15) < 12
    return ((i & 7) < 6) & (i + start < LOUT + GOUT)


def sweep(body, init):
    done = []
    for group, (first, steps, rows) in enumerate(((0, 1, 144), (144, 5, 80))):

        def step(s, carry, group=group, first=first, rows=rows):
            return body(group, pl.multiple_of(first + s * rows, 16), rows, carry)

        done.append(lax.fori_loop(0, steps, step, init))
    return done


LINES = ((0, 6, 96), (576, 14, 112))


def wide_sweep(body, init):
    done = []
    for group, (first, steps, rows) in enumerate(LINES):

        def step(s, carry, group=group, first=first, rows=rows):
            return body(group, s, pl.multiple_of(first + s * rows, 16), rows, carry)

        done.append(lax.fori_loop(0, steps, step, init))
    return done


def lines_in(src, dst, sem):
    for group, (first, steps, rows) in enumerate(LINES):
        for s in range(steps):
            here = pl.ds(first + s * rows, rows)
            go(src.at[here, :], dst.at[here, :], sem.at[6 * group + s])


def line_wait(src, dst, sem, group, s, start, rows):
    here = pl.ds(start, rows)
    pltpu.make_async_copy(src.at[here, :], dst.at[here, :], sem.at[6 * group + s]).wait()


def two(width):
    z = jnp.zeros((8, width), F32)
    return (z, z)


def put_stats(out, done, cols=None):
    rows = jnp.concatenate([row1(s) for group in done for s in group], axis=0)
    if cols is None:
        for p in range(out.shape[0]):
            out[p] = rows
    else:
        out[:, cols] = rows


def moments(z_ref, cols=slice(None)):
    def body(group, start, rows, carry):
        v = z_ref[pl.ds(start, rows), cols]
        return carry[0] + rows8(v), carry[1] + rows8(v * v)

    return sweep(body, two(512))


def added(st, cols=None):
    return jnp.sum(st[...] if cols is None else st[:, :, cols], axis=0)


def dot(a, b):
    return jnp.dot(a, b, preferred_element_type=F32)


def dot_t(a, b):
    return lax.dot_general(a, b, (((1,), (1,)), ((), ())), preferred_element_type=F32)


def riding_in(zi, tops, w, sem):
    return [
        go(
            tops[k].at[pl.ds(TOP, 512), pl.ds(128 * i, 128)],
            w.at[pl.ds(512 * i, 512), pl.ds(pl.multiple_of(zi[k] * 128, 128), 128)],
            sem.at[2 * k + i],
        )
        for k in range(4)
        for i in (0, 1)
    ]


def bundle_in(bundle, at, w, sem):
    n = w.shape[1]
    return [
        go(bundle.at[:, z, pl.ds(at, n), :], w.at[:, :, pl.ds(z * 128, 128)], sem.at[z])
        for z in range(4)
    ]


def bundle_out_in(bundle, at, w, sem):
    n = w.shape[1]
    return [
        go(
            bundle.at[:, z, pl.ds(at + n * j, n), :],
            w.at[:, :, pl.ds(z * 512 + j * 128, 128)],
            sem.at[4 * z + j],
        )
        for z in range(4)
        for j in range(4)
    ]


def pack_kernel(side, cuts, local, glob, *refs):
    more, outs, tmp = refs[: -1 - len(cuts)], refs[-1 - len(cuts) : -1], refs[-1]
    tmp[...] = jnp.zeros_like(tmp)
    base = side[0] * side[0] * 16
    if more:
        outs[0][pl.ds(outs[0].shape[0] - 512, 512), 0:128] = more[0][0:512, :]
        outs[0][pl.ds(outs[0].shape[0] - 512, 512), 128:256] = more[0][512:1024, :]
    for lane in range(tmp.shape[0]):
        cols = slice(lane * 128, lane * 128 + 128)
        for n in range(12):
            for h in range(side[0]):
                v = local[n, h, :, cols].astype(F32)
                tmp[lane, pl.ds(h * side[0] * 16 + n, side[0], stride=16), :] = v
        for n in range(6):
            for h in range(side[1]):
                v = glob[n, h, :, cols].astype(F32)
                tmp[lane, pl.ds(base + h * side[1] * 8 + n, side[1], stride=8), :] = v
        at = 0
        for out, n in zip(outs, cuts):
            out[pl.ds(0, n), cols] = tmp[lane, pl.ds(at, n), :].astype(out.dtype)
            at += n


def pack(name, local, glob, side, cuts, more=()):
    c = local.shape[-1]
    rows = sum(cuts)
    extra = (512 * len(more), 0)
    return launch(
        name,
        functools.partial(pack_kernel, side, cuts),
        [(v, FAR) for v in (local, glob) + more],
        [(shape((n + e, c), BF), VM) for n, e in zip(cuts, extra)],
        [pltpu.VMEM((c // 128, rows, 128), F32)],
        (0, 4 * rows * c),
    )


def unpack_kernel(side, lanes, local, glob):
    base = side[0] * side[0] * 16
    for lane in range(lanes.shape[0]):
        cols = slice(lane * 128, lane * 128 + 128)
        for n in range(12):
            for h in range(side[0]):
                v = lanes[lane, pl.ds(h * side[0] * 16 + n, side[0], stride=16), :]
                local[n, h, :, cols] = v
        for n in range(6):
            for h in range(side[1]):
                v = lanes[lane, pl.ds(base + h * side[1] * 8 + n, side[1], stride=8), :]
                glob[n, h, :, cols] = v


def unpack_whole(side, rows, local, glob, lanes):
    for lane in range(lanes.shape[0]):
        lanes[lane] = rows[:, lane * 128 : lane * 128 + 128]
    unpack_kernel(side, lanes, local, glob)


def unpack(name, rows, side):
    c = rows.shape[-1]
    return launch(
        name,
        functools.partial(unpack_whole, side),
        [(rows, VM)],
        [
            (shape((12, side[0], side[0], c)), VM),
            (shape((6, side[1], side[1], c)), VM),
        ],
        [pltpu.VMEM((c // 128,) + rows.shape[:1] + (128,), F32)],
        (0, 8 * rows.size),
    )


def pieces_kernel(at, spatial_one, expand_one, shortcut, reduce_two, spatial_two, expand_two, near, late, sem):
    copies = []

    def take(src, dst, first):
        n = src.shape[0] // 32
        rows = pl.ds(pl.multiple_of(at[0] * n, 16), n)
        for j in range(src.shape[1] // 128):
            here = dst.at[pl.ds(first, n), :]
            copies.append(go(src.at[rows, pl.ds(128 * j, 128)], here, sem.at[len(copies)]))
            first += n

    take(spatial_one, near, 0)
    take(expand_one, near, 144)
    take(shortcut, near, 208)
    take(reduce_two, near, 336)
    take(spatial_two, late, 0)
    take(expand_two, late, 144)
    wait(copies)


def square_kernel(*refs):
    out = refs[-1]
    for i, w in enumerate(refs[:-1]):
        n = w.shape[0] // 8
        total = jnp.zeros((8, 128), F32)
        for lane in range(w.shape[1] // 128):
            cols = slice(lane * 128, lane * 128 + 128)

            def step(s, t, w=w, cols=cols, n=n):
                v = w[pl.ds(pl.multiple_of(s * n, 16), n), cols].astype(F32)
                return t + rows8(v * v)

            total = lax.fori_loop(0, 8, step, total)
        out[i] = total


PARTS = ((0, 576), (576, 224), (800, 672), (1472, 672))
TOP = 800


def wide_moments(z_ref, parts):
    z8 = jnp.zeros((8, 512), F32)
    carry = (z8, z8)
    for first, rows in parts:

        def step(s, c, first=first):
            v = z_ref[pl.ds(pl.multiple_of(first + s * 64, 16), 64), :]
            return c[0] + rows8(v), c[1] + rows8(v * v)

        carry = lax.fori_loop(0, rows // 64, step, carry)
        left = rows % 64
        if left:
            v = z_ref[pl.ds(first + rows - left, left), :]
            carry = (carry[0] + rows8(v), carry[1] + rows8(v * v))
    return carry


def first_kernel(zi, *refs):
    xs, rest = refs[:8], refs[8:]
    z1, stats, xv, zv, w, xsem, osem, ws = rest
    weight = riding_in(zi, xs[::2], w, ws)
    cin = []
    for i, (first, rows) in enumerate(PARTS):
        half, base = (0, 0) if first < TOP else (1, TOP)
        one = []
        for k in range(4):
            cols = pl.ds(pl.multiple_of(zi[k] * 256, 256), 256)
            src = xs[2 * k + half].at[pl.ds(first - base, rows), :]
            one.append(go(src, xv.at[pl.ds(first, rows), cols], xsem.at[i, k]))
        cin.append(one)
    wait(weight)
    wf = w
    out, sums = [], []
    for i, (first, rows) in enumerate(PARTS):
        here = pl.ds(first, rows)
        wait(cin[i])
        zv[here, :] = dot(xv[here, :], wf[...])
        out.append(go(zv.at[here, :], z1.at[here, :], osem.at[i]))
    put_stats(stats, [wide_moments(zv, PARTS[:1]), wide_moments(zv, PARTS[1:])])
    wait(out)


def load_taps(local, glob, i, j, stride):
    c = local.shape[-1]
    if stride == 2:
        lv = local.reshape(4, 2, 4, 2, 16, c)
        gv = glob.reshape(8, 2, 8, 2, 8, c)
        a, p, b, q = i // 2, i % 2, j // 2, j % 2
        lt = lv[a : a + 3, p, b : b + 3, q]
        gt = gv[a : a + 7, p, b : b + 7, q]
    else:
        lt = local[i : i + 3, j : j + 3]
        gt = glob[i : i + 7, j : j + 7]
    return jnp.concatenate(
        [lt.reshape(LOUT, c), gt.reshape(GOUT, c), jnp.zeros((8, c), F32)], axis=0
    )


def clear_border(ref):
    side = ref.shape[0]
    zero = jnp.zeros((side,) + ref.shape[2:], F32)
    ref[0] = zero
    ref[side - 1] = zero
    for r in range(1, side - 1):
        ref[r, 0] = zero[0]
        ref[r, side - 1] = zero[0]


def conv_tail(stride, hl, hg, weight, wf, tv, taps, ts, zv, z, zsem, stats):
    out = []
    for k in range(9):
        cols = pl.ds(k * 512, 512)
        tv[:, cols] = load_taps(hl, hg, k // 3, k % 3, stride).astype(BF)
        out.append(go(tv.at[:, cols], taps.at[:, cols], ts.at[k]))
        if k == 0:
            wait(weight)
            zv[...] = dot(tv[:, cols], wf[0:512, :])
        else:
            zv[...] += dot(tv[:, cols], wf[k * 512 : (k + 1) * 512, :])
    out.append(go(zv, z, zsem))
    put_stats(stats, moments(zv))
    wait(out)


def second_kernel(st, norms, z1, near, taps, z2, stats, sums, zin, hl, hg, w, tv, zv, xs, ws, ts, zsem):
    lines_in(z1, zin, xs)
    weight = bundle_in(near, 0, w, ws)
    total = added(st)
    sums[...] = total
    gb = mid_gb(norms, 0)
    cs = [coefs(total, k, M_IN[k], gb) for k in (0, 1)]
    clear_border(hl)
    clear_border(hg)

    def body(group, s, start, rows, carry):
        _, _, a, sh = cs[group]
        line_wait(z1, zin, xs, group, s, start, rows)
        i = lax.broadcasted_iota(jnp.int32, (rows, 512), 0)
        ok = (i & 15) < 12 if group == 0 else (i & 7) < 6
        h = jnp.where(ok, act(zin[pl.ds(start, rows), :] * a + sh), 0.0)
        if group == 0:
            hl[s + 1, 1:7] = h.reshape(6, 16, 512)
        else:
            hg[s + 1, 1:15] = h.reshape(14, 8, 512)
        return carry

    wide_sweep(body, 0)
    conv_tail(2, hl, hg, weight, w.reshape(4608, 512), tv, taps, ts, zv, z2, zsem.at[0], stats)


def fifth_kernel(st, norms, z4, late, taps, z5, stats, sums, zin, hl, hg, w, tv, zv, xs, ws, ts, zsem):
    cin = go(z4, zin, xs.at[0])
    weight = bundle_in(late, 0, w, ws)
    total = added(st)
    sums[...] = total
    gb = mid_gb(norms, 2)
    cs = [coefs(total, k, M_OUT[k], gb) for k in (0, 1)]
    clear_border(hl)
    clear_border(hg)
    cin.wait()
    for group, (first, side, rows) in enumerate(((0, 3, 48), (144, 7, 56))):
        _, _, a, sh = cs[group]
        i = lax.broadcasted_iota(jnp.int32, (rows, 512), 0)
        ok = (i & 15) < 12 if group == 0 else (i & 7) < 6

        def step(s, carry, group=group, first=first, rows=rows, a=a, sh=sh, ok=ok):
            v = zin[pl.ds(pl.multiple_of(first + s * rows, 8), rows), :]
            h = jnp.where(ok, act(v * a + sh), 0.0)
            if group == 0:
                hl[s + 1, 1:4] = h.reshape(3, 16, 512)
            else:
                hg[s + 1, 1:8] = h.reshape(7, 8, 512)
            return carry

        lax.fori_loop(0, side, step, 0)
    conv_tail(1, hl, hg, weight, w.reshape(4608, 512), tv, taps, ts, zv, z5, zsem.at[0], stats)


def conv_call(name, kernel, ins, rows, sides, n, flops):
    sl, sg = sides
    return launch(
        name,
        kernel,
        ins,
        [
            (shape((ROUT, 4608), BF), ANY),
            (shape((ROUT, 512)), ANY),
            (shape((32, 4, 512)), FAR),
            (shape((4, 512)), VM),
        ],
        [
            pltpu.VMEM((rows, 512), F32),
            pltpu.VMEM((sl, sl, 16, 512), F32),
            pltpu.VMEM((sg, sg, 8, 512), F32),
            pltpu.VMEM((32, 144, 512), BF),
            pltpu.VMEM((ROUT, 4608), BF),
            pltpu.VMEM((ROUT, 512), F32),
            sems(n),
            sems(13),
            sems(9),
            sems(1),
        ],
        (flops, 20_000_000),
    )


def expand_kernel(which, at, st, norms, z, bundle, h, zo, stats, sums, zin, hv, zv, w, wsem, hsem, zsem, isem):
    cin = go(z, zin, isem.at[0])
    weight = bundle_out_in(bundle, at, w.reshape(32, 16, 2048), wsem)
    total = added(st)
    sums[...] = total
    gb = mid_gb(norms, which)
    cs = [coefs(total, k, M_OUT[k], gb) for k in (0, 1)]
    cin.wait()

    def body(group, start, rows, carry):
        _, _, a, sh = cs[group]
        v = act(zin[pl.ds(start, rows), :] * a + sh)
        hv[pl.ds(start, rows), :] = jnp.where(keep(rows, 512, group, start), v, 0.0).astype(BF)
        return carry

    sweep(body, 0)
    out = [go(hv, h, hsem.at[0])]
    wait(weight)
    for n in range(4):
        cols = quarter(n)
        zv[:, cols] = dot(hv[...], w[:, cols])
        out.append(go(zv.at[:, cols], zo.at[:, cols], zsem.at[n]))
        put_stats(stats, moments(zv, cols), cols)
    wait(out)


def expand_call(name, which, at, st, norms, z, bundle):
    return launch(
        name,
        functools.partial(expand_kernel, which, at),
        [(st, NEAR), (norms, VM), (z, ANY), (bundle, ANY)],
        [
            (shape((ROUT, 512), BF), ANY),
            (shape((ROUT, 2048)), ANY),
            (shape((4, 2048)), VM),
            (shape((4, 512)), VM),
        ],
        [
            pltpu.VMEM((ROUT, 512), F32),
            pltpu.VMEM((ROUT, 512), BF),
            pltpu.VMEM((ROUT, 2048), F32),
            pltpu.VMEM((512, 2048), BF),
            sems(16),
            sems(1),
            sems(4),
            sems(1),
        ],
        (2 * 544 * 512 * 2048, 9_000_000),
    )


def skip_kernel(zi, *refs):
    x, bundle, rest = refs[:8], refs[8], refs[9:]
    xe, zs, stats, xv, ev, tmp, zv, w, xs, ws, es, os = rest
    xin = [
        [
            go(x[2 * k].at[pl.ds(0, TOP), :], xv.at[k, pl.ds(0, TOP), :], xs.at[k, 0]),
            go(x[2 * k + 1], xv.at[k, pl.ds(TOP, RIN - TOP), :], xs.at[k, 1]),
        ]
        for k in range(4)
    ]
    weight = bundle_out_in(bundle, 208, w.reshape(32, 32, 2048), ws)
    tmp[pl.ds(536, 8), :] = jnp.zeros((8, 256), F32)
    for k in range(4):
        wait(xin[k])
        for r in range(3):
            v = xv[k, pl.ds(r * 192, 96), :].astype(F32).reshape(3, 2, 16, 256)[:, 0]
            tmp[pl.ds(r * 48, 48), :] = v.reshape(48, 256)
        for r in range(7):
            v = xv[k, pl.ds(576 + r * 224, 112), :].astype(F32).reshape(7, 2, 8, 256)[:, 0]
            tmp[pl.ds(144 + r * 56, 56), :] = v.reshape(56, 256)
        at = pl.multiple_of(zi[k] * 256, 256)
        ev[:, pl.ds(at, 256)] = tmp[...].astype(BF)
    out = [go(ev, xe, es.at[0])]
    wait(weight)
    for n in range(4):
        cols = quarter(n)
        zv[:, cols] = dot(ev[...], w[:, cols])
        out.append(go(zv.at[:, cols], zs.at[:, cols], os.at[n]))
        put_stats(stats, moments(zv, cols), cols)
    wait(out)


def middle_kernel(st3, norms, z3, zs, late, mid, h3, z4, stats, sum3, sums, z3v, zsv, hv, zv, w, ins, ws, os, hs, zsem):
    cin = []
    for n in range(4):
        cols = quarter(n)
        cin.append(
            [go(z3.at[:, cols], z3v.at[:, cols], ins.at[0, n]), go(zs.at[:, cols], zsv.at[:, cols], ins.at[1, n])]
        )
    weight = bundle_in(late, 336, w, ws)
    wf = w.reshape(2048, 512)
    out = []
    for n in range(4):
        cols = quarter(n)
        both = added(st3, cols)
        s3, ss = both[0:4], both[4:8]
        sum3[:, cols] = s3
        sums[:, cols] = ss
        cs = []
        for k in (0, 1):
            _, _, a3, b3 = coefs(s3, k, M_OUT[k], out_gb(norms, 0, n))
            _, _, a5, b5 = coefs(ss, k, M_OUT[k], out_gb(norms, 1, n))
            cs.append((a3, a5, b3 + b5))
        wait(cin[n])

        def body(group, start, rows, carry, cols=cols, cs=cs):
            a3, a5, b = cs[group]
            here = (pl.ds(start, rows), cols)
            v = act(z3v[here] * a3 + zsv[here] * a5 + b)
            v = jnp.where(keep(rows, 512, group, start), v, 0.0)
            z3v[here] = v
            hv[here] = v.astype(BF)
            return carry

        sweep(body, 0)
        out.append(go(z3v.at[:, cols], mid.at[:, cols], os.at[n]))
        out.append(go(hv.at[:, cols], h3.at[:, cols], hs.at[n]))
        if n == 0:
            wait(weight)
            zv[...] = dot(hv[:, cols], wf[0:512, :])
        else:
            zv[...] += dot(hv[:, cols], wf[n * 512 : (n + 1) * 512, :])
    out.append(go(zv, z4, zsem.at[0]))
    put_stats(stats, moments(zv))
    wait(out)


def last_kernel(zi, st, norms, z6, mid, *refs):
    cots, rest = refs[:8], refs[8:]
    out, dv6, stats, sums, zv, mv, cv, ov, ins, os = rest
    cin = []
    for k in range(4):
        cols = pl.ds(pl.multiple_of(zi[k] * 512, 512), 512)
        cin.append(
            [
                go(z6.at[:, cols], zv.at[k], ins.at[0, k]),
                go(mid.at[:, cols], mv.at[k], ins.at[1, k]),
                go(cots[2 * k], cv.at[k, pl.ds(0, 272), :], ins.at[2, k]),
                go(cots[2 * k + 1], cv.at[k, pl.ds(272, 272), :], ins.at[3, k]),
            ]
        )
    sums[...] = added(st)
    done_out = []
    for k in range(4):
        cols = pl.ds(pl.multiple_of(zi[k] * 512, 512), 512)
        total = sums[:, cols]
        gb = out_gb(norms, 2, zi[k])
        cs = [coefs(total, j, M_OUT[j], gb) for j in (0, 1)]
        wait(cin[k])

        def body(group, start, rows, carry, cs=cs, k=k):
            m, _, a, sh = cs[group]
            here = pl.ds(start, rows)
            z = zv[k, here, :]
            v = z * a + sh + mv[k, here, :]
            if k == 0:
                ov[here, :] = act(v)
            d = slope(v) * cv[k, here, :].astype(F32)
            mv[k, here, :] = d
            return carry[0] + rows8(d), carry[1] + rows8(d * (z - m))

        done = sweep(body, two(512))
        done_out.append(go(mv.at[k], dv6.at[:, cols], os.at[k]))
        if k == 0:
            done_out.append(go(ov, out, os.at[4]))
        done = [(s, q * cs[j][1]) for j, (s, q) in enumerate(done)]
        put_stats(stats, done, cols)
    wait(done_out)


def grads_out(ref, grads, cols=slice(None)):
    ref[0:1, cols] = grads[0:1] + grads[2:3]
    ref[1:2, cols] = grads[1:2] + grads[3:4]


def slope_rows(dy, z, cs):
    def body(group, start, rows, carry):
        m, _, a, sh = cs[group]
        here = (pl.ds(start, rows), slice(None))
        v = z[here]
        d = jnp.where(keep(rows, 512, group, start), slope(v * a + sh) * dy[here], 0.0)
        dy[here] = d
        return carry[0] + rows8(d), carry[1] + rows8(d * (v - m))

    return [(s, q * cs[j][1]) for j, (s, q) in enumerate(sweep(body, two(512)))]


def norm_rows(dy, z, cs, cols, dz):
    def body(group, start, rows, carry):
        a, c1, c0 = cs[group]
        here = (pl.ds(start, rows), cols)
        d = a * dy[here] - c1 * z[here] - c0
        dz[here] = jnp.where(keep(rows, 512, group, start), d, 0.0).astype(dz.dtype)
        return carry

    sweep(body, 0)


def all_coefs(sums, gb):
    return [coefs(sums, k, M_OUT[k], gb) for k in (0, 1)]


def all_back(sums, grads, gb, members=M_OUT):
    return [back_coefs(sums, grads, k, members[k], gb) for k in (0, 1)]


def own_cols(dst, src, zi, width):
    at = pl.multiple_of(zi[0] * width, width)
    dst[...] = src[:, pl.ds(at, width)].astype(dst.dtype)


def back_six_kernel(zi, stb, norms, sum6, sum5, z6, dv6, z5, late, own, dv5, stats, grad, zv, dv, z5v, acc, dz, w, ins, i5, ws, os):
    cin = []
    for n in range(4):
        cols = quarter(n)
        cin.append(
            [go(z6.at[:, cols], zv.at[:, cols], ins.at[0, n]), go(dv6.at[:, cols], dv.at[:, cols], ins.at[1, n])]
        )
    weight = bundle_out_in(late, 144, w.reshape(32, 16, 2048), ws)
    c5 = go(z5, z5v, i5.at[0])
    for n in range(4):
        cols = quarter(n)
        grads = added(stb, cols)
        grads_out(grad, grads, cols)
        cs = all_back(sum6[:, cols], grads, out_gb(norms, 2, n))
        wait(cin[n])
        norm_rows(dv, zv, cs, cols, dz)
        if n == 0:
            wait(weight)
            acc[...] = dot_t(dz[:, cols], w[:, cols])
        else:
            acc[...] += dot_t(dz[:, cols], w[:, cols])
    own_cols(own, dz, zi, 512)
    c5.wait()
    done = slope_rows(acc, z5v, all_coefs(sum5[...], mid_gb(norms, 3)))
    out = go(acc, dv5, os.at[0])
    put_stats(stats, done)
    out.wait()


def pad_back(dzl, dzg, dz, at):
    dzl[...] = jnp.zeros_like(dzl)
    dzg[...] = jnp.zeros_like(dzg)
    for r in range(3):
        dzl[at + r, at : at + 3] = dz[pl.ds(48 * r, 48), :].reshape(3, 16, 512)
    for r in range(7):
        dzg[at + r, at : at + 7] = dz[pl.ds(144 + 56 * r, 56), :].reshape(7, 8, 512)


def back_five_kernel(zi, stb, norms, sum5, sum4, z5, dv5, z4, late, own, dv4, stats, grad, zv, dv, z4v, acc, dz, dzl, dzg, w, ins, ws, os):
    cin = [go(z5, zv, ins.at[0]), go(dv5, dv, ins.at[1])]
    weight = bundle_in(late, 0, w, ws)
    c4 = go(z4, z4v, ins.at[2])
    grads = added(stb)
    grads_out(grad, grads)
    cs = all_back(sum5[...], grads, mid_gb(norms, 3))
    wait(cin)
    norm_rows(dv, zv, cs, slice(None), dv)
    own_cols(own, dv, zi, 128)
    pad_back(dzl, dzg, dv, 1)
    wait(weight)
    wf = w.reshape(4608, 512)
    for k in range(9):
        dz[...] = load_taps(dzl, dzg, 2 - k // 3, 2 - k % 3, 1).astype(BF)
        part = dot_t(dz[...], wf[k * 512 : (k + 1) * 512, :])
        if k == 0:
            acc[...] = part
        else:
            acc[...] += part
    c4.wait()
    done = slope_rows(acc, z4v, all_coefs(sum4[...], mid_gb(norms, 2)))
    out = go(acc, dv4, os.at[0])
    put_stats(stats, done)
    out.wait()


def back_four_kernel(zi, stb, norms, sum4, sum3, sums, z4, dv4, dv6, z3, zs, late, own, dpre, stats, grad, zv, dv, d6, z3v, zsv, dz, w, in4, ins, ws, os):
    cin = [go(z4, zv, in4.at[0]), go(dv4, dv, in4.at[1])]
    weight = bundle_in(late, 336, w, ws)
    wide = []
    for n in range(4):
        cols = quarter(n)
        wide.append(
            [
                go(src.at[:, cols], dst.at[:, cols], ins.at[i, n])
                for i, (src, dst) in enumerate(((dv6, d6), (z3, z3v), (zs, zsv)))
            ]
        )
    grads = added(stb)
    grads_out(grad, grads)
    cs4 = all_back(sum4[...], grads, mid_gb(norms, 2))
    wait(cin)
    norm_rows(dv, zv, cs4, slice(None), dz)
    own_cols(own, dz, zi, 128)
    wait(weight)
    wf = w.reshape(2048, 512)
    z8 = jnp.zeros((8, 512), F32)
    out = []
    for n in range(4):
        cols = quarter(n)
        s3, ss = sum3[:, cols], sums[:, cols]
        cs = []
        for k in (0, 1):
            m3, i3, a3, b3 = coefs(s3, k, M_OUT[k], out_gb(norms, 0, n))
            ms, is_, a5, b5 = coefs(ss, k, M_OUT[k], out_gb(norms, 1, n))
            cs.append((a3, a5, b3 + b5, m3, ms, i3, is_))
        zv[...] = dot_t(dz[...], wf[n * 512 : (n + 1) * 512, :])
        wait(wide[n])

        def body(group, start, rows, carry, cols=cols, cs=cs):
            a3, a5, b, m3, ms, _, _ = cs[group]
            here = (pl.ds(start, rows), cols)
            u, v = z3v[here], zsv[here]
            d = slope(u * a3 + v * a5 + b) * (zv[pl.ds(start, rows), :] + d6[here])
            d = jnp.where(keep(rows, 512, group, start), d, 0.0)
            d6[here] = d
            return (
                carry[0] + rows8(d),
                carry[1] + rows8(d * (u - m3)),
                carry[2] + rows8(d * (v - ms)),
            )

        done = sweep(body, (z8, z8, z8))
        out.append(go(d6.at[:, cols], dpre.at[:, cols], os.at[n]))
        done = [(s, p * cs[j][5], q * cs[j][6]) for j, (s, p, q) in enumerate(done)]
        put_stats(stats, done, cols)
    wait(out)


def pick(grads, rows):
    return jnp.concatenate([grads[r : r + 1] for r in rows], axis=0)


def back_three_kernel(zi, stb, norms, sum3, sum2, z3, dpre, z2, bundle, own, dv2, stats, grad, gsum, zv, dv, z2v, acc, dz, w, ins, i2, ws, os):
    cin = []
    for n in range(4):
        cols = quarter(n)
        cin.append(
            [go(z3.at[:, cols], zv.at[:, cols], ins.at[0, n]), go(dpre.at[:, cols], dv.at[:, cols], ins.at[1, n])]
        )
    weight = bundle_out_in(bundle, 144, w.reshape(32, 16, 2048), ws)
    c2 = go(z2, z2v, i2.at[0])
    for n in range(4):
        cols = quarter(n)
        grads = added(stb, cols)
        gsum[:, cols] = pick(grads, (0, 2, 3, 5))
        grads = pick(grads, (0, 1, 3, 4))
        grads_out(grad, grads, cols)
        cs = all_back(sum3[:, cols], grads, out_gb(norms, 0, n))
        wait(cin[n])
        norm_rows(dv, zv, cs, cols, dz)
        if n == 0:
            wait(weight)
            acc[...] = dot_t(dz[:, cols], w[:, cols])
        else:
            acc[...] += dot_t(dz[:, cols], w[:, cols])
    own_cols(own, dz, zi, 512)
    c2.wait()
    done = slope_rows(acc, z2v, all_coefs(sum2[...], mid_gb(norms, 1)))
    out = go(acc, dv2, os.at[0])
    put_stats(stats, done)
    out.wait()


def back_skip_kernel(zi, norms, gsum, sums, zs, dpre, bundle, own, skip, grad, zv, dv, dz, w, ins, ws):
    cin = []
    for n in range(4):
        cols = quarter(n)
        cin.append(
            [go(zs.at[:, cols], zv.at[:, cols], ins.at[0, n]), go(dpre.at[:, cols], dv.at[:, cols], ins.at[1, n])]
        )
    wv = w.reshape(8, 32, 2048)
    weight = [
        go(
            bundle.at[pl.ds(zi[0] * 8, 8), z, pl.ds(208 + 32 * j, 32), :],
            wv.at[:, :, pl.ds(z * 512 + j * 128, 128)],
            ws.at[4 * z + j],
        )
        for z in range(4)
        for j in range(4)
    ]
    for n in range(4):
        here = quarter(n)
        grads = gsum[:, here]
        grads_out(grad, grads, here)
        cs = all_back(sums[:, here], grads, out_gb(norms, 1, n))
        wait(cin[n])
        norm_rows(dv, zv, cs, here, dz)
    own_cols(own, dz, zi, 512)
    wait(weight)
    skip[...] = dot_t(dz[...], w[...])


def back_two_kernel(zi, stb, norms, sum2, sum1, z2, dv2, z1, near, *refs):
    (own, dv1, stats, grad, zv, dv, dz, acc, dzl, dzg, w, z1v, ins, ws, os) = refs
    cin = [go(z2, zv, ins.at[0]), go(dv2, dv, ins.at[1])]
    weight = bundle_in(near, 0, w, ws)
    c1 = go(z1, z1v, ins.at[2])
    grads = added(stb)
    grads_out(grad, grads)
    cs = all_back(sum2[...], grads, mid_gb(norms, 1))
    wait(cin)
    norm_rows(dv, zv, cs, slice(None), dv)
    own_cols(own, dv, zi, 128)
    pad_back(dzl, dzg, dv, 0)
    for i in range(4):
        dz[i] = load_taps(dzl, dzg, i // 2, i % 2, 1).astype(BF)
    wait(weight)
    wf = w.reshape(4608, 512)
    gb1 = mid_gb(norms, 0)
    c1s = [coefs(sum1[...], k, M_IN[k], gb1) for k in (0, 1)]
    reach = (((1, 0),), ((2, 0), (0, 1)))
    z8 = jnp.zeros((8, 512), F32)
    totals = [(z8, z8), (z8, z8)]
    out = []
    for p in (0, 1):
        for q in (0, 1):
            first = True
            for i, di in reach[p]:
                for j, dj in reach[q]:
                    k = 3 * i + j
                    part = dot_t(dz[2 * di + dj], wf[k * 512 : (k + 1) * 512, :])
                    if first:
                        acc[...] = part
                    else:
                        acc[...] += part
                    first = False
            if p == 0 and q == 0:
                c1.wait()
            for group, (base, side, n, from_row) in enumerate(((0, 3, 16, 0), (576, 7, 8, 144))):
                m, _, a, sh = c1s[group]
                rows = side * n
                i_ = lax.broadcasted_iota(jnp.int32, (rows, 512), 0)
                okay = (i_ & 15) < 12 if group == 0 else (i_ & 7) < 6
                cells = z1v.at[pl.ds(base, 4 * side * side * n), :]
                cells = cells.reshape(side, 2, side, 2, n, 512)

                def step(r, carry, n=n, side=side, rows=rows, from_row=from_row, m=m, a=a, sh=sh, okay=okay, cells=cells, p=p, q=q):
                    v = cells[r, p, :, q].reshape(rows, 512)
                    g = acc[pl.ds(pl.multiple_of(from_row + r * rows, 8), rows), :]
                    d = jnp.where(okay, slope(v * a + sh) * g, 0.0)
                    cells[r, p, :, q] = d.reshape(side, n, 512)
                    return carry[0] + rows8(d), carry[1] + rows8(d * (v - m))

                totals[group] = lax.fori_loop(0, side, step, totals[group])
        for group, (first_row, steps, rows) in enumerate(LINES):
            for s in range(p, steps, 2):
                here = pl.ds(first_row + s * rows, rows)
                out.append(go(z1v.at[here, :], dv1.at[here, :], os.at[6 * group + s]))
    put_stats(stats, [(s, t * c1s[j][1]) for j, (s, t) in enumerate(totals)])
    wait(out)


def back_one_kernel(zi, stb, norms, sum1, z1, dv1, own, dz1, grad, zv, dv, dzv, is0, is1, os):
    lines_in(z1, zv, is0)
    lines_in(dv1, dv, is1)
    grads = added(stb)
    grads_out(grad, grads)
    cs = all_back(sum1[...], grads, mid_gb(norms, 0), M_IN)

    def body(group, s, start, rows, carry):
        a, c1, c0 = cs[group]
        line_wait(z1, zv, is0, group, s, start, rows)
        line_wait(dv1, dv, is1, group, s, start, rows)
        here = (pl.ds(start, rows), slice(None))
        i = lax.broadcasted_iota(jnp.int32, (rows, 512), 0)
        ok = (i & 15) < 12 if group == 0 else (i & 7) < 6
        d = a * dv[here] - c1 * zv[here] - c0
        dzv[here] = jnp.where(ok, d, 0.0).astype(BF)
        return carry

    wide_sweep(body, 0)
    out = go(dzv, dz1, os.at[0])
    own_cols(own, dzv, zi, 128)
    out.wait()


def image_kernel(zi, dz1, t0, t1, t2, t3, skip, local, glob, img, w, ws):
    wait(riding_in(zi, (t0, t1, t2, t3), w, ws))
    mine = w[pl.ds(pl.multiple_of(zi[0] * 256, 256), 256), :]
    for lane in range(2):
        cols = slice(lane * 128, lane * 128 + 128)
        img[lane] = dot_t(dz1[...], mine[lane * 128 : lane * 128 + 128])
        lv = img.at[lane, pl.ds(0, LIN)].reshape(3, 2, 3, 2, 16, 128)
        gv = img.at[lane, pl.ds(LIN, GIN)].reshape(7, 2, 7, 2, 8, 128)
        lv[:, 0, :, 0] += skip[pl.ds(0, LOUT), cols].reshape(3, 3, 16, 128)
        gv[:, 0, :, 0] += skip[pl.ds(LOUT, GOUT), cols].reshape(7, 7, 8, 128)
    unpack_kernel((6, 14), img, local, glob)


def flipped(a, bt):
    return dot(bt, a).T.astype(BF)


def halves_out(zi, a, bt, width, held, give, at):
    for c, dst in enumerate((held, give)):
        half = zi[4] if c == 0 else 1 - zi[4]
        begin = pl.multiple_of(half * width, width)
        for k in range(0, width, 256):
            n = min(256, width - k)
            v = flipped(a[:, pl.ds(pl.multiple_of(begin + k, 128), n)], bt)
            for j in range(v.shape[1] // 128):
                row = at + j * width + k
                dst[row : row + n, :] = v[:, 128 * j : 128 * (j + 1)]


def grad_kernel(widths, zi, *refs):
    held, give = refs[-2:]
    at = 0
    for i, width in enumerate(widths):
        a, b = refs[2 * i], refs[2 * i + 1]
        bt = b[...].astype(F32).T.astype(BF)
        halves_out(zi, a, bt, width, held, give, at)
        at += width * b.shape[1] // 128


def grad_call(name, zi, pairs):
    widths = [a.shape[1] // 2 for a, _ in pairs]
    rows = sum(a.shape[1] * b.shape[1] // 256 for a, b in pairs)
    return launch(
        name,
        functools.partial(grad_kernel, widths),
        [(zi, SM)] + [(v, VM) for pair in pairs for v in pair],
        [(shape((rows, 128), BF), VM)] * 2,
        (),
        (4 * ROUT * rows * 128, 7_000_000),
    )


def first_grad_kernel(zi, *refs):
    xs, (o1, held, give) = refs[:8], refs[8:]
    bt = o1[...].astype(F32).T.astype(BF)
    for k in range(4):
        v = dot(bt[:, :768], xs[2 * k][0:768, :]) + dot(bt[:, 896:], xs[2 * k + 1][96:, :])
        edge = jnp.concatenate([xs[2 * k][768:800, :], xs[2 * k + 1][0:96, :]], axis=0)
        v = v + dot(bt[:, 768:896], edge)
        v = v.T.astype(BF)
        mine = zi[4] == k // 2
        rows = slice((k % 2) * 256, (k % 2) * 256 + 256)

        @pl.when(mine)
        def _():
            held[rows, :] = v

        @pl.when(jnp.logical_not(mine))
        def _():
            give[rows, :] = v


SPANS = (
    (6, 0, 1024),
    (5, 1024, 3328),
    (4, 3328, 4352),
    (2, 4352, 5376),
    (3, 5376, 7424),
), ((1, 0, 2304), (0, 2304, 2816))


def slice_kernel(spans, at, src, *refs):
    out = refs[0] if spans is SPANS[0] else refs[1]
    squares = [jnp.zeros((1, 128), F32)] * 8
    n = src.shape[1]
    v = src[0].astype(F32)
    for p in range(1, 16):
        v = v + src[p].astype(F32)
    out[0:n, :] = v.astype(BF)
    v = v * v
    row = lax.broadcasted_iota(jnp.int32, (n, 128), 0) + at[0] * n
    for i, lo, hi in spans:
        squares[i] = row1(jnp.where((row >= lo) & (row < hi), v, 0.0))
    left = jnp.concatenate(squares, axis=0)
    if spans is SPANS[0]:
        refs[1][...] = left
        return
    left = left + refs[0][...]
    left = jnp.concatenate([left, left], axis=0)
    for k in range(3):
        part = left.astype(BF)
        out[n + 16 * k : n + 16 * k + 16, :] = part
        left = left - part.astype(F32)


def spill_kernel(other, zi, places, a0, a1, a2, a3, b, *refs):
    refs = refs[7:] if other else refs
    outs, (v6, v5, v4, v3, vs, v2, v1, fa, fb, ins, sem) = refs[:7], refs[7:]
    cin = []
    for j, a in enumerate((a0, a1, a2, a3)):
        for k in range(4):
            dst = fa.at[pl.ds(pl.multiple_of(places[4 * j + k] * 464, 16), 464), :]
            cin.append(go(a.at[pl.ds(464 * k, 464), :], dst, ins.at[4 * j + k]))
    last = go(b.at[:, pl.ds(0, 176), :], fb.reshape(16, 176, 128), ins.at[16])
    c = 1 - zi[4] if other else zi[4]
    copies = []
    plan = (
        (v5, 1, fa, 1024, 2304, 1),
        (vs, 4, fa, 5376, 512, 4),
        (v6, 0, fa, 0, 256, 4),
        (v4, 2, fa, 3328, 1024, 1),
        (v3, 3, fa, 4352, 256, 4),
        (v2, 5, fb, 0, 2304, 1),
    )
    wait(cin)
    for dst, i, flat, at, n, blocks in plan:
        if i == 5:
            last.wait()
        for j in range(blocks):
            dst[:, 128 * j : 128 * (j + 1)] = flat[at + j * n : at + (j + 1) * n, :].astype(F32)
        rows = pl.ds(pl.multiple_of(c * n, n), n)
        copies.append(go(dst, outs[i].at[rows, :], sem.at[i]))
    for k in range(2):
        v1[256 * k : 256 * (k + 1), :] = fb[2304 + 256 * k : 2560 + 256 * k, :].astype(F32)
        rows = pl.ds(pl.multiple_of(zi[2 * c + k] * 256, 256), 256)
        copies.append(go(v1.at[pl.ds(256 * k, 256), :], outs[6].at[rows, :], sem.at[6 + k]))
    wait(copies)


GRADS = ((512, 512), (4608, 128), (2048, 128), (512, 512), (1024, 512), (4608, 128), (1024, 128))


def spill(name, zi, places, srcs, before):
    other = bool(before)
    return pl.pallas_call(
        functools.partial(spill_kernel, other),
        name=name,
        out_shape=tuple(pltpu.HBM(d, F32) for d in GRADS),
        in_specs=[SM, SM] + [ANY] * (5 + len(before)),
        out_specs=tuple(ANY for _ in GRADS),
        scratch_shapes=[pltpu.VMEM((r // 2, c), F32) for r, c in GRADS]
        + [pltpu.VMEM((7424, 128), BF), pltpu.VMEM((2816, 128), BF), sems(17), sems(8)],
        input_output_aliases={7 + i: i for i in range(len(before))},
        compiler_params=pltpu.CompilerParams(vmem_limit_bytes=50 * 1024 * 1024),
        cost_estimate=pl.CostEstimate(flops=0, bytes_accessed=8_000_000, transcendentals=0),
    )(zi, places, *srcs, *before)


def ring(n, k):
    return [(i, (i + k) % n) for i in range(n)]


def spread(v, axes, n):
    return lax.all_to_all(jnp.broadcast_to(v[None], (n,) + v.shape), axes, 0, 0)


def share(v):
    v = v + lax.ppermute(v, "c", ring(2, 1))
    return spread(v, PLANE, 16)


def tell(v):
    return lax.all_to_all(v, BATCH, 0, 0)


def tie(*vs):
    return lax.optimization_barrier(vs)


def plane_index():
    return lax.axis_index("y") * 4 + lax.axis_index("x")


def piece(shard, index):
    n = shard.shape[0] // 32
    return lax.dynamic_slice_in_dim(shard, index * n, n, 0)


def swap(v):
    return lax.ppermute(v, "c", ring(2, 1))


def around(parts):
    left = [lax.ppermute(v, "z", ring(4, 1)) for v in parts]
    right = [lax.ppermute(v, "z", ring(4, 3)) for v in parts]
    left[0], left[1], right[0], right[1] = tie(*left, *right)
    far = [lax.ppermute(left[0], "z", ring(4, 1)), lax.ppermute(right[1], "z", ring(4, 3))]
    return right, far, left


def after(v, *first):
    return tie(v, *first)[0]


def add_halves(held, give):
    return (held.astype(F32) + swap(give).astype(F32)).astype(BF)


def body(
    image_global,
    image_local,
    cotangent_global,
    cotangent_local,
    reduce_one,
    spatial_one,
    expand_one,
    shortcut,
    reduce_two,
    spatial_two,
    expand_two,
    factors_mid,
    factors_out,
    shifts_mid,
    shifts_out,
):
    zi = lax.axis_index("z")
    ci = lax.axis_index("c")
    where = jnp.stack([zi, (zi + 1) % 4, (zi + 2) % 4, (zi + 3) % 4, ci]).astype(jnp.int32)
    flat2, flat5 = spatial_one.reshape(-1, 128), spatial_two.reshape(-1, 128)
    own = [reduce_one, flat2, expand_one, shortcut, reduce_two, flat5, expand_two]

    x = pack(
        "pack_image", image_local, image_global, (6, 14), (TOP, RIN - TOP), (reduce_one,)
    )
    x_right, x_far, x_left = around(x)
    xs = tuple(x) + tuple(x_right) + tuple(x_far) + tuple(x_left)

    norms = jnp.concatenate(
        [factors_mid, shifts_mid, factors_out.reshape(12, 128), shifts_out.reshape(12, 128)]
    )
    norms = after(norms, x[0])
    high = lax.reduce_precision(norms, 8, 7)
    middle = lax.reduce_precision(norms - high, 8, 7)
    low = norms - high - middle
    norms = spread(jnp.concatenate([v.astype(BF) for v in (high, middle, low)]), "z", 4)
    norms = norms[:, 0:32].astype(F32) + norms[:, 32:64].astype(F32) + norms[:, 64:96].astype(F32)

    xs = tuple(after(v, norms) for v in xs)

    near, late = launch(
        "pieces",
        pieces_kernel,
        [((plane_index() * 2 + ci).reshape(1).astype(jnp.int32), SM)]
        + [(after(v, x[0]), ANY) for v in (flat2, expand_one, shortcut, reduce_two, flat5, expand_two)],
        [(shape((400, 128), BF), VM), (shape((208, 128), BF), VM)],
        [sems(15)],
    )
    near = lax.all_gather(near, EVERY, axis=0).reshape(32, 4, 400, 128)
    late = lax.all_gather(late, EVERY, axis=0).reshape(32, 4, 208, 128)

    cot = pack("pack_cotangent", cotangent_local, cotangent_global, (3, 7), (272, 272))
    c_right, c_far, c_left = around(cot)
    cots = tuple(cot) + tuple(c_right) + tuple(c_far) + tuple(c_left)
    square = launch(
        "weight_squares",
        square_kernel,
        [(w, VM) for w in own],
        [(shape((7, 8, 128)), VM)],
        (),
        (0, 6_000_000),
    )[0]

    mid_stats = (shape((32, 4, 512)), FAR)
    out_stats = (shape((4, 2048)), VM)
    narrow, wide = (shape((ROUT, 512)), ANY), (shape((ROUT, 2048)), ANY)
    z1, s1 = launch(
        "reduce_one",
        first_kernel,
        [(where, SM)] + [(v, ANY) for v in xs],
        [(shape((RIN, 512)), ANY), mid_stats],
        [
            pltpu.VMEM((RIN, 1024), BF),
            pltpu.VMEM((RIN, 512), F32),
            pltpu.VMEM((1024, 512), BF),
            sems(4, 4),
            sems(4),
            sems(8),
        ],
        (2 * RIN * 1024 * 512, 10_000_000),
    )
    st1 = tell(s1)
    t1, z2, s2, sum1 = conv_call(
        "spatial_one",
        second_kernel,
        [(st1, NEAR), (norms, VM), (z1, ANY), (near, ANY)],
        RIN,
        (8, 16),
        20,
        40_000_000_000,
    )
    st2 = tell(s2)
    xe, zs, ss = launch(
        "shortcut",
        skip_kernel,
        [(where, SM)] + [(v, ANY) for v in xs + (near,)],
        [(shape((ROUT, 1024), BF), ANY), wide, out_stats],
        [
            pltpu.VMEM((4, RIN, 256), BF),
            pltpu.VMEM((ROUT, 1024), BF),
            pltpu.VMEM((ROUT, 256), F32),
            pltpu.VMEM((ROUT, 2048), F32),
            pltpu.VMEM((1024, 2048), BF),
            sems(4, 2),
            sems(16),
            sems(1),
            sems(4),
        ],
        (2 * ROUT * 1024 * 2048, 14_000_000),
    )
    h2, z3, s3, sum2 = expand_call(
        "expand_one", 1, 144, st2, norms, z2, near
    )
    st3 = share(jnp.concatenate([s3, ss]))
    st3, *cots = tie(st3, *cots)
    cots = tuple(cots)
    mid, h3, z4, s4, sum3, sums = launch(
        "reduce_two",
        middle_kernel,
        [(st3, NEAR), (norms, VM), (z3, ANY), (zs, ANY), (near, ANY)],
        [wide, (shape((ROUT, 2048), BF), ANY), narrow, mid_stats, out_stats, out_stats],
        [
            pltpu.VMEM((ROUT, 2048), F32),
            pltpu.VMEM((ROUT, 2048), F32),
            pltpu.VMEM((ROUT, 2048), BF),
            pltpu.VMEM((ROUT, 512), F32),
            pltpu.VMEM((32, 64, 512), BF),
            sems(2, 4),
            sems(4),
            sems(4),
            sems(4),
            sems(1),
        ],
        (2 * ROUT * 2048 * 512, 20_000_000),
    )
    st4 = tell(s4)
    st4, square = tie(st4, square)
    t4, z5, s5, sum4 = conv_call(
        "spatial_two",
        fifth_kernel,
        [(st4, NEAR), (norms, VM), (z4, ANY), (late, ANY)],
        ROUT,
        (5, 9),
        1,
        2 * 544 * 4608 * 512,
    )
    st5 = tell(s5)
    h5, z6, s6, sum5 = expand_call("expand_two", 3, 144, st5, norms, z5, late)
    st6 = share(s6)
    out, dv6, b6, sum6 = launch(
        "output",
        last_kernel,
        [(where, SM), (st6, NEAR), (norms, VM)] + [(v, ANY) for v in (z6, mid) + cots],
        [narrow, wide, out_stats, out_stats],
        [
            pltpu.VMEM((4, ROUT, 512), F32),
            pltpu.VMEM((4, ROUT, 512), F32),
            pltpu.VMEM((4, ROUT, 512), BF),
            pltpu.VMEM((ROUT, 512), F32),
            sems(4, 4),
            sems(5),
        ],
        (0, 20_000_000),
    )
    output_local, output_global = unpack("unpack_output", out, (3, 7))
    bt6 = share(b6)
    bt6, output_local, output_global = tie(bt6, output_local, output_global)

    wide_in = [pltpu.VMEM((ROUT, 2048), F32), pltpu.VMEM((ROUT, 2048), F32)]
    flat = [pltpu.VMEM((ROUT, 512), F32)]
    mid_grad, out_grad = (shape((2, 512)), VM), (shape((2, 2048)), VM)
    own_mid, own_out = (shape((ROUT, 128), BF), VM), (shape((ROUT, 512), BF), VM)
    o6, dv5, b5, gr6 = launch(
        "back_expand_two",
        back_six_kernel,
        [(where, SM), (bt6, NEAR), (norms, VM), (sum6, VM), (sum5, VM)]
        + [(v, ANY) for v in (z6, dv6, z5, late)],
        [own_out, narrow, mid_stats, out_grad],
        wide_in
        + flat * 2
        + [
            pltpu.VMEM((ROUT, 2048), BF),
            pltpu.VMEM((512, 2048), BF),
            sems(2, 4),
            sems(1),
            sems(16),
            sems(1),
        ],
        (2 * ROUT * 2048 * 512, 14_000_000),
    )
    bt5 = tell(b5)
    gw6 = grad_call("grad_expand_two", where, [(h5, o6)])
    bt5, *gw6 = tie(bt5, *gw6)
    conv_weight = [pltpu.VMEM((32, 144, 512), BF)]
    o5, dv4, b4, gr5 = launch(
        "back_spatial_two",
        back_five_kernel,
        [(where, SM), (bt5, NEAR), (norms, VM), (sum5, VM), (sum4, VM)]
        + [(v, ANY) for v in (z5, dv5, z4, late)],
        [own_mid, narrow, mid_stats, mid_grad],
        flat * 4
        + [
            pltpu.VMEM((ROUT, 512), BF),
            pltpu.VMEM((5, 5, 16, 512), F32),
            pltpu.VMEM((9, 9, 8, 512), F32),
        ]
        + conv_weight
        + [sems(3), sems(4), sems(1)],
        (2 * ROUT * 4608 * 512, 10_000_000),
    )
    bt4 = tell(b4)
    gw5 = grad_call("grad_spatial_two", where, [(t4, o5)])
    bt4, *gw5 = tie(bt4, *gw5)
    o4, dpre, b3, gr4 = launch(
        "back_reduce_two",
        back_four_kernel,
        [(where, SM), (bt4, NEAR), (norms, VM), (sum4, VM), (sum3, VM), (sums, VM)]
        + [(v, ANY) for v in (z4, dv4, dv6, z3, zs, near)],
        [own_mid, wide, (shape((6, 2048)), VM), mid_grad],
        flat * 2
        + wide_in
        + wide_in[:1]
        + [
            pltpu.VMEM((ROUT, 512), BF),
            pltpu.VMEM((32, 64, 512), BF),
            sems(2),
            sems(3, 4),
            sems(4),
            sems(4),
        ],
        (2 * ROUT * 2048 * 512, 22_000_000),
    )
    bt3 = share(b3)
    gw4 = grad_call("grad_reduce_two", where, [(h3, o4)])
    bt3, *gw4 = tie(bt3, *gw4)
    o3, dv2, b2, gr3, gsum = launch(
        "back_expand_one",
        back_three_kernel,
        [(where, SM), (bt3, NEAR), (norms, VM), (sum3, VM), (sum2, VM)]
        + [(v, ANY) for v in (z3, dpre, z2, near)],
        [own_out, narrow, mid_stats, out_grad, out_stats],
        wide_in
        + flat * 2
        + [
            pltpu.VMEM((ROUT, 2048), BF),
            pltpu.VMEM((512, 2048), BF),
            sems(2, 4),
            sems(1),
            sems(16),
            sems(1),
        ],
        (2 * ROUT * 2048 * 512, 16_000_000),
    )
    bt2 = tell(b2)
    o_s, skip, grs = launch(
        "back_shortcut",
        back_skip_kernel,
        [(where, SM), (norms, VM), (gsum, VM), (sums, VM)]
        + [(v, ANY) for v in (zs, dpre, near)],
        [own_out, (shape((ROUT, 256)), VM), out_grad],
        wide_in
        + [pltpu.VMEM((ROUT, 2048), BF), pltpu.VMEM((256, 2048), BF), sems(2, 4), sems(16)],
        (2 * ROUT * 2048 * 256, 10_000_000),
    )
    pair = grad_call("grad_pair", where, [(h2, o3), (xe, o_s)])
    bt2, skip, *pair = tie(bt2, skip, *pair)
    o2, dv1, b1, gr2 = launch(
        "back_spatial_one",
        back_two_kernel,
        [(where, SM), (bt2, NEAR), (norms, VM), (sum2, VM), (sum1, VM)]
        + [(v, ANY) for v in (z2, dv2, z1, near)],
        [own_mid, (shape((RIN, 512)), ANY), mid_stats, mid_grad],
        flat * 2
        + [
            pltpu.VMEM((4, ROUT, 512), BF),
            pltpu.VMEM((ROUT, 512), F32),
            pltpu.VMEM((4, 4, 16, 512), F32),
            pltpu.VMEM((8, 8, 8, 512), F32),
        ]
        + conv_weight
        + [pltpu.VMEM((RIN, 512), F32), sems(3), sems(4), sems(20)],
        (2 * ROUT * 4608 * 512, 20_000_000),
    )
    bt1 = tell(b1)
    conv = grad_call("grad_spatial_one", where, [(t1, o2)])
    some = jnp.concatenate([add_halves(*v) for v in (gw6, gw5, gw4, pair)]).reshape(16, 464, 128)
    bt1, some, *conv = tie(bt1, some, *conv)
    some = lax.all_to_all(some, PLANE, 0, 0)
    o1, dz1, gr1 = launch(
        "back_reduce_one",
        back_one_kernel,
        [(where, SM), (bt1, NEAR), (norms, VM), (sum1, VM), (z1, ANY), (dv1, ANY)],
        [(shape((RIN, 128), BF), VM), (shape((RIN, 512), BF), ANY), mid_grad],
        [
            pltpu.VMEM((RIN, 512), F32),
            pltpu.VMEM((RIN, 512), F32),
            pltpu.VMEM((RIN, 512), BF),
            sems(20),
            sems(20),
            sems(1),
        ],
        (0, 12_000_000),
    )
    first = launch(
        "grad_reduce_one",
        first_grad_kernel,
        [(where, SM)] + [(v, VM) for v in xs + (o1,)],
        [(shape((512, 128), BF), VM)] * 2,
        (),
        (2 * RIN * 1024 * 128, 6_000_000),
    )
    rest = jnp.concatenate([add_halves(*conv), add_halves(*first)]).reshape(16, 176, 128)
    some, rest = tie(some, rest)
    rest = lax.all_to_all(rest, PLANE, 0, 0)
    here = plane_index().reshape(1).astype(jnp.int32)
    some, squares_ = launch(
        "slice_some",
        functools.partial(slice_kernel, SPANS[0]),
        [(here, SM), (some, VM)],
        [(shape((464, 128), BF), VM), (shape((8, 128)), VM)],
        (),
        (0, 2_000_000),
    )
    some = [some] + [lax.ppermute(some, "x", ring(4, k)) for k in (1, 2, 3)]
    rest, *some = tie(rest, *some)
    rest = launch(
        "slice_rest",
        functools.partial(slice_kernel, SPANS[1]),
        [(here, SM), (rest, VM), (squares_, VM)],
        [(shape((224, 128), BF), VM)],
        (),
        (0, 1_000_000),
    )[0]
    dimage_local, dimage_global = launch(
        "image_grad",
        image_kernel,
        [(where, SM), (dz1, VM)] + [(v, ANY) for v in xs[::2]] + [(skip, VM)],
        [(shape((12, 6, 6, 256)), VM), (shape((6, 14, 14, 256)), VM)],
        [pltpu.VMEM((2, RIN, 128), F32), pltpu.VMEM((1024, 512), BF), sems(8)],
        (2 * RIN * 512 * 256, 8_000_000),
    )
    rest, dimage_local, dimage_global = tie(rest, dimage_local, dimage_global)
    some = jnp.concatenate(some)
    some = [some] + [lax.ppermute(some, "y", ring(4, k)) for k in (1, 2, 3)]
    yi, xi = lax.axis_index("y"), lax.axis_index("x")
    places = jnp.stack([(yi - j) % 4 * 4 + (xi - k) % 4 for j in range(4) for k in range(4)])
    places = places.astype(jnp.int32)
    rest = spread(rest, PLANE, 16)
    rest, *some = tie(rest, *some)
    grads = spill("grads_kept", where, places, (*some, rest), ())
    given = swap(rest)
    others = [swap(v) for v in some]
    t6, t5, t4w, t3, ts, t2, t1w = spill("grads_given", where, places, (*others, given), grads)

    def squares(v):
        v = v[:, 176:224].astype(F32).reshape(16, 3, 16, 128)[:, :, :8]
        return jnp.sum(v, axis=(0, 1, 3))

    grad_sq = squares(rest) + squares(given)
    weight_sq = jnp.pad(jnp.sum(square, axis=(1, 2)), (0, 1))
    sq = jnp.concatenate([weight_sq[None], grad_sq[None]])
    sq = sq + lax.ppermute(sq, "z", ring(4, 2))
    sq = (sq + lax.ppermute(sq, "z", ring(4, 1)))[:, :7]
    weight_norm = jnp.sqrt(sq[0])
    ratios = weight_norm / (jnp.sqrt(sq[1]) / 12864.0 + DECAY * weight_norm)

    def cut_own(v, n):
        return lax.dynamic_slice_in_dim(v, zi * n, n, 2)

    mids = cut_own(jnp.stack([gr1, gr2, gr4, gr5]), 128)
    wides = cut_own(jnp.stack([gr3, grs, gr6]), 512)
    return (
        output_global,
        output_local,
        dimage_global,
        dimage_local,
        t1w,
        t2.reshape(spatial_one.shape),
        t3,
        ts,
        t4w,
        t5.reshape(spatial_two.shape),
        t6,
        mids[:, 1],
        wides[:, 1],
        mids[:, 0],
        wides[:, 0],
        ratios,
    )


def solution(mesh):
    fine = Mesh(np.asarray(mesh.devices).reshape(4, 4, 2, 4), EVERY)
    crops = P(BATCH, None, None, "z")
    mat = P(None, "z")
    conv = P(None, None, None, "z")
    weights = (mat, conv, mat, mat, mat, conv, mat)
    return jax.shard_map(
        body,
        mesh=fine,
        in_specs=(crops,) * 4 + weights + (mat,) * 4,
        out_specs=(crops,) * 4 + weights + (mat,) * 4 + (P(),),
        check_vma=False,
    )
```
